32 devices in a mesh: expert: 8 (over z, y), tensor: 4 (over x, core).
Axes of the slice: x: 2, y: 2, z: 4, core: 2. Of those that a mesh axis runs over, the one named last changes fastest.
Arguments:
- inputs: bfloat16 [8192, 768], P('expert'), may hold values from -6 to 6
- gain_attn: float32 [768], replicated, may hold values from 0.5 to 1.5
- gain_ffn: float32 [768], replicated, may hold values from 0.5 to 1.5
- weight_qkv: bfloat16 [3, 768, 768], P(None, None, 'tensor'), may hold values from -0.21875 to 0.21875
- weight_attn_out: bfloat16 [768, 768], P('tensor'), may hold values from -0.875 to 0.875
- rel_table: float32 [32, 12], P(None, 'tensor'), may hold values from -4 to 4
- weight_router: bfloat16 [768, 8], replicated, may hold values from -0.15625 to 0.15625
- weight_in: bfloat16 [8, 768, 3072], P('expert', None, 'tensor'), may hold values from -0.21875 to 0.21875
- weight_out: bfloat16 [8, 3072, 768], P('expert', 'tensor'), may hold values from -0.109375 to 0.109375
- routes: int32 [8192, 2], P('expert'), may hold values from 0 to 7, all different within a row; in each aligned block of 1024 rows (0 to 1023, 1024 to 2047, ...) at most 344 rows name the same one
- segments: int32 [8192], P('expert'), may hold values from 0 to 95, never falling along the last dimension, each value on 1 to 512 neighbouring positions
- cotangent: bfloat16 [8192, 768], P('expert', 'tensor'), may hold values from -6 to 6
Outputs:
- activations: bfloat16 [8192, 768], P('expert', 'tensor')
- grad_input: float32 [8192, 768], P('expert')
- grad_gain_attn: float32 [768], replicated
- grad_gain_ffn: float32 [768], replicated
- grad_weight_qkv: float32 [3, 768, 768], P(None, None, 'tensor')
- grad_weight_attn_out: float32 [768, 768], P('tensor')
- grad_rel_table: float32 [32, 12], P(None, 'tensor')
- grad_weight_router: float32 [768, 8], replicated
- grad_weight_in: float32 [8, 768, 3072], P('expert', None, 'tensor')
- grad_weight_out: float32 [8, 3072, 768], P('expert', 'tensor')
The draws below stay inside these ranges and needn't reach their ends.
Inputs may be any that keep to these rules, and one draw needn't show every extreme that they name: Each row names 2 different experts. In the rows of one device (aligned blocks of 1024 rows) no expert is named by more than 344 routes, a bound that some block reaches. `segments`: document numbers never fall along the tokens; a document has 1 to 512 tokens, and one has exactly 512.
All inputs are finite; a program needn't handle non-finite values.
Results may differ from the reference program's by a relative error of at most 0.012.
The reference program's roundings to bfloat16 on the way count: a program that leaves them out, or rounds other values in their place, can miss the bound.
Values may be sent and summed in bfloat16 or wider, within the bound.
A program may use at most 256 MiB of HBM per device.

```python
import math
from functools import partial
import jax
import jax.numpy as jnp
import numpy as np
from jax import lax

D = 768
HEADS = 12
FF = 3072
TOP = 2
TOK_DEV = 1024
BUCKETS = 32
EXPERTS = 8
TOKENS = 8192
DOCS = 96
CAP = 344


def block_levels(key, shape, shards, low, top_value):
    factor_of = 1.0
    for position, shards_of in shards:
        steps = jax.random.uniform(jax.random.fold_in(jax.random.fold_in(key, 6), position), (shards_of,), jnp.float32, low / len(shards), top_value / len(shards))
        factor_of = factor_of * jnp.repeat(jnp.exp(steps), shape[position] // shards_of).reshape((-1,) + (1,) * (len(shape) - 1 - position))
    return factor_of


def profile(number_of, total, reach, slope):
    loads = [(1 << 20) // math.isqrt(standing ** slope) + 1 for standing in range(2, number_of + 1)]
    rest, given = total - reach - (number_of - 1), [1] * (number_of - 1)
    while rest > 0:
        movable = [i for i in range(number_of - 1) if given[i] < reach]
        whole, left = sum([loads[i] for i in movable]), rest
        for i in movable:
            extra = min(reach - given[i], max(1, left * loads[i] // whole), rest)
            given[i] = given[i] + extra
            rest = rest - extra
    return np.array([reach] + given)


def uneven_parts(own_key, count, total, limit, slope):
    if count == 2:
        one = jax.random.randint(own_key, (), max(1, total - limit), min(limit, total - 1) + 1)
        return jnp.stack([one, total - one])
    tallies = jnp.asarray(profile(count, total, limit, slope), jnp.int32)
    couples = (count - 1) // 2
    donor, receiver = tallies[1:1 + 2 * couples:2], tallies[2:2 + 2 * couples:2]
    margin = jnp.minimum(donor - 1, limit - receiver)
    moved = jax.random.randint(jax.random.fold_in(own_key, 1), (couples,), 0, 1 << 20) % (margin + 1)
    tallies = tallies.at[1:1 + 2 * couples:2].set(donor - moved).at[2:2 + 2 * couples:2].set(receiver + moved)
    return tallies[jax.random.permutation(jax.random.fold_in(own_key, 2), count)]


def assign_block(key, own, number, rows, amount, top, reach, slope):
    ranking = jax.random.permutation(key, amount)
    crowded, ordinary = load_shares(amount, rows * top, reach, slope, True), load_shares(amount, rows * top, reach, slope, False)
    places = jnp.arange(amount)

    def named(sizes, turn):
        used = int((sizes > 0).sum())
        fixed = max(1, used // 4)
        passed = fixed + (places - fixed + turn * (used - fixed)) % max(1, amount - fixed)
        return jnp.zeros((amount,), jnp.int32).at[ranking[jnp.where(places < fixed, places, passed)]].set(jnp.asarray(sizes, jnp.int32))

    sizes = jnp.where(number % 4 == 0, named(crowded, number // 4), named(ordinary, number - number // 4 - 1))
    mixed = jax.random.permutation(jax.random.fold_in(own, 3), amount)
    giver, taker = mixed[0:amount // 2 * 2:2], mixed[1:amount // 2 * 2:2]
    margin = jnp.minimum(sizes[giver] - 1, reach - sizes[taker]) // 2
    margin = jnp.where((giver == ranking[0]) | (taker == ranking[0]) | (sizes[taker] == 0), 0, jnp.maximum(margin, 0))
    passed = jax.random.randint(jax.random.fold_in(own, 4), (amount // 2,), 0, 1 << 20) % (margin + 1)
    sizes = sizes.at[giver].add(-passed).at[taker].add(passed)
    members = jnp.searchsorted(jnp.cumsum(sizes), jnp.arange(rows * top), side="right").astype(jnp.int32)
    grid = members.reshape(top, rows).T
    grid = grid[jax.random.permutation(jax.random.fold_in(own, 1), rows)]
    turn = jax.random.randint(jax.random.fold_in(own, 2), (rows, 1), 0, top)
    return jnp.take_along_axis(grid, (jnp.arange(top)[None, :] + turn) % top, axis=1)


def load_shares(number_of, total, most, lean, full):
    loads = [(1 << 20) // math.isqrt(grade ** lean) + 1 for grade in range(1, number_of + 1)]
    largest = most if full else min(most, max(-(-total // number_of), total * loads[0] // sum(loads)))
    least = 1 if total - largest >= number_of - 1 else 0
    holding, rest = [largest] + [least] * (number_of - 1), total - largest - least * (number_of - 1)
    while rest > 0:
        free = [i for i in range(1, number_of) if holding[i] < largest] or [i for i in range(1, number_of) if holding[i] < most]
        mass, remaining = sum([loads[i] for i in free]), rest
        for i in free:
            addition = min(most - holding[i], max(1, remaining * loads[i] // mass), rest)
            holding[i] = holding[i] + addition
            rest = rest - addition
    return np.array(holding)


def normal_values(stream_key, dims, deviation, bound, split=(), kind=jnp.bfloat16):
    entries = jax.random.normal(stream_key, dims, jnp.float32) * deviation
    if len(split) > 0:
        entries = block_levels(stream_key, dims, split, -0.22, 0.18) * entries
    return jnp.clip(entries, min=-bound, max=bound).astype(kind)


def setup_inputs(seed: int = 0) -> dict:
    keys = jax.random.split(jax.random.key(seed), 13)
    inputs = normal_values(keys[0], (TOKENS, D), 1.0, 6.0, ((0, 8),))
    gain_attn = jnp.clip(1.0 + 0.1 * jax.random.normal(keys[1], (D,), jnp.float32), 0.5, 1.5)
    gain_ffn = jnp.clip(1.0 + 0.1 * jax.random.normal(keys[2], (D,), jnp.float32), 0.5, 1.5)
    weight_qkv = normal_values(keys[3], (3, D, D), D ** -0.5, 0.21875, ((2, 4),))
    weight_attn_out = normal_values(keys[4], (D, D), (D // 16) ** -0.5, 0.875, ((0, 4),))
    rel_table = normal_values(keys[5], (BUCKETS, HEADS), 1.0, 4.0, ((1, 4),), jnp.float32)
    weight_router = normal_values(keys[6], (D, EXPERTS), (2 * D) ** -0.5, 0.15625)
    weight_in = normal_values(keys[7], (EXPERTS, D, FF), D ** -0.5, 0.21875, ((0, 8), (2, 4)))
    weight_out = normal_values(keys[8], (EXPERTS, FF, D), FF ** -0.5, 0.109375, ((0, 8), (1, 4)))
    routes_keys = jax.random.split(jax.random.fold_in(keys[9], 1), TOKENS // TOK_DEV)
    routes_turns = jax.random.permutation(jax.random.fold_in(keys[9], 3), TOKENS // TOK_DEV)
    routes = jax.vmap(lambda own, number: assign_block(jax.random.fold_in(keys[9], 2), own, number, TOK_DEV, EXPERTS, TOP, CAP, 2))(routes_keys, routes_turns).reshape((TOKENS, TOP))
    segments = jnp.searchsorted(jnp.cumsum(uneven_parts(keys[10], DOCS, TOKENS, TOK_DEV // 2, 2)), jnp.arange(TOKENS), side="right").astype(jnp.int32)
    cotangent = normal_values(keys[11], (TOKENS, D), 1.0, 6.0, ((0, 8), (1, 4)))
    return {"inputs": inputs, "gain_attn": gain_attn, "gain_ffn": gain_ffn, "weight_qkv": weight_qkv, "weight_attn_out": weight_attn_out, "rel_table": rel_table, "weight_router": weight_router, "weight_in": weight_in, "weight_out": weight_out, "routes": routes, "segments": segments, "cotangent": cotangent}


@jax.custom_vjp
def low(v):
    return lax.optimization_barrier(v.astype(jnp.bfloat16)).astype(jnp.float32)

@jax.custom_vjp
def low_back(v):
    return v

def low_keep(v):
    return (low(v), None)

def low_pass(kept, grad):
    return (grad,)

def back_keep(v):
    return (v, None)

def back_low(kept, grad):
    return (low(grad),)
low.defvjp(low_keep, low_pass)
low_back.defvjp(back_keep, back_low)
epsilon = 1e-06
negative = -1e+30
highest = lax.Precision.HIGHEST

def far_limits(buckets):
    half_size = buckets // 2
    base_ratio = 256.0 / buckets
    return [int(math.ceil(half_size * base_ratio ** (step / half_size))) for step in range(1, half_size)]

def bucket_of(distance, buckets):
    half_size = buckets // 2
    limits = jnp.array(far_limits(buckets), dtype=jnp.int32)
    far_bucket = half_size + lax.optimization_barrier(jnp.sum((distance[..., None] >= limits).astype(jnp.int32), axis=-1))
    return jnp.where(distance < half_size, distance, far_bucket).astype(jnp.int32)

def rms_norm(values, gain_vector):
    return values * lax.rsqrt(lax.optimization_barrier(jnp.mean(values * values, axis=-1, keepdims=True)) + epsilon) * gain_vector

def slot_ranks(route_rows, experts):
    route_flat = route_rows.reshape(-1)
    route_hot = (route_flat[:, None] == jnp.arange(experts, dtype=jnp.int32)[None, :]).astype(jnp.int32)
    earlier = jnp.cumsum(route_hot, axis=0) - route_hot
    return lax.optimization_barrier(jnp.sum(earlier * route_hot, axis=1)).astype(jnp.int32)

def attend_sequence(pieces, rel_table):
    queries, keys_all, values_all, segment_ids = pieces
    seq_len = queries.shape[0]
    head_count = rel_table.shape[1]
    head_size = queries.shape[1] // head_count
    query_heads = queries.reshape(seq_len, head_count, head_size)
    key_heads = keys_all.reshape(seq_len, head_count, head_size)
    value_heads = values_all.reshape(seq_len, head_count, head_size)
    positions = jnp.arange(seq_len, dtype=jnp.int32)
    distance = jnp.maximum(positions[:, None] - positions[None, :], 0)
    bias_grid = jnp.transpose(rel_table[bucket_of(distance, BUCKETS)], (2, 0, 1))
    scores = jnp.einsum('qhd,khd->hqk', query_heads, key_heads, precision=highest) * head_size ** (-0.5) + bias_grid
    scores = low_back(scores)
    allowed = (positions[None, :] <= positions[:, None]) & (segment_ids[:, None] == segment_ids[None, :])
    scores = jnp.where(allowed[None], scores, negative)
    attn_probs = low(jax.nn.softmax(scores, axis=-1))
    mixed_heads = jnp.einsum('hqk,khd->qhd', attn_probs, value_heads, precision=highest)
    return mixed_heads.reshape(seq_len, head_count * head_size)

def layer_forward(inputs, gain_attn, gain_ffn, weight_qkv, weight_attn_out, rel_table, weight_router, weight_in, weight_out, routes, segments):
    tokens = inputs.shape[0]
    seq_count = tokens // TOK_DEV
    normed_attn = low(rms_norm(inputs, gain_attn))
    projected = low(low_back(jnp.einsum('td,kdc->ktc', normed_attn, weight_qkv, precision=highest)))
    pieces = (projected[0].reshape(seq_count, TOK_DEV, D), projected[1].reshape(seq_count, TOK_DEV, D), projected[2].reshape(seq_count, TOK_DEV, D), segments.reshape(seq_count, TOK_DEV))
    mixed_heads = lax.map(jax.checkpoint(partial(attend_sequence, rel_table=rel_table)), pieces)
    mixed_heads = low(low_back(mixed_heads.reshape(tokens, D)))
    attn_total = jnp.dot(mixed_heads, weight_attn_out, precision=highest)
    stream_mid = inputs + low_back(attn_total)
    normed_ffn = low(rms_norm(stream_mid, gain_ffn))
    logits = low_back(jnp.dot(normed_ffn, weight_router, precision=highest))
    chosen = jnp.take_along_axis(logits, routes, axis=1)
    gate_weights = jax.nn.softmax(chosen, axis=-1)
    route_seq = routes.reshape(seq_count, TOK_DEV * TOP)
    ranks = jax.vmap(partial(slot_ranks, experts=EXPERTS))(route_seq)
    seq_ids = jnp.arange(seq_count, dtype=jnp.int32)[:, None]
    buffer_index = route_seq * (seq_count * CAP) + seq_ids * CAP + ranks
    token_ids = seq_ids * TOK_DEV + jnp.arange(TOK_DEV * TOP, dtype=jnp.int32)[None, :] // TOP
    slot_token = jnp.full((EXPERTS * seq_count * CAP,), tokens, jnp.int32).at[buffer_index.reshape(-1)].set(token_ids.reshape(-1))
    padded_rows = jnp.concatenate([normed_ffn, jnp.zeros((1, D), normed_ffn.dtype)], axis=0)

    def expert_rows(expert_pieces):
        slot_rows, weight_first, weight_second = expert_pieces
        arrived = low_back(padded_rows[slot_rows])
        hidden_pre = low_back(jnp.dot(arrived, weight_first, precision=highest))
        hidden = low(jax.nn.gelu(hidden_pre))
        return low_back(low(jnp.dot(hidden, weight_second, precision=highest)))
    results = lax.map(jax.checkpoint(expert_rows), (slot_token.reshape(EXPERTS, seq_count * CAP), weight_in, weight_out))
    picked = results.reshape(-1, D)[buffer_index.reshape(tokens, TOP)]
    combined = lax.optimization_barrier(jnp.sum(gate_weights[:, :, None] * picked, axis=1))
    return stream_mid + combined

def reference(inputs, gain_attn, gain_ffn, weight_qkv, weight_attn_out, rel_table, weight_router, weight_in, weight_out, routes, segments, cotangent):
    float_args = (inputs.astype(jnp.float32), gain_attn.astype(jnp.float32), gain_ffn.astype(jnp.float32), weight_qkv.astype(jnp.float32), weight_attn_out.astype(jnp.float32), rel_table.astype(jnp.float32), weight_router.astype(jnp.float32), weight_in.astype(jnp.float32), weight_out.astype(jnp.float32))
    outputs, pullback = jax.vjp(partial(layer_forward, routes=routes, segments=segments), *float_args)
    gradients = pullback(cotangent.astype(jnp.float32))
    return (outputs.astype(jnp.bfloat16), gradients[0], gradients[1], gradients[2], gradients[3], gradients[4], gradients[5], gradients[6], gradients[7], gradients[8])
```

```python
import functools
import math

import jax
import jax.numpy as jnp
from jax import lax
from jax.experimental import pallas as pl
from jax.experimental.pallas import tpu as pltpu
from jax.sharding import PartitionSpec as P

BLOCK = 512
BUCKETS = 32


epsilon = 1e-06
negative = -1e30
highest = lax.Precision.HIGHEST


F32 = jnp.float32
BF16 = jnp.bfloat16
MESH = pl.DeviceIdType.MESH
VMEM_SPEC = pl.BlockSpec(memory_space=pltpu.VMEM)
ANY_SPEC = pl.BlockSpec(memory_space=pl.ANY)
LANES = 128
ROW_TILE = 256
COL_TILE = 256
VMEM_LIMIT = 60 * 2**20


def dot_nn(left, right):
    return lax.dot_general(left, right, (((1,), (0,)), ((), ())), preferred_element_type=F32)


def dot_nt(left, right):
    return lax.dot_general(left, right, (((1,), (1,)), ((), ())), preferred_element_type=F32)


def dot_tn(left, right):
    return lax.dot_general(left, right, (((0,), (0,)), ((), ())), preferred_element_type=F32)


def round_up(value, step):
    return (value + step - 1) // step * step


class Sizes:
    def __init__(self, experts, seq_len, top_count, width):
        self.experts = experts
        self.seq = seq_len
        self.width = width
        self.half_width = width // 2
        capacity = (4 * seq_len * top_count + 24 * experts - 1) // (24 * experts) * 8
        self.slots = round_up(capacity, 32)
        self.half = self.slots // 2
        self.slot_lanes = round_up(self.slots, LANES)


class Place:
    def __init__(self, sizes):
        self.count = sizes.experts
        self.e = lax.axis_index("expert")
        self.t = lax.axis_index("tensor")
        self.c = lax.rem(self.t, 2)
        self.x = lax.div(self.t, 2)
        self.core_peer = self.t + 1 - 2 * self.c
        self.x_peer = lax.rem(self.t + 2, 4)

    def ahead(self, k):
        return lax.rem(self.e + k, self.count)

    def behind(self, k):
        return lax.rem(self.e + self.count - k, self.count)

    def greet(self, expert_peers=True, all_tensor=True):
        barrier = pltpu.get_barrier_semaphore()
        count = 0
        if expert_peers:

            def one(k, carry):
                pl.semaphore_signal(
                    barrier, inc=1, device_id=(self.ahead(k), self.t), device_id_type=MESH
                )
                return carry

            lax.fori_loop(1, self.count, one, 0)
            count += self.count - 1
        for d in range(1, 4):
            pl.semaphore_signal(
                barrier,
                inc=1,
                device_id=(self.e, lax.rem(self.t + d, 4)),
                device_id_type=MESH,
            )
        count += 3
        pl.semaphore_wait(barrier, count)


def remote(src, dst, send_sem, recv_sem, device):
    return pltpu.make_async_remote_copy(
        src_ref=src,
        dst_ref=dst,
        send_sem=send_sem,
        recv_sem=recv_sem,
        device_id=device,
        device_id_type=MESH,
    )


class Gather:
    sem_kinds = 4

    def __init__(self, sizes, place, stage, buf, send, recv):
        self.z, self.p = sizes, place
        self.stage, self.buf, self.send, self.recv = stage, buf, send, recv

    def quarter(self, k, c, x):
        h, w = self.z.half, self.z.half_width
        return self.buf.at[
            k, pl.ds(pl.multiple_of(c * h, 16), h), pl.ds(pl.multiple_of(x * w, LANES), w)
        ]

    def out(self, k):
        p = self.p
        return remote(
            self.stage.at[k],
            self.quarter(k, p.c, p.x),
            self.send.at[0, k],
            self.recv.at[0, k],
            (p.ahead(k), p.t),
        )

    def to_core(self, k):
        p = self.p
        ref = self.quarter(k, p.c, p.x)
        return remote(ref, ref, self.send.at[1, k], self.recv.at[1, k], (p.e, p.core_peer))

    def to_x(self, k):
        p = self.p
        ref = self.quarter(k, p.c, p.x)
        return remote(ref, ref, self.send.at[2, k], self.recv.at[2, k], (p.e, p.x_peer))

    def on_to_core(self, k):
        p = self.p
        ref = self.quarter(k, p.c, 1 - p.x)
        return remote(ref, ref, self.send.at[3, k], self.recv.at[3, k], (p.e, p.core_peer))

    def pack_own(self, rk_row, rows_ref):
        z, p = self.z, self.p
        pick = slot_onehot(rk_row[pl.ds(p.e, 1), :], z.slots, 0)
        for j in range(0, z.width, COL_TILE):
            self.buf[0, :, j : j + COL_TILE] = dot_nn(
                pick, rows_ref[:, j : j + COL_TILE]
            ).astype(BF16)

    def pack(self, k, pick, rows_ref):
        z, p = self.z, self.p
        cols = rows_ref[:, pl.ds(pl.multiple_of(p.x * z.half_width, LANES), z.half_width)]
        self.stage[k] = dot_nn(pick, cols).astype(BF16)

    def first(self, k):
        self.out(k).wait_recv()
        self.to_core(k).start()
        self.to_x(k).start()

    def second(self, k):
        self.to_x(k).wait_recv()
        self.on_to_core(k).start()

    def last(self, k):
        self.to_core(k).wait_recv()
        self.on_to_core(k).wait_recv()

    def finish(self, k):
        self.out(k).wait_send()
        self.to_core(k).wait_send()
        self.to_x(k).wait_send()
        self.on_to_core(k).wait_send()


class Return:
    sem_kinds = 3

    def __init__(self, sizes, place, part, from_core, stage_x, from_x, ret, send, recv):
        self.z, self.p = sizes, place
        self.part, self.from_core, self.stage_x = part, from_core, stage_x
        self.from_x, self.ret = from_x, ret
        self.send, self.recv = send, recv

    def rows(self, c):
        return pl.ds(pl.multiple_of(c * self.z.half, 16), self.z.half)

    def cols(self, x):
        return pl.ds(pl.multiple_of(x * self.z.half_width, LANES), self.z.half_width)

    def to_core(self, k):
        p = self.p
        return remote(
            self.part.at[k, self.rows(1 - p.c), :],
            self.from_core.at[k],
            self.send.at[0, k],
            self.recv.at[0, k],
            (p.e, p.core_peer),
        )

    def to_x(self, k):
        p = self.p
        return remote(
            self.stage_x.at[k],
            self.from_x.at[k],
            self.send.at[1, k],
            self.recv.at[1, k],
            (p.e, p.x_peer),
        )

    def home(self, k):
        p = self.p
        return remote(
            self.from_core.at[k, :, self.cols(p.x)],
            self.ret.at[k],
            self.send.at[2, k],
            self.recv.at[2, k],
            (p.behind(k), p.t),
        )

    def first(self, k):
        self.to_core(k).start()

    def second(self, k):
        p = self.p
        self.to_core(k).wait_recv()
        rows = self.rows(p.c)
        for x in (1 - p.x, p.x):
            cols = self.cols(x)
            both = self.part[k, rows, cols].astype(F32) + self.from_core[k, :, cols].astype(F32)
            if x is p.x:
                self.from_core[k, :, cols] = both.astype(BF16)
            else:
                self.stage_x[k] = both.astype(BF16)
                self.to_x(k).start()

    def third(self, k):
        self.to_x(k).wait_recv()
        cols = self.cols(self.p.x)
        total = self.from_core[k, :, cols].astype(F32) + self.from_x[k].astype(F32)

        @pl.when(k == 0)
        def _():
            self.ret[0] = total.astype(BF16)

        @pl.when(k > 0)
        def _():
            self.from_core[k, :, cols] = total.astype(BF16)
            self.home(k).start()

    def arrive(self, k):
        @pl.when(k > 0)
        def _():
            self.home(k).wait_recv()

    def finish(self, k):
        self.to_core(k).wait_send()
        self.to_x(k).wait_send()

        @pl.when(k > 0)
        def _():
            self.home(k).wait_send()


def return_scratch(z):
    e, h, w = z.experts, z.half, z.half_width
    return [
        pltpu.VMEM((e, z.slots, z.width), BF16),
        pltpu.VMEM((e, h, z.width), BF16),
        pltpu.VMEM((e, h, w), BF16),
        pltpu.VMEM((e, h, w), BF16),
        pltpu.VMEM((e, h, w), BF16),
        pltpu.SemaphoreType.DMA((Return.sem_kinds, e)),
        pltpu.SemaphoreType.DMA((Return.sem_kinds, e)),
    ]


def gather_scratch(z):
    e, h, w = z.experts, z.half, z.half_width
    return [
        pltpu.VMEM((e, h, w), BF16),
        pltpu.VMEM((e, z.slots, z.width), BF16),
        pltpu.SemaphoreType.DMA((Gather.sem_kinds, e)),
        pltpu.SemaphoreType.DMA((Gather.sem_kinds, e)),
    ]


def slot_onehot(rank_row, count, offset):
    slot = lax.broadcasted_iota(jnp.int32, (count, rank_row.shape[1]), 0).astype(F32)
    shift = lax.convert_element_type(offset, F32)
    return jnp.where(rank_row - shift == slot, 1.0, 0.0).astype(BF16)


def pick_lane(values, lane):
    lanes = lax.broadcasted_iota(jnp.int32, values.shape, 1)
    return jnp.sum(jnp.where(lanes == lane, values, 0.0), axis=1, keepdims=True)


def row_to_col(row, count, offset):
    rows = lax.broadcasted_iota(jnp.int32, (count, row.shape[1]), 0) + offset
    lanes = lax.broadcasted_iota(jnp.int32, (count, row.shape[1]), 1)
    return jnp.sum(jnp.where(rows == lanes, row, 0.0), axis=1, keepdims=True)


def col_to_row(col, lane_count):
    rows = lax.broadcasted_iota(jnp.int32, (col.shape[0], lane_count), 0)
    lanes = lax.broadcasted_iota(jnp.int32, (col.shape[0], lane_count), 1)
    return jnp.sum(jnp.where(rows == lanes, col, 0.0), axis=0, keepdims=True)


def loop(start, stop, body):
    def step(i, carry):
        body(i)
        return carry

    lax.fori_loop(start, stop, step, 0)


def fill_ranks(routes_ref, rk_col, rk_row):
    seq = routes_ref.shape[0]
    ids = lax.broadcasted_iota(jnp.int32, (seq, LANES), 1)
    routes = routes_ref[...]
    hot = (routes[:, 0:1] == ids) | (routes[:, 1:2] == ids)
    hot_low = jnp.where(hot, 1.0, 0.0).astype(BF16)
    hot_mark = jnp.where(hot, 1.0, 0.0)
    for r in range(0, seq, ROW_TILE):
        rows = lax.broadcasted_iota(jnp.int32, (ROW_TILE, seq), 0) + r
        cols = lax.broadcasted_iota(jnp.int32, (ROW_TILE, seq), 1)
        before = jnp.where(cols < rows, 1.0, 0.0).astype(BF16)
        rank = dot_nn(before, hot_low)
        rank = jnp.where(hot_mark[r : r + ROW_TILE] > 0.5, rank, -1.0)
        rk_col[r : r + ROW_TILE, :] = rank
        rk_row[:, r : r + ROW_TILE] = rank.T


def send_grads_kernel(
    z, routes_ref, cot_ref, w_out_ref, rk_col, rk_row, og_out, hg_out,
    stage, buf, g_send, g_recv, hg, out_sem,
):
    p = Place(z)
    fill_ranks(routes_ref, rk_col, rk_row)
    p.greet()
    g = Gather(z, p, stage, buf, g_send, g_recv)

    def pack(k):
        pick = slot_onehot(rk_row[pl.ds(p.ahead(k), 1), :], z.half, p.c * z.half)
        g.pack(k, pick, cot_ref)
        g.out(k).start()

    loop(1, z.experts, pack)
    g.pack_own(rk_row, cot_ref)

    def save(k):
        return (
            pltpu.make_async_copy(buf.at[k], og_out.at[k], out_sem.at[0, k]),
            pltpu.make_async_copy(hg.at[k], hg_out.at[k], out_sem.at[1, k]),
        )

    def body(i):
        @pl.when(i + 1 < z.experts)
        def _():
            g.first(i + 1)

        @pl.when((i >= 1) & (i < z.experts))
        def _():
            g.second(i)

        @pl.when(i >= 2)
        def _():
            g.last(i - 1)

        @pl.when(i >= 1)
        def _():
            k = i - 1
            for j in range(0, w_out_ref.shape[0], COL_TILE):
                hg[k, :, j : j + COL_TILE] = dot_nt(
                    buf[k], w_out_ref[j : j + COL_TILE, :]
                ).astype(BF16)
            for copy in save(k):
                copy.start()

    loop(0, z.experts + 1, body)

    def finish(k):
        @pl.when(k > 0)
        def _():
            g.finish(k)

        for copy in save(k):
            copy.wait()

    loop(0, z.experts, finish)


def send_grads(z, routes, cot_full, w_out):
    e = z.experts
    return pl.pallas_call(
        functools.partial(send_grads_kernel, z),
        out_shape=(
            jax.ShapeDtypeStruct((z.seq, LANES), F32),
            jax.ShapeDtypeStruct((LANES, z.seq), F32),
            jax.ShapeDtypeStruct((e, z.slots, z.width), BF16),
            jax.ShapeDtypeStruct((e, z.slots, w_out.shape[0]), BF16),
        ),
        in_specs=[VMEM_SPEC] * 3,
        out_specs=(VMEM_SPEC, VMEM_SPEC, ANY_SPEC, ANY_SPEC),
        scratch_shapes=gather_scratch(z)
        + [
            pltpu.VMEM((e, z.slots, w_out.shape[0]), BF16),
            pltpu.SemaphoreType.DMA((2, e)),
        ],
        compiler_params=pltpu.CompilerParams(
            collective_id=1, has_side_effects=True, vmem_limit_bytes=VMEM_LIMIT
        ),
        name="send_grads",
    )(routes, cot_full, w_out)


def gelu_pair(h):
    scale = 0.7978845608028654
    square = h * h
    t = jnp.tanh(scale * h * (1.0 + 0.044715 * square))
    half = 0.5 + 0.5 * t
    slope = half + (0.5 * scale) * h * (1.0 - t * t) * (1.0 + 0.134145 * square)
    return h * half, slope


def experts_kernel(
    z, x_ref, mixed_ref, wao_ref, gain_ref, wr_ref, rk_col, rk_row, w_in_ref, hg_ref,
    mid_ref, nrm_ref, gates_ref, nf_out, gg_out, gs_in, rows_out, hid_out, pre_out,
    stage, buf, g_send, g_recv,
    part, from_core, stage_x, from_x, ret, r_send, r_recv,
    hid, pre, wr_pad, gate_row, gs_out, gg_send, gg_recv, acc, retx,
    d_send, d_recv, gd_send, gd_recv, nf,
    gs_sems, gg_sems, out_sem, d_sems,
):
    p = Place(z)
    experts = z.experts
    wr_pad[...] = jnp.zeros_like(wr_pad)
    wr_pad[:, 0:experts] = wr_ref[...]
    for r in range(0, z.seq, ROW_TILE):
        rows = slice(r, r + ROW_TILE)
        mid = x_ref[rows, :].astype(F32) + dot_nn(mixed_ref[rows, :], wao_ref[...])
        mid_ref[rows, :] = mid
        root = lax.rsqrt(jnp.mean(mid * mid, axis=1, keepdims=True) + epsilon)
        nrm = (mid * root * gain_ref[...]).astype(BF16)
        nrm_ref[rows, :] = nrm
        logits = dot_nn(nrm, wr_pad[...])
        hot = rk_col[rows, :] > -0.5
        logits = jnp.where(hot, logits, negative)
        peak = jnp.max(logits, axis=1, keepdims=True)
        power = jnp.where(hot, jnp.exp(logits - peak), 0.0)
        gates = power / jnp.sum(power, axis=1, keepdims=True)
        gates_ref[rows, :] = gates
        gate_row[:, rows] = gates.T
    p.greet()
    g = Gather(z, p, stage, buf, g_send, g_recv)
    b = Return(z, p, part, from_core, stage_x, from_x, ret, r_send, r_recv)

    def gate_copy(k):
        return remote(
            gs_out.at[k], gs_in.at[k], gs_sems.at[0, k], gs_sems.at[1, k], (p.ahead(k), p.t)
        )

    def slot_gates(k):
        pick = slot_onehot(rk_row[pl.ds(p.ahead(k), 1), :], z.slot_lanes, 0)
        row = gate_row[pl.ds(p.ahead(k), 1), :]
        high = row.astype(BF16).astype(F32)
        low = row - high
        which = lax.broadcasted_iota(jnp.int32, (16, z.seq), 0)
        both = jnp.where(which == 0, high, jnp.where(which == 1, low, 0.0)).astype(BF16)
        sums = dot_nt(both, pick)
        return sums[0:1, :] + sums[1:2, :]

    def pack(k):
        pick = slot_onehot(rk_row[pl.ds(p.ahead(k), 1), :], z.half, p.c * z.half)
        g.pack(k, pick, nrm_ref)
        g.out(k).start()

    loop(1, experts, pack)

    def send_gates(k):
        gs_out[k] = slot_gates(k)
        gate_copy(k).start()

    loop(1, experts, send_gates)
    gs_in[0] = slot_gates(0)
    g.pack_own(rk_row, nrm_ref)

    def gg_copy(k, d):
        return remote(
            gg_send.at[k],
            gg_recv.at[k, p.t],
            gg_sems.at[0, k, d],
            gg_sems.at[1, k, d],
            (p.behind(k), lax.rem(p.t + d, 4)),
        )

    def save(k):
        return (
            pltpu.make_async_copy(buf.at[k], rows_out.at[k], out_sem.at[0, k]),
            pltpu.make_async_copy(hid.at[k], hid_out.at[k], out_sem.at[1, k]),
            pltpu.make_async_copy(pre.at[k], pre_out.at[k], out_sem.at[2, k]),
        )

    def expert(k):
        @pl.when(k > 0)
        def _():
            gate_copy(k).wait_recv()
            g.last(k)

        gate = row_to_col(gs_in[k], z.slots, 0)
        sums = jnp.zeros((z.slots, 1), F32)
        for j in range(0, w_in_ref.shape[1], COL_TILE):
            cols = slice(j, j + COL_TILE)
            up, slope = gelu_pair(dot_nn(buf[k], w_in_ref[:, cols]))
            back = hg_ref[k, :, cols].astype(F32)
            hid[k, :, cols] = up.astype(BF16)
            pre[k, :, cols] = (gate * back * slope).astype(BF16)
            sums = sums + jnp.sum(up * back, axis=1, keepdims=True)
        for j in range(0, z.width, COL_TILE):
            part[k, :, j : j + COL_TILE] = dot_nt(
                pre[k], w_in_ref[j : j + COL_TILE, :]
            ).astype(BF16)
        b.first(k)
        gg_send[k] = col_to_row(sums, z.slot_lanes)
        for d in range(1, 4):
            gg_copy(k, d).start()

        @pl.when(k > 0)
        def _():
            gg_copy(k, 0).start()

        @pl.when(k == 0)
        def _():
            gg_recv[0, p.t] = gg_send[0]

        for copy in save(k):
            copy.start()

    def body(i):
        @pl.when(i < experts)
        def _():
            expert(i)

        @pl.when(i == 0)
        def _():
            g.first(1)

        @pl.when(i + 2 < experts)
        def _():
            g.first(i + 2)

        @pl.when(i + 1 < experts)
        def _():
            g.second(i + 1)

        @pl.when((i >= 1) & (i <= experts))
        def _():
            b.second(i - 1)

        @pl.when(i >= 2)
        def _():
            b.third(i - 2)

    loop(0, experts + 2, body)
    acc[...] = jnp.zeros_like(acc)

    def combine(k):
        b.arrive(k)
        for d in range(1, 4):
            gg_copy(k, d).wait_recv()

        @pl.when(k > 0)
        def _():
            gg_copy(k, 0).wait_recv()

        row = gg_recv[k, 0] + gg_recv[k, 1] + gg_recv[k, 2] + gg_recv[k, 3]
        col = row_to_col(row, z.half, p.c * z.half)
        high = col.astype(BF16).astype(F32)
        lanes = lax.broadcasted_iota(jnp.int32, (z.half, LANES), 1)
        who = p.ahead(k)
        retx[:, 0 : z.half_width] = ret[k]
        retx[:, z.half_width :] = jnp.where(
            lanes == who, high, jnp.where(lanes == who + experts, col - high, 0.0)
        ).astype(BF16)
        for r in range(0, z.seq, ROW_TILE):
            rows = slice(r, r + ROW_TILE)
            rank = pick_lane(rk_col[rows, :], who) - lax.convert_element_type(p.c * z.half, F32)
            slot = lax.broadcasted_iota(jnp.int32, (ROW_TILE, z.half), 1).astype(F32)
            pick = jnp.where(rank == slot, 1.0, 0.0).astype(BF16)
            acc[rows, :] += dot_nn(pick, retx[...])

    loop(0, experts, combine)
    half_seq = z.seq // 2

    def tokens(c):
        return pl.ds(pl.multiple_of(c * half_seq, 16), half_seq)

    d_send[...] = acc[tokens(1 - p.c), 0 : z.half_width].astype(BF16)
    gd_send[...] = acc[:, z.half_width :].astype(BF16)
    copy_d = remote(d_send, d_recv, d_sems.at[0, 0], d_sems.at[1, 0], (p.e, p.core_peer))
    copy_g = remote(gd_send, gd_recv, d_sems.at[0, 1], d_sems.at[1, 1], (p.e, p.core_peer))
    copy_d.start()
    copy_g.start()
    copy_d.wait_recv()

    def piece(x):
        return nf.at[tokens(p.c), pl.ds(pl.multiple_of(x * z.half_width, LANES), z.half_width)]

    piece(p.x)[...] = (
        acc[tokens(p.c), 0 : z.half_width] + d_recv[...].astype(F32)
    ).astype(BF16)
    to_x = remote(piece(p.x), piece(p.x), d_sems.at[0, 2], d_sems.at[1, 2], (p.e, p.x_peer))
    to_core = remote(piece(p.x), piece(p.x), d_sems.at[0, 3], d_sems.at[1, 3], (p.e, p.core_peer))
    on_to_core = remote(
        piece(1 - p.x), piece(1 - p.x), d_sems.at[0, 4], d_sems.at[1, 4], (p.e, p.core_peer)
    )
    to_x.start()
    to_core.start()
    copy_g.wait_recv()
    gg_out[...] = acc[:, z.half_width :] + gd_recv[...].astype(F32)

    def finish(k):
        b.finish(k)
        for d in range(1, 4):
            gg_copy(k, d).wait_send()

        @pl.when(k > 0)
        def _():
            g.finish(k)
            gate_copy(k).wait_send()
            gg_copy(k, 0).wait_send()

        for copy in save(k):
            copy.wait()

    loop(0, experts, finish)
    to_x.wait_recv()
    on_to_core.start()
    to_core.wait_recv()
    on_to_core.wait_recv()
    nf_out[...] = nf[...]
    for copy in (copy_d, copy_g, to_x, to_core, on_to_core):
        copy.wait_send()


def run_experts(z, inputs, mixed_all, wao_full, gain_ffn, weight_router, rk_col, rk_row, w_in, hg):
    e = z.experts
    hidden_count = w_in.shape[1]
    rows_shape = jax.ShapeDtypeStruct((e, z.slots, z.width), BF16)
    hid_shape = jax.ShapeDtypeStruct((e, z.slots, hidden_count), BF16)
    half_seq = z.seq // 2
    return pl.pallas_call(
        functools.partial(experts_kernel, z),
        out_shape=(
            jax.ShapeDtypeStruct((z.seq, z.width), F32),
            jax.ShapeDtypeStruct((z.seq, z.width), BF16),
            jax.ShapeDtypeStruct((z.seq, LANES), F32),
            jax.ShapeDtypeStruct((z.seq, z.width), BF16),
            jax.ShapeDtypeStruct((z.seq, LANES), F32),
            jax.ShapeDtypeStruct((e, 1, z.slot_lanes), F32),
            rows_shape,
            hid_shape,
            hid_shape,
        ),
        in_specs=[VMEM_SPEC] * 9,
        out_specs=(VMEM_SPEC,) * 6 + (ANY_SPEC,) * 3,
        scratch_shapes=gather_scratch(z)
        + return_scratch(z)
        + [
            pltpu.VMEM((e, z.slots, hidden_count), BF16),
            pltpu.VMEM((e, z.slots, hidden_count), BF16),
            pltpu.VMEM((z.width, LANES), BF16),
            pltpu.VMEM((LANES, z.seq), F32),
            pltpu.VMEM((e, 1, z.slot_lanes), F32),
            pltpu.VMEM((e, 1, z.slot_lanes), F32),
            pltpu.VMEM((e, 4, 1, z.slot_lanes), F32),
            pltpu.VMEM((z.seq, z.half_width + LANES), F32),
            pltpu.VMEM((z.half, z.half_width + LANES), BF16),
            pltpu.VMEM((half_seq, z.half_width), BF16),
            pltpu.VMEM((half_seq, z.half_width), BF16),
            pltpu.VMEM((z.seq, LANES), BF16),
            pltpu.VMEM((z.seq, LANES), BF16),
            pltpu.VMEM((z.seq, z.width), BF16),
            pltpu.SemaphoreType.DMA((2, e)),
            pltpu.SemaphoreType.DMA((2, e, 4)),
            pltpu.SemaphoreType.DMA((3, e)),
            pltpu.SemaphoreType.DMA((2, 5)),
        ],
        compiler_params=pltpu.CompilerParams(
            collective_id=2, has_side_effects=True, vmem_limit_bytes=VMEM_LIMIT
        ),
        name="run_experts",
    )(
        inputs, mixed_all, wao_full, gain_ffn.reshape(1, -1), weight_router, rk_col, rk_row,
        w_in, hg,
    )


def results_kernel(
    z, hid_ref, w_out_ref, rk_col, gates_ref, mid_ref, out_ref,
    part, from_core, stage_x, from_x, ret, r_send, r_recv,
    acc, d_send, d_recv, d_sems,
):
    p = Place(z)
    p.greet()
    b = Return(z, p, part, from_core, stage_x, from_x, ret, r_send, r_recv)

    def body(i):
        @pl.when(i < z.experts)
        def _():
            for j in range(0, z.width, COL_TILE):
                part[i, :, j : j + COL_TILE] = dot_nn(
                    hid_ref[i], w_out_ref[:, j : j + COL_TILE]
                ).astype(BF16)
            b.first(i)

        @pl.when((i >= 1) & (i <= z.experts))
        def _():
            b.second(i - 1)

        @pl.when(i >= 2)
        def _():
            b.third(i - 2)

    loop(0, z.experts + 2, body)
    acc[...] = jnp.zeros_like(acc)

    def combine(k):
        b.arrive(k)
        who = p.ahead(k)
        for r in range(0, z.seq, ROW_TILE):
            rows = slice(r, r + ROW_TILE)
            rank = pick_lane(rk_col[rows, :], who) - lax.convert_element_type(p.c * z.half, F32)
            slot = lax.broadcasted_iota(jnp.int32, (ROW_TILE, z.half), 1).astype(F32)
            pick = jnp.where(rank == slot, 1.0, 0.0).astype(BF16)
            acc[rows, :] += pick_lane(gates_ref[rows, :], who) * dot_nn(pick, ret[k])

    loop(0, z.experts, combine)
    own = z.half_width // 2
    first = acc[:, 0:own]
    second = acc[:, own:]
    d_send[...] = jnp.where(p.c == 0, second, first).astype(BF16)
    copy = remote(d_send, d_recv, d_sems.at[0], d_sems.at[1], (p.e, p.core_peer))
    copy.start()
    mid = mid_ref[:, pl.ds(pl.multiple_of(p.x * z.half_width, LANES), z.half_width)]
    mine = jnp.where(p.c == 0, first + mid[:, 0:own], second + mid[:, own:])
    copy.wait_recv()
    out_ref[...] = (mine + d_recv[...].astype(F32)).astype(BF16)
    copy.wait_send()
    loop(0, z.experts, b.finish)


def return_results(z, hid, w_out, rk_col, gates, mid):
    own = z.half_width // 2
    return pl.pallas_call(
        functools.partial(results_kernel, z),
        out_shape=jax.ShapeDtypeStruct((z.seq, own), BF16),
        in_specs=[VMEM_SPEC] * 5,
        out_specs=VMEM_SPEC,
        scratch_shapes=return_scratch(z)
        + [
            pltpu.VMEM((z.seq, z.half_width), F32),
            pltpu.VMEM((z.seq, own), BF16),
            pltpu.VMEM((z.seq, own), BF16),
            pltpu.SemaphoreType.DMA((2,)),
        ],
        compiler_params=pltpu.CompilerParams(
            collective_id=3, has_side_effects=True, vmem_limit_bytes=VMEM_LIMIT
        ),
        name="return_results",
    )(hid, w_out, rk_col, gates, mid)


def far_limits(buckets):
    half_size = buckets // 2
    base_ratio = 256.0 / buckets
    return [
        int(math.ceil(half_size * base_ratio ** (step / half_size))) for step in range(1, half_size)
    ]


def bucket_of(distance, buckets):
    half_size = buckets // 2
    limits = jnp.array(far_limits(buckets), dtype=jnp.int32)
    far_bucket = half_size + jnp.sum((distance[..., None] >= limits).astype(jnp.int32), axis=-1)
    return jnp.where(distance < half_size, distance, far_bucket)


def block_onehot(offset, wide_count, buckets):
    distance = jnp.maximum(offset + jnp.arange(wide_count, dtype=jnp.int32), 0)
    return (
        bucket_of(distance, buckets)[:, None] == jnp.arange(buckets, dtype=jnp.int32)[None, :]
    ).astype(jnp.float32)


def block_bias(diagonal_values, row_count, col_count):
    head_count, wide_count = diagonal_values.shape
    pattern = jnp.concatenate(
        [
            diagonal_values[:, :col_count][:, ::-1],
            jnp.zeros((head_count, 1), diagonal_values.dtype),
            diagonal_values[:, col_count:][:, ::-1],
        ],
        axis=1,
    )
    repeated = jnp.tile(pattern, (1, row_count))[:, : row_count * wide_count]
    return repeated.reshape(head_count, row_count, wide_count)[:, :, :col_count]


def block_allowed(positions, segments, row_start, key_len):
    return (positions[None, :key_len] <= positions[row_start:key_len, None]) & (
        segments[row_start:key_len, None] == segments[None, :key_len]
    )


def gather_diagonals(grid, row_count, col_count):
    head_count = grid.shape[0]
    wide_count = row_count + col_count - 1
    flipped = jnp.pad(grid[:, :, ::-1], ((0, 0), (0, 0), (0, row_count)))
    flat_rows = flipped.reshape(head_count, row_count * (row_count + col_count))[
        :, : row_count * wide_count
    ]
    return jnp.sum(flat_rows.reshape(head_count, row_count, wide_count), axis=1, dtype=jnp.float32)


def block_scores(query_block, key_block, bias_block, allowed, score_scale):
    scores = (
        jnp.einsum("qhd,khd->hqk", query_block, key_block, preferred_element_type=jnp.float32)
        * score_scale
        + bias_block
    )
    return jnp.where(allowed[None], scores, negative)


def norm_back(row_grads, unit_rows, root_rows, gain_vector):
    unit_grads = row_grads * gain_vector
    return root_rows * (
        unit_grads - unit_rows * jnp.mean(unit_grads * unit_rows, axis=-1, keepdims=True)
    )


def per_device(
    inputs,
    gain_attn,
    gain_ffn,
    weight_qkv,
    weight_attn_out,
    rel_table,
    weight_router,
    weight_in,
    weight_out,
    routes,
    segments,
    cotangent,
):
    seq_len, width = inputs.shape
    heads_local = rel_table.shape[1]
    col_width = weight_qkv.shape[2]
    head_size = col_width // heads_local
    score_scale = head_size ** (-0.5)
    block_rows = min(BLOCK, seq_len)
    block_count = seq_len // block_rows
    experts = weight_router.shape[1]
    top_count = routes.shape[1]
    stream_in = inputs.astype(jnp.float32)
    root_attn = lax.rsqrt(jnp.mean(stream_in * stream_in, axis=-1, keepdims=True) + epsilon)
    unit_attn = stream_in * root_attn
    normed_attn = (unit_attn * gain_attn).astype(jnp.bfloat16)
    projected = jnp.einsum(
        "td,kdc->ktc", normed_attn, weight_qkv, preferred_element_type=jnp.float32
    ).astype(jnp.bfloat16)
    queries = projected[0].reshape(seq_len, heads_local, head_size)
    keys_all = projected[1].reshape(seq_len, heads_local, head_size)
    values_all = projected[2].reshape(seq_len, heads_local, head_size)
    positions = jnp.arange(seq_len, dtype=jnp.int32)
    onehot_list, diagonal_list, log_sums, mixed_parts = ([], [], [], [])
    for which_block in range(block_count):
        row_start = which_block * block_rows
        key_len = row_start + block_rows
        wide_count = block_rows + key_len - 1
        onehot_block = block_onehot(row_start - (key_len - 1), wide_count, BUCKETS)
        allowed = block_allowed(positions, segments, row_start, key_len)
        diagonal_values = jnp.einsum("bh,wb->hw", rel_table, onehot_block, precision=highest)
        bias_block = block_bias(diagonal_values, block_rows, key_len)
        scores = block_scores(
            queries[row_start:key_len], keys_all[:key_len], bias_block, allowed, score_scale
        )
        row_peak = jnp.max(scores, axis=-1, keepdims=True)
        exp_scores = jnp.exp(scores - row_peak)
        row_total = jnp.sum(exp_scores, axis=-1, keepdims=True)
        probs_low = (exp_scores / row_total).astype(jnp.bfloat16)
        mixed_parts.append(
            jnp.einsum(
                "hqk,khd->qhd", probs_low, values_all[:key_len], preferred_element_type=jnp.float32
            )
        )
        log_sums.append(row_peak + jnp.log(row_total))
        onehot_list.append(onehot_block)
        diagonal_list.append(diagonal_values)
    mixed_heads = (
        jnp.concatenate(mixed_parts, axis=0).reshape(seq_len, col_width).astype(jnp.bfloat16)
    )
    z = Sizes(experts, seq_len, top_count, width)
    cot_full = lax.all_gather(cotangent, "tensor", axis=1, tiled=True)
    rk_col, rk_row, og_rows, hg = send_grads(z, routes, cot_full, weight_out[0])
    mixed_all = lax.all_gather(mixed_heads, "tensor", axis=1, tiled=True)
    wao_full = lax.all_gather(weight_attn_out, "tensor", axis=0, tiled=True)
    stream_mid, normed_ffn, gates, normed_part, gate_pairs, gate_slots, slot_rows, hidden, pre_grads = run_experts(
        z, inputs, mixed_all, wao_full, gain_ffn, weight_router, rk_col, rk_row, weight_in[0], hg
    )
    activations = return_results(z, hidden, weight_out[0], rk_col, gates, stream_mid)
    flat = (experts * z.slots, -1)
    grad_weight_in = jnp.einsum(
        "sd,sf->df", slot_rows.reshape(flat), pre_grads.reshape(flat), preferred_element_type=jnp.float32
    )[None]
    slot_grads = (gate_slots[:, 0, : z.slots, None] * og_rows.astype(jnp.float32)).astype(jnp.bfloat16)
    grad_weight_out = jnp.einsum(
        "sf,sd->fd", hidden.reshape(flat), slot_grads.reshape(flat), preferred_element_type=jnp.float32
    )[None]
    root_ffn = lax.rsqrt(jnp.mean(stream_mid * stream_mid, axis=-1, keepdims=True) + epsilon)
    unit_ffn = stream_mid * root_ffn
    gate_weights = gates[:, :experts]
    gate_grads = gate_pairs[:, :experts] + gate_pairs[:, experts : 2 * experts]
    logit_grads = (gate_weights * (
        gate_grads - jnp.sum(gate_weights * gate_grads, axis=-1, keepdims=True)
    )).astype(jnp.bfloat16)
    grad_weight_router = jnp.einsum(
        "td,te->de", normed_ffn, logit_grads, preferred_element_type=jnp.float32
    )
    router_back = jnp.einsum(
        "te,de->td", logit_grads, weight_router, preferred_element_type=jnp.float32
    )
    normed_grads = normed_part.astype(jnp.float32) + router_back
    grad_gain_ffn = jnp.sum(normed_grads * unit_ffn, axis=0)
    mid_grads = cot_full.astype(jnp.float32) + norm_back(normed_grads, unit_ffn, root_ffn, gain_ffn)
    attn_grads = mid_grads.astype(jnp.bfloat16)
    grad_weight_attn_out = jnp.einsum(
        "tc,td->cd", mixed_heads, attn_grads, preferred_element_type=jnp.float32
    )
    mixed_grads = jnp.einsum(
        "td,cd->tc", attn_grads, weight_attn_out, preferred_element_type=jnp.float32
    )
    mixed_grads = mixed_grads.astype(jnp.bfloat16).reshape(seq_len, heads_local, head_size)
    key_grads = jnp.zeros((seq_len, heads_local, head_size), jnp.float32)
    value_grads = jnp.zeros((seq_len, heads_local, head_size), jnp.float32)
    table_grad = jnp.zeros((BUCKETS, heads_local), jnp.float32)
    query_parts = []
    for which_block in range(block_count):
        row_start = which_block * block_rows
        key_len = row_start + block_rows
        allowed = block_allowed(positions, segments, row_start, key_len)
        bias_block = block_bias(diagonal_list[which_block], block_rows, key_len)
        scores = block_scores(
            queries[row_start:key_len], keys_all[:key_len], bias_block, allowed, score_scale
        )
        attn_probs = jnp.exp(scores - log_sums[which_block])
        probs_low = attn_probs.astype(jnp.bfloat16)
        grad_rows = mixed_grads[row_start:key_len]
        prob_grads = jnp.einsum(
            "qhd,khd->hqk", grad_rows, values_all[:key_len], preferred_element_type=jnp.float32
        )
        value_part = jnp.einsum(
            "hqk,qhd->khd", probs_low, grad_rows, preferred_element_type=jnp.float32
        )
        value_grads = value_grads + jnp.pad(value_part, ((0, seq_len - key_len), (0, 0), (0, 0)))
        row_dots = jnp.sum(attn_probs * prob_grads, axis=-1, keepdims=True)
        score_grads = (attn_probs * (prob_grads - row_dots)).astype(jnp.bfloat16)
        query_parts.append(
            jnp.einsum(
                "hqk,khd->qhd", score_grads, keys_all[:key_len], preferred_element_type=jnp.float32
            )
            * score_scale
        )
        key_part = (
            jnp.einsum(
                "hqk,qhd->khd",
                score_grads,
                queries[row_start:key_len],
                preferred_element_type=jnp.float32,
            )
            * score_scale
        )
        key_grads = key_grads + jnp.pad(key_part, ((0, seq_len - key_len), (0, 0), (0, 0)))
        diagonal_grads = gather_diagonals(score_grads, block_rows, key_len)
        table_grad = table_grad + jnp.einsum(
            "hw,wb->bh", diagonal_grads, onehot_list[which_block], precision=highest
        )
    qkv_grads = jnp.stack(
        [
            jnp.concatenate(query_parts, axis=0).reshape(seq_len, col_width),
            key_grads.reshape(seq_len, col_width),
            value_grads.reshape(seq_len, col_width),
        ],
        axis=0,
    ).astype(jnp.bfloat16)
    grad_weight_qkv = jnp.einsum(
        "td,ktc->kdc", normed_attn, qkv_grads, preferred_element_type=jnp.float32
    )
    normed_attn_part = jnp.einsum(
        "ktc,kdc->td", qkv_grads, weight_qkv, preferred_element_type=jnp.float32
    )
    normed_attn_grads = lax.psum(normed_attn_part, "tensor")
    grad_gain_attn = jnp.sum(normed_attn_grads * unit_attn, axis=0)
    grad_input = mid_grads + norm_back(normed_attn_grads, unit_attn, root_attn, gain_attn)
    shared = lax.psum(
        (
            grad_gain_attn,
            grad_gain_ffn,
            grad_weight_qkv,
            grad_weight_attn_out,
            table_grad,
            grad_weight_router,
        ),
        "expert",
    )
    return (
        activations,
        grad_input,
        shared[0],
        shared[1],
        shared[2],
        shared[3],
        shared[4],
        shared[5],
        grad_weight_in,
        grad_weight_out,
    )


def solution(mesh):
    in_specs = (
        P("expert", None),
        P(),
        P(),
        P(None, None, "tensor"),
        P("tensor", None),
        P(None, "tensor"),
        P(),
        P("expert", None, "tensor"),
        P("expert", "tensor", None),
        P("expert", None),
        P("expert"),
        P("expert", "tensor"),
    )
    out_specs = (
        P("expert", "tensor"),
        P("expert", None),
        P(),
        P(),
        P(None, None, "tensor"),
        P("tensor", None),
        P(None, "tensor"),
        P(),
        P("expert", None, "tensor"),
        P("expert", "tensor", None),
    )
    return jax.shard_map(
        per_device, mesh=mesh, in_specs=in_specs, out_specs=out_specs, check_vma=False
    )
```

```python
import functools
import math

import jax
import jax.numpy as jnp
from jax import lax
from jax.experimental import pallas as pl
from jax.experimental.pallas import tpu as pltpu
from jax.sharding import PartitionSpec as P

BUCKETS = 32
epsilon = 1e-06
negative = -1e30
F32 = jnp.float32
BF16 = jnp.bfloat16
MESH = pl.DeviceIdType.MESH
VMEM_SPEC = pl.BlockSpec(memory_space=pltpu.VMEM)
ANY_SPEC = pl.BlockSpec(memory_space=pl.ANY)
LANES = 128
ROW_TILE = 256
COL_TILE = 256
VMEM_LIMIT = 60 * 2**20


def dot_nn(left, right):
    return lax.dot_general(left, right, (((1,), (0,)), ((), ())), preferred_element_type=F32)


def dot_nt(left, right):
    return lax.dot_general(left, right, (((1,), (1,)), ((), ())), preferred_element_type=F32)


def dot_tn(left, right):
    return lax.dot_general(left, right, (((0,), (0,)), ((), ())), preferred_element_type=F32)


def round_up(value, step):
    return (value + step - 1) // step * step


class Sizes:
    def __init__(self, experts, seq_len, top_count, width):
        self.experts = experts
        self.seq = seq_len
        self.width = width
        self.half_width = width // 2
        capacity = (4 * seq_len * top_count + 24 * experts - 1) // (24 * experts) * 8
        self.slots = round_up(capacity, 32)
        self.half = self.slots // 2
        self.slot_lanes = round_up(self.slots, LANES)


class Place:
    def __init__(self, sizes):
        self.count = sizes.experts
        self.e = lax.axis_index("expert")
        self.t = lax.axis_index("tensor")
        self.c = lax.rem(self.t, 2)
        self.x = lax.div(self.t, 2)
        self.core_peer = self.t + 1 - 2 * self.c
        self.x_peer = lax.rem(self.t + 2, 4)

    def ahead(self, k):
        return lax.rem(self.e + k, self.count)

    def behind(self, k):
        return lax.rem(self.e + self.count - k, self.count)

    def greet(self, expert_peers=True, all_tensor=True):
        barrier = pltpu.get_barrier_semaphore()
        count = 0
        if expert_peers:

            def one(k, carry):
                pl.semaphore_signal(
                    barrier, inc=1, device_id=(self.ahead(k), self.t), device_id_type=MESH
                )
                return carry

            lax.fori_loop(1, self.count, one, 0)
            count += self.count - 1
        for d in range(1, 4):
            pl.semaphore_signal(
                barrier,
                inc=1,
                device_id=(self.e, lax.rem(self.t + d, 4)),
                device_id_type=MESH,
            )
        count += 3
        pl.semaphore_wait(barrier, count)


def remote(src, dst, send_sem, recv_sem, device):
    return pltpu.make_async_remote_copy(
        src_ref=src,
        dst_ref=dst,
        send_sem=send_sem,
        recv_sem=recv_sem,
        device_id=device,
        device_id_type=MESH,
    )


class Gather:
    sem_kinds = 4

    def __init__(self, sizes, place, stage, buf, send, recv):
        self.z, self.p = sizes, place
        self.stage, self.buf, self.send, self.recv = stage, buf, send, recv

    def quarter(self, k, c, x):
        h, w = self.z.half, self.z.half_width
        return self.buf.at[
            k, pl.ds(pl.multiple_of(c * h, 16), h), pl.ds(pl.multiple_of(x * w, LANES), w)
        ]

    def out(self, k):
        p = self.p
        return remote(
            self.stage.at[k],
            self.quarter(k, p.c, p.x),
            self.send.at[0, k],
            self.recv.at[0, k],
            (p.ahead(k), p.t),
        )

    def to_core(self, k):
        p = self.p
        ref = self.quarter(k, p.c, p.x)
        return remote(ref, ref, self.send.at[1, k], self.recv.at[1, k], (p.e, p.core_peer))

    def to_x(self, k):
        p = self.p
        ref = self.quarter(k, p.c, p.x)
        return remote(ref, ref, self.send.at[2, k], self.recv.at[2, k], (p.e, p.x_peer))

    def on_to_core(self, k):
        p = self.p
        ref = self.quarter(k, p.c, 1 - p.x)
        return remote(ref, ref, self.send.at[3, k], self.recv.at[3, k], (p.e, p.core_peer))

    def pack_own(self, rk_row, rows_ref):
        z, p = self.z, self.p
        pick = slot_onehot(rk_row[pl.ds(p.e, 1), :], z.slots, 0)
        for j in range(0, z.width, COL_TILE):
            self.buf[0, :, j : j + COL_TILE] = dot_nn(
                pick, rows_ref[:, j : j + COL_TILE]
            ).astype(BF16)

    def pack(self, k, pick, rows_ref):
        z, p = self.z, self.p
        cols = rows_ref[:, pl.ds(pl.multiple_of(p.x * z.half_width, LANES), z.half_width)]
        self.stage[k] = dot_nn(pick, cols).astype(BF16)

    def first(self, k):
        self.out(k).wait_recv()
        self.to_core(k).start()
        self.to_x(k).start()

    def second(self, k):
        self.to_x(k).wait_recv()
        self.on_to_core(k).start()

    def last(self, k):
        self.to_core(k).wait_recv()
        self.on_to_core(k).wait_recv()

    def finish(self, k):
        self.out(k).wait_send()
        self.to_core(k).wait_send()
        self.to_x(k).wait_send()
        self.on_to_core(k).wait_send()


class Return:
    sem_kinds = 3

    def __init__(self, sizes, place, part, from_core, stage_x, from_x, ret, send, recv):
        self.z, self.p = sizes, place
        self.part, self.from_core, self.stage_x = part, from_core, stage_x
        self.from_x, self.ret = from_x, ret
        self.send, self.recv = send, recv

    def rows(self, c):
        return pl.ds(pl.multiple_of(c * self.z.half, 16), self.z.half)

    def cols(self, x):
        return pl.ds(pl.multiple_of(x * self.z.half_width, LANES), self.z.half_width)

    def to_core(self, k):
        p = self.p
        return remote(
            self.part.at[k, self.rows(1 - p.c), :],
            self.from_core.at[k],
            self.send.at[0, k],
            self.recv.at[0, k],
            (p.e, p.core_peer),
        )

    def to_x(self, k):
        p = self.p
        return remote(
            self.stage_x.at[k],
            self.from_x.at[k],
            self.send.at[1, k],
            self.recv.at[1, k],
            (p.e, p.x_peer),
        )

    def home(self, k):
        p = self.p
        return remote(
            self.from_core.at[k, :, self.cols(p.x)],
            self.ret.at[k],
            self.send.at[2, k],
            self.recv.at[2, k],
            (p.behind(k), p.t),
        )

    def first(self, k):
        self.to_core(k).start()

    def second(self, k):
        p = self.p
        self.to_core(k).wait_recv()
        rows = self.rows(p.c)
        for x in (1 - p.x, p.x):
            cols = self.cols(x)
            both = self.part[k, rows, cols].astype(F32) + self.from_core[k, :, cols].astype(F32)
            if x is p.x:
                self.from_core[k, :, cols] = both.astype(BF16)
            else:
                self.stage_x[k] = both.astype(BF16)
                self.to_x(k).start()

    def third(self, k):
        self.to_x(k).wait_recv()
        cols = self.cols(self.p.x)
        total = self.from_core[k, :, cols].astype(F32) + self.from_x[k].astype(F32)

        @pl.when(k == 0)
        def _():
            self.ret[0] = total.astype(BF16)

        @pl.when(k > 0)
        def _():
            self.from_core[k, :, cols] = total.astype(BF16)
            self.home(k).start()

    def arrive(self, k):
        @pl.when(k > 0)
        def _():
            self.home(k).wait_recv()

    def finish(self, k):
        self.to_core(k).wait_send()
        self.to_x(k).wait_send()

        @pl.when(k > 0)
        def _():
            self.home(k).wait_send()


def return_scratch(z):
    e, h, w = z.experts, z.half, z.half_width
    return [
        pltpu.VMEM((e, z.slots, z.width), BF16),
        pltpu.VMEM((e, h, z.width), BF16),
        pltpu.VMEM((e, h, w), BF16),
        pltpu.VMEM((e, h, w), BF16),
        pltpu.VMEM((e, h, w), BF16),
        pltpu.SemaphoreType.DMA((Return.sem_kinds, e)),
        pltpu.SemaphoreType.DMA((Return.sem_kinds, e)),
    ]


def gather_scratch(z):
    e, h, w = z.experts, z.half, z.half_width
    return [
        pltpu.VMEM((e, h, w), BF16),
        pltpu.VMEM((e, z.slots, z.width), BF16),
        pltpu.SemaphoreType.DMA((Gather.sem_kinds, e)),
        pltpu.SemaphoreType.DMA((Gather.sem_kinds, e)),
    ]


def slot_onehot(rank_row, count, offset):
    slot = lax.broadcasted_iota(jnp.int32, (count, rank_row.shape[1]), 0).astype(F32)
    shift = lax.convert_element_type(offset, F32)
    return jnp.where(rank_row - shift == slot, 1.0, 0.0).astype(BF16)


def pick_lane(values, lane):
    lanes = lax.broadcasted_iota(jnp.int32, values.shape, 1)
    return jnp.sum(jnp.where(lanes == lane, values, 0.0), axis=1, keepdims=True)


def row_to_col(row, count, offset):
    rows = lax.broadcasted_iota(jnp.int32, (count, row.shape[1]), 0) + offset
    lanes = lax.broadcasted_iota(jnp.int32, (count, row.shape[1]), 1)
    return jnp.sum(jnp.where(rows == lanes, row, 0.0), axis=1, keepdims=True)


def col_to_row(col, lane_count):
    rows = lax.broadcasted_iota(jnp.int32, (col.shape[0], lane_count), 0)
    lanes = lax.broadcasted_iota(jnp.int32, (col.shape[0], lane_count), 1)
    return jnp.sum(jnp.where(rows == lanes, col, 0.0), axis=0, keepdims=True)


def loop(start, stop, body):
    def step(i, carry):
        body(i)
        return carry

    lax.fori_loop(start, stop, step, 0)


def fill_ranks(routes_ref, rk_col, rk_row):
    seq = routes_ref.shape[0]
    ids = lax.broadcasted_iota(jnp.int32, (seq, LANES), 1)
    routes = routes_ref[...]
    hot = (routes[:, 0:1] == ids) | (routes[:, 1:2] == ids)
    hot_low = jnp.where(hot, 1.0, 0.0).astype(BF16)
    hot_mark = jnp.where(hot, 1.0, 0.0)
    for r in range(0, seq, ROW_TILE):
        rows = lax.broadcasted_iota(jnp.int32, (ROW_TILE, seq), 0) + r
        cols = lax.broadcasted_iota(jnp.int32, (ROW_TILE, seq), 1)
        before = jnp.where(cols < rows, 1.0, 0.0).astype(BF16)
        rank = dot_nn(before, hot_low)
        rank = jnp.where(hot_mark[r : r + ROW_TILE] > 0.5, rank, -1.0)
        rk_col[r : r + ROW_TILE, :] = rank
        rk_row[:, r : r + ROW_TILE] = rank.T


def gelu_pair(h):
    scale = 0.7978845608028654
    square = h * h
    t = jnp.tanh(scale * h * (1.0 + 0.044715 * square))
    half = 0.5 + 0.5 * t
    slope = half + (0.5 * scale) * h * (1.0 - t * t) * (1.0 + 0.134145 * square)
    return h * half, slope


def experts_kernel(
    z, x_ref, mixed_ref, wao_ref, gain_ref, wr_ref, rk_col, rk_row, w_in_ref, hg_ref,
    mid_ref, nrm_ref, gates_ref, nf_out, gg_out, gs_in, rows_out, hid_out, pre_out,
    stage, buf, g_send, g_recv,
    part, from_core, stage_x, from_x, ret, r_send, r_recv,
    hid, pre, wr_pad, gate_row, gs_out, gg_send, gg_recv, acc, retx,
    d_send, d_recv, gd_send, gd_recv, nf,
    gs_sems, gg_sems, out_sem, d_sems,
):
    p = Place(z)
    experts = z.experts
    wr_pad[...] = jnp.zeros_like(wr_pad)
    wr_pad[:, 0:experts] = wr_ref[...]
    for r in range(0, z.seq, ROW_TILE):
        rows = slice(r, r + ROW_TILE)
        mid = x_ref[rows, :].astype(F32) + dot_nn(mixed_ref[rows, :], wao_ref[...])
        mid_ref[rows, :] = mid
        root = lax.rsqrt(jnp.mean(mid * mid, axis=1, keepdims=True) + epsilon)
        nrm = (mid * root * gain_ref[...]).astype(BF16)
        nrm_ref[rows, :] = nrm
        logits = dot_nn(nrm, wr_pad[...])
        hot = rk_col[rows, :] > -0.5
        logits = jnp.where(hot, logits, negative)
        peak = jnp.max(logits, axis=1, keepdims=True)
        power = jnp.where(hot, jnp.exp(logits - peak), 0.0)
        gates = power / jnp.sum(power, axis=1, keepdims=True)
        gates_ref[rows, :] = gates
        gate_row[:, rows] = gates.T
    p.greet()
    g = Gather(z, p, stage, buf, g_send, g_recv)
    b = Return(z, p, part, from_core, stage_x, from_x, ret, r_send, r_recv)

    def gate_copy(k):
        return remote(
            gs_out.at[k], gs_in.at[k], gs_sems.at[0, k], gs_sems.at[1, k], (p.ahead(k), p.t)
        )

    def slot_gates(k):
        pick = slot_onehot(rk_row[pl.ds(p.ahead(k), 1), :], z.slot_lanes, 0)
        row = gate_row[pl.ds(p.ahead(k), 1), :]
        high = row.astype(BF16).astype(F32)
        low = row - high
        which = lax.broadcasted_iota(jnp.int32, (16, z.seq), 0)
        both = jnp.where(which == 0, high, jnp.where(which == 1, low, 0.0)).astype(BF16)
        sums = dot_nt(both, pick)
        return sums[0:1, :] + sums[1:2, :]

    def pack(k):
        pick = slot_onehot(rk_row[pl.ds(p.ahead(k), 1), :], z.half, p.c * z.half)
        g.pack(k, pick, nrm_ref)
        g.out(k).start()

    loop(1, experts, pack)

    def send_gates(k):
        gs_out[k] = slot_gates(k)
        gate_copy(k).start()

    loop(1, experts, send_gates)
    gs_in[0] = slot_gates(0)
    g.pack_own(rk_row, nrm_ref)

    def gg_copy(k, d):
        return remote(
            gg_send.at[k],
            gg_recv.at[k, p.t],
            gg_sems.at[0, k, d],
            gg_sems.at[1, k, d],
            (p.behind(k), lax.rem(p.t + d, 4)),
        )

    def save(k):
        return (
            pltpu.make_async_copy(buf.at[k], rows_out.at[k], out_sem.at[0, k]),
            pltpu.make_async_copy(hid.at[k], hid_out.at[k], out_sem.at[1, k]),
            pltpu.make_async_copy(pre.at[k], pre_out.at[k], out_sem.at[2, k]),
        )

    def expert(k):
        @pl.when(k > 0)
        def _():
            gate_copy(k).wait_recv()
            g.last(k)

        gate = row_to_col(gs_in[k], z.slots, 0)
        sums = jnp.zeros((z.slots, 1), F32)
        for j in range(0, w_in_ref.shape[1], COL_TILE):
            cols = slice(j, j + COL_TILE)
            up, slope = gelu_pair(dot_nn(buf[k], w_in_ref[:, cols]))
            back = hg_ref[k, :, cols].astype(F32)
            hid[k, :, cols] = up.astype(BF16)
            pre[k, :, cols] = (gate * back * slope).astype(BF16)
            sums = sums + jnp.sum(up * back, axis=1, keepdims=True)
        for j in range(0, z.width, COL_TILE):
            part[k, :, j : j + COL_TILE] = dot_nt(
                pre[k], w_in_ref[j : j + COL_TILE, :]
            ).astype(BF16)
        b.first(k)
        gg_send[k] = col_to_row(sums, z.slot_lanes)
        for d in range(1, 4):
            gg_copy(k, d).start()

        @pl.when(k > 0)
        def _():
            gg_copy(k, 0).start()

        @pl.when(k == 0)
        def _():
            gg_recv[0, p.t] = gg_send[0]

        for copy in save(k):
            copy.start()

    def body(i):
        @pl.when(i < experts)
        def _():
            expert(i)

        @pl.when(i == 0)
        def _():
            g.first(1)

        @pl.when(i + 2 < experts)
        def _():
            g.first(i + 2)

        @pl.when(i + 1 < experts)
        def _():
            g.second(i + 1)

        @pl.when((i >= 1) & (i <= experts))
        def _():
            b.second(i - 1)

        @pl.when(i >= 2)
        def _():
            b.third(i - 2)

    loop(0, experts + 2, body)
    acc[...] = jnp.zeros_like(acc)

    def combine(k):
        b.arrive(k)
        for d in range(1, 4):
            gg_copy(k, d).wait_recv()

        @pl.when(k > 0)
        def _():
            gg_copy(k, 0).wait_recv()

        row = gg_recv[k, 0] + gg_recv[k, 1] + gg_recv[k, 2] + gg_recv[k, 3]
        col = row_to_col(row, z.half, p.c * z.half)
        high = col.astype(BF16).astype(F32)
        lanes = lax.broadcasted_iota(jnp.int32, (z.half, LANES), 1)
        who = p.ahead(k)
        retx[:, 0 : z.half_width] = ret[k]
        retx[:, z.half_width :] = jnp.where(
            lanes == who, high, jnp.where(lanes == who + experts, col - high, 0.0)
        ).astype(BF16)
        for r in range(0, z.seq, ROW_TILE):
            rows = slice(r, r + ROW_TILE)
            rank = pick_lane(rk_col[rows, :], who) - lax.convert_element_type(p.c * z.half, F32)
            slot = lax.broadcasted_iota(jnp.int32, (ROW_TILE, z.half), 1).astype(F32)
            pick = jnp.where(rank == slot, 1.0, 0.0).astype(BF16)
            acc[rows, :] += dot_nn(pick, retx[...])

    loop(0, experts, combine)
    half_seq = z.seq // 2

    def tokens(c):
        return pl.ds(pl.multiple_of(c * half_seq, 16), half_seq)

    d_send[...] = acc[tokens(1 - p.c), 0 : z.half_width].astype(BF16)
    gd_send[...] = acc[:, z.half_width :].astype(BF16)
    copy_d = remote(d_send, d_recv, d_sems.at[0, 0], d_sems.at[1, 0], (p.e, p.core_peer))
    copy_g = remote(gd_send, gd_recv, d_sems.at[0, 1], d_sems.at[1, 1], (p.e, p.core_peer))
    copy_d.start()
    copy_g.start()
    copy_d.wait_recv()

    def piece(x):
        return nf.at[tokens(p.c), pl.ds(pl.multiple_of(x * z.half_width, LANES), z.half_width)]

    piece(p.x)[...] = (
        acc[tokens(p.c), 0 : z.half_width] + d_recv[...].astype(F32)
    ).astype(BF16)
    to_x = remote(piece(p.x), piece(p.x), d_sems.at[0, 2], d_sems.at[1, 2], (p.e, p.x_peer))
    to_core = remote(piece(p.x), piece(p.x), d_sems.at[0, 3], d_sems.at[1, 3], (p.e, p.core_peer))
    on_to_core = remote(
        piece(1 - p.x), piece(1 - p.x), d_sems.at[0, 4], d_sems.at[1, 4], (p.e, p.core_peer)
    )
    to_x.start()
    to_core.start()
    copy_g.wait_recv()
    gg_out[...] = acc[:, z.half_width :] + gd_recv[...].astype(F32)

    def finish(k):
        b.finish(k)
        for d in range(1, 4):
            gg_copy(k, d).wait_send()

        @pl.when(k > 0)
        def _():
            g.finish(k)
            gate_copy(k).wait_send()
            gg_copy(k, 0).wait_send()

        for copy in save(k):
            copy.wait()

    loop(0, experts, finish)
    to_x.wait_recv()
    on_to_core.start()
    to_core.wait_recv()
    on_to_core.wait_recv()
    nf_out[...] = nf[...]
    for copy in (copy_d, copy_g, to_x, to_core, on_to_core):
        copy.wait_send()


def run_experts(z, inputs, mixed_all, wao_full, gain_ffn, weight_router, rk_col, rk_row, w_in, hg):
    e = z.experts
    hidden_count = w_in.shape[1]
    rows_shape = jax.ShapeDtypeStruct((e, z.slots, z.width), BF16)
    hid_shape = jax.ShapeDtypeStruct((e, z.slots, hidden_count), BF16)
    half_seq = z.seq // 2
    return pl.pallas_call(
        functools.partial(experts_kernel, z),
        out_shape=(
            jax.ShapeDtypeStruct((z.seq, z.width), F32),
            jax.ShapeDtypeStruct((z.seq, z.width), BF16),
            jax.ShapeDtypeStruct((z.seq, LANES), F32),
            jax.ShapeDtypeStruct((z.seq, z.width), BF16),
            jax.ShapeDtypeStruct((z.seq, LANES), F32),
            jax.ShapeDtypeStruct((e, 1, z.slot_lanes), F32),
            rows_shape,
            hid_shape,
            hid_shape,
        ),
        in_specs=[VMEM_SPEC] * 9,
        out_specs=(VMEM_SPEC,) * 6 + (ANY_SPEC,) * 3,
        scratch_shapes=gather_scratch(z)
        + return_scratch(z)
        + [
            pltpu.VMEM((e, z.slots, hidden_count), BF16),
            pltpu.VMEM((e, z.slots, hidden_count), BF16),
            pltpu.VMEM((z.width, LANES), BF16),
            pltpu.VMEM((LANES, z.seq), F32),
            pltpu.VMEM((e, 1, z.slot_lanes), F32),
            pltpu.VMEM((e, 1, z.slot_lanes), F32),
            pltpu.VMEM((e, 4, 1, z.slot_lanes), F32),
            pltpu.VMEM((z.seq, z.half_width + LANES), F32),
            pltpu.VMEM((z.half, z.half_width + LANES), BF16),
            pltpu.VMEM((half_seq, z.half_width), BF16),
            pltpu.VMEM((half_seq, z.half_width), BF16),
            pltpu.VMEM((z.seq, LANES), BF16),
            pltpu.VMEM((z.seq, LANES), BF16),
            pltpu.VMEM((z.seq, z.width), BF16),
            pltpu.SemaphoreType.DMA((2, e)),
            pltpu.SemaphoreType.DMA((2, e, 4)),
            pltpu.SemaphoreType.DMA((3, e)),
            pltpu.SemaphoreType.DMA((2, 5)),
        ],
        compiler_params=pltpu.CompilerParams(
            collective_id=2, has_side_effects=True, vmem_limit_bytes=VMEM_LIMIT
        ),
        name="run_experts",
    )(
        inputs, mixed_all, wao_full, gain_ffn.reshape(1, -1), weight_router, rk_col, rk_row,
        w_in, hg,
    )


def results_kernel(
    z, hid_ref, w_out_ref, rk_col, gates_ref, mid_ref, out_ref,
    part, from_core, stage_x, from_x, ret, r_send, r_recv,
    acc, d_send, d_recv, d_sems,
):
    p = Place(z)
    p.greet()
    b = Return(z, p, part, from_core, stage_x, from_x, ret, r_send, r_recv)

    def body(i):
        @pl.when(i < z.experts)
        def _():
            for j in range(0, z.width, COL_TILE):
                part[i, :, j : j + COL_TILE] = dot_nn(
                    hid_ref[i], w_out_ref[:, j : j + COL_TILE]
                ).astype(BF16)
            b.first(i)

        @pl.when((i >= 1) & (i <= z.experts))
        def _():
            b.second(i - 1)

        @pl.when(i >= 2)
        def _():
            b.third(i - 2)

    loop(0, z.experts + 2, body)
    acc[...] = jnp.zeros_like(acc)

    def combine(k):
        b.arrive(k)
        who = p.ahead(k)
        for r in range(0, z.seq, ROW_TILE):
            rows = slice(r, r + ROW_TILE)
            rank = pick_lane(rk_col[rows, :], who) - lax.convert_element_type(p.c * z.half, F32)
            slot = lax.broadcasted_iota(jnp.int32, (ROW_TILE, z.half), 1).astype(F32)
            pick = jnp.where(rank == slot, 1.0, 0.0).astype(BF16)
            acc[rows, :] += pick_lane(gates_ref[rows, :], who) * dot_nn(pick, ret[k])

    loop(0, z.experts, combine)
    own = z.half_width // 2
    first = acc[:, 0:own]
    second = acc[:, own:]
    d_send[...] = jnp.where(p.c == 0, second, first).astype(BF16)
    copy = remote(d_send, d_recv, d_sems.at[0], d_sems.at[1], (p.e, p.core_peer))
    copy.start()
    mid = mid_ref[:, pl.ds(pl.multiple_of(p.x * z.half_width, LANES), z.half_width)]
    mine = jnp.where(p.c == 0, first + mid[:, 0:own], second + mid[:, own:])
    copy.wait_recv()
    out_ref[...] = (mine + d_recv[...].astype(F32)).astype(BF16)
    copy.wait_send()
    loop(0, z.experts, b.finish)


def return_results(z, hid, w_out, rk_col, gates, mid):
    own = z.half_width // 2
    return pl.pallas_call(
        functools.partial(results_kernel, z),
        out_shape=jax.ShapeDtypeStruct((z.seq, own), BF16),
        in_specs=[VMEM_SPEC] * 5,
        out_specs=VMEM_SPEC,
        scratch_shapes=return_scratch(z)
        + [
            pltpu.VMEM((z.seq, z.half_width), F32),
            pltpu.VMEM((z.seq, own), BF16),
            pltpu.VMEM((z.seq, own), BF16),
            pltpu.SemaphoreType.DMA((2,)),
        ],
        compiler_params=pltpu.CompilerParams(
            collective_id=3, has_side_effects=True, vmem_limit_bytes=VMEM_LIMIT
        ),
        name="return_results",
    )(hid, w_out, rk_col, gates, mid)


def far_limits(buckets):
    half_size = buckets // 2
    base_ratio = 256.0 / buckets
    return [
        int(math.ceil(half_size * base_ratio ** (step / half_size))) for step in range(1, half_size)
    ]


TILE = 256
WINDOW = 3 * TILE
SLOT = 256


def distance_of(lane):
    return jnp.where(lane < WINDOW, 2 * TILE - lane, 2 * TILE + 4 * TILE - lane)


def bucket_grid(distance):
    half_size = BUCKETS // 2
    far = jnp.full(distance.shape, half_size, jnp.int32)
    for limit in far_limits(BUCKETS):
        far = far + jnp.where(distance >= limit, 1, 0)
    return jnp.where(distance < half_size, distance, far)


def fill_bias(table_ref, bias, heads):
    lane = lax.broadcasted_iota(jnp.int32, (1, 4 * TILE), 1)
    distance = distance_of(lane)
    bucket = bucket_grid(distance)
    for h in range(heads):
        values = jnp.full((1, 4 * TILE), negative, F32)
        for b in range(BUCKETS):
            values = jnp.where(bucket == b, table_ref[b, h], values)
        wide = jnp.broadcast_to(values, (TILE, 4 * TILE))
        rolled = pltpu.roll(wide, 0, 1, stride=1, stride_axis=0)
        bias[h] = rolled[:, 0:WINDOW]


def fill_weights(weight_ref, padded):
    padded[...] = jnp.zeros_like(padded)
    for k in range(3):
        padded[:, k * SLOT : k * SLOT + weight_ref.shape[2]] = weight_ref[k]


def head_lanes(rows, h, size):
    lanes = lax.broadcasted_iota(jnp.int32, (rows, SLOT), 1)
    return (lanes >= h * size) & (lanes < (h + 1) * size)


def mask_head(values, h, size):
    keep = head_lanes(values.shape[0], h, size)
    return jnp.where(keep, values, jnp.zeros_like(values))


def tiles_of(seq):
    return range(seq // TILE)


def window_of(i):
    start = max(0, i - 2) * TILE
    return start, (i + 1) * TILE - start


def attention_tile(i, h, size, qkv, seg_col, seg_row, bias):
    start, width = window_of(i)
    query = mask_head(qkv[i * TILE : (i + 1) * TILE, 0:SLOT], h, size)
    keys = qkv[start : start + width, SLOT : 2 * SLOT]
    scores = dot_nt(query, keys) + bias[h, :, WINDOW - width :]
    same = seg_col[i * TILE : (i + 1) * TILE, :] == seg_row[:, start : start + width]
    scores = jnp.where(same, scores, negative)
    power = jnp.exp(scores - jnp.max(scores, axis=1, keepdims=True))
    probs = power * (1.0 / jnp.sum(power, axis=1, keepdims=True))
    return probs.astype(BF16)


def front_kernel(
    z, heads, table_ref, x_ref, gain_ref, wqkv_ref, seg_col, seg_row, routes_ref, cot_ref, w_out_ref,
    rk_col, rk_row, na_ref, qkv, mixed_ref, mc_out, og_out, hg_out, probs_out,
    stage, buf, g_send, g_recv, hg, wp, bias, probs, cot_in, cot_half, mixed_in, mc,
    out_sem, p_sem, c_sems, m_sems,
):
    p = Place(z)
    size = wqkv_ref.shape[2] // heads
    cols = wqkv_ref.shape[2]
    p.greet()
    cot_copy = remote(cot_ref, cot_in, c_sems.at[0], c_sems.at[1], (p.e, p.core_peer))
    cot_copy.start()
    fill_ranks(routes_ref, rk_col, rk_row)
    g = Gather(z, p, stage, buf, g_send, g_recv)

    def in_chip(own, peer):
        return jnp.where(
            p.c == 0,
            jnp.concatenate([own, peer], axis=1),
            jnp.concatenate([peer, own], axis=1),
        )

    cot_copy.wait_recv()
    for r in range(0, z.seq, TILE):
        rows = slice(r, r + TILE)
        cot_half[rows, :] = in_chip(cot_ref[rows, :], cot_in[rows, :])

    def pack(k):
        pick = slot_onehot(rk_row[pl.ds(p.ahead(k), 1), :], z.half, p.c * z.half)
        rows = dot_nn(pick, cot_half[...]).astype(BF16)

        @pl.when(k > 0)
        def _():
            stage[k] = rows
            g.out(k).start()

        @pl.when(k == 0)
        def _():
            g.quarter(0, p.c, p.x)[...] = rows
            g.to_core(0).start()
            g.to_x(0).start()

    loop(0, z.experts, pack)
    fill_weights(wqkv_ref, wp)
    for i in tiles_of(z.seq):
        rows = slice(i * TILE, (i + 1) * TILE)
        stream = x_ref[rows, :].astype(F32)
        root = lax.rsqrt(jnp.mean(stream * stream, axis=1, keepdims=True) + epsilon)
        normed = (stream * root * gain_ref[...]).astype(BF16)
        na_ref[rows, :] = normed
        for k in range(3):
            cut = slice(k * SLOT, (k + 1) * SLOT)
            out = dot_nn(normed, wp[:, cut]).astype(BF16)
            if k == 0:
                out = (out.astype(F32) * size ** (-0.5)).astype(BF16)
            qkv[rows, cut] = out
    fill_bias(table_ref, bias, heads)

    def save_probs(i, h):
        _, width = window_of(i)
        part = (h, slice(i * TILE, (i + 1) * TILE), slice(0, width))
        return pltpu.make_async_copy(
            probs.at[part[0], pl.ds(i * TILE, TILE), pl.ds(0, width)],
            probs_out.at[part[0], pl.ds(i * TILE, TILE), pl.ds(0, width)],
            p_sem.at[i, h],
        )

    def mixed_core(i):
        rows = pl.ds(i * TILE, TILE)
        return remote(
            mixed_ref.at[rows, :], mixed_in.at[rows, :], m_sems.at[0, 0, i], m_sems.at[1, 0, i],
            (p.e, p.core_peer),
        )

    def mixed_piece(i, x):
        half = TILE // 2
        return mc.at[
            pl.ds(pl.multiple_of(i * TILE + p.c * half, 16), half),
            pl.ds(pl.multiple_of(x * z.half_width, LANES), z.half_width),
        ]

    def mixed_x(i):
        ref = mixed_piece(i, p.x)
        return remote(ref, ref, m_sems.at[0, 1, i], m_sems.at[1, 1, i], (p.e, p.x_peer))

    def mixed_on(i):
        ref = mixed_piece(i, 1 - p.x)
        return remote(ref, ref, m_sems.at[0, 2, i], m_sems.at[1, 2, i], (p.e, p.core_peer))

    def attend(i):
        rows = slice(i * TILE, (i + 1) * TILE)
        start, width = window_of(i)
        total = jnp.zeros((TILE, SLOT), F32)
        for h in range(heads):
            low = attention_tile(i, h, size, qkv, seg_col, seg_row, bias)
            probs[h, rows, 0:width] = low
            save_probs(i, h).start()
            values = mask_head(qkv[start : start + width, 2 * SLOT :], h, size)
            total = total + dot_nn(low, values)
        mixed_ref[rows, :] = total[:, 0:cols].astype(BF16)
        mixed_core(i).start()

    def share(i):
        mixed_core(i).wait_recv()
        rows = slice(i * TILE, (i + 1) * TILE)
        both = in_chip(mixed_ref[rows, :], mixed_in[rows, :])
        mc[rows, pl.ds(pl.multiple_of(p.x * z.half_width, LANES), z.half_width)] = both
        mixed_x(i).start()

    count = len(tiles_of(z.seq))
    for i in range(count):
        attend(i)
        if i >= 1:
            share(i - 1)
        if i >= 1:
            g.first(i)
        if i >= 2:
            g.second(i - 2)
    share(count - 1)

    def save(k):
        return (
            pltpu.make_async_copy(buf.at[k], og_out.at[k], out_sem.at[0, k]),
            pltpu.make_async_copy(hg.at[k], hg_out.at[k], out_sem.at[1, k]),
        )

    def body(k):
        @pl.when(k + count < z.experts)
        def _():
            g.first(k + count)

        @pl.when(k + count - 2 < z.experts)
        def _():
            g.second(k + count - 2)

        g.last(k)
        for j in range(0, w_out_ref.shape[0], COL_TILE):
            hg[k, :, j : j + COL_TILE] = dot_nt(buf[k], w_out_ref[j : j + COL_TILE, :]).astype(BF16)
        for copy in save(k):
            copy.start()

    loop(0, z.experts, body)
    for i in range(count):
        mixed_x(i).wait_recv()
        mixed_on(i).start()

    def finish(k):
        @pl.when(k > 0)
        def _():
            g.out(k).wait_send()

        g.to_core(k).wait_send()
        g.to_x(k).wait_send()
        g.on_to_core(k).wait_send()
        for copy in save(k):
            copy.wait()

    loop(0, z.experts, finish)
    cot_copy.wait_send()
    for i in range(count):
        mixed_on(i).wait_recv()
        for h in range(heads):
            save_probs(i, h).wait()
        mixed_core(i).wait_send()
        mixed_x(i).wait_send()
        mixed_on(i).wait_send()
    mc_out[...] = mc[...]


def run_front(z, inputs, gain_attn, weight_qkv, rel_table, segments, routes, cotangent, w_out):
    e = z.experts
    heads = rel_table.shape[1]
    cols = weight_qkv.shape[2]
    tiles = len(tiles_of(z.seq))
    smem = pl.BlockSpec(memory_space=pltpu.SMEM)
    return pl.pallas_call(
        functools.partial(front_kernel, z, heads),
        out_shape=(
            jax.ShapeDtypeStruct((z.seq, LANES), F32),
            jax.ShapeDtypeStruct((LANES, z.seq), F32),
            jax.ShapeDtypeStruct((z.seq, z.width), BF16),
            jax.ShapeDtypeStruct((z.seq, 3 * SLOT), BF16),
            jax.ShapeDtypeStruct((z.seq, cols), BF16),
            jax.ShapeDtypeStruct((z.seq, z.width), BF16),
            jax.ShapeDtypeStruct((e, z.slots, z.width), BF16),
            jax.ShapeDtypeStruct((e, z.slots, w_out.shape[0]), BF16),
            jax.ShapeDtypeStruct((heads, z.seq, WINDOW), BF16),
        ),
        in_specs=[smem] + [VMEM_SPEC] * 8,
        out_specs=(VMEM_SPEC,) * 6 + (ANY_SPEC,) * 3,
        scratch_shapes=gather_scratch(z)
        + [
            pltpu.VMEM((e, z.slots, w_out.shape[0]), BF16),
            pltpu.VMEM((z.width, 3 * SLOT), BF16),
            pltpu.VMEM((heads, TILE, WINDOW), F32),
            pltpu.VMEM((heads, z.seq, WINDOW), BF16),
            pltpu.VMEM((z.seq, cols), BF16),
            pltpu.VMEM((z.seq, z.half_width), BF16),
            pltpu.VMEM((z.seq, cols), BF16),
            pltpu.VMEM((z.seq, z.width), BF16),
            pltpu.SemaphoreType.DMA((2, e)),
            pltpu.SemaphoreType.DMA((tiles, heads)),
            pltpu.SemaphoreType.DMA((2,)),
            pltpu.SemaphoreType.DMA((2, 3, tiles)),
        ],
        compiler_params=pltpu.CompilerParams(
            collective_id=1, has_side_effects=True, vmem_limit_bytes=VMEM_LIMIT
        ),
        name="run_front",
    )(
        rel_table, inputs, gain_attn.reshape(1, -1), weight_qkv, segments.reshape(-1, 1),
        segments.reshape(1, -1), routes, cotangent, w_out,
    )


class Reduce:
    def __init__(self, z, p, blocks, in_pair, in_group, half_sum, result, pair_sems, group_sems):
        self.z, self.p = z, p
        self.blocks, self.in_pair, self.in_group = blocks, in_pair, in_group
        self.half_sum, self.result = half_sum, result
        self.pair_sems, self.group_sems = pair_sems, group_sems
        self.half_rows, self.group, self.row_parts, self.col_parts = reduce_cut(z, blocks.shape[1])
        self.owners = self.row_parts * self.col_parts
        self.piece_rows = self.half_rows // self.row_parts
        self.piece_cols = z.width // self.col_parts
        self.parity = lax.rem(p.e, 2)
        self.member = lax.div(p.e, 2)
        self.partner = p.e + 1 - 2 * self.parity

    def half(self, which):
        return pl.ds(pl.multiple_of(which * self.half_rows, 16), self.half_rows)

    def piece(self, owner, base):
        row = base + lax.div(owner, self.col_parts) * self.piece_rows
        col = lax.rem(owner, self.col_parts) * self.piece_cols
        return (
            pl.ds(pl.multiple_of(row, 16), self.piece_rows),
            pl.ds(pl.multiple_of(col, LANES), self.piece_cols),
        )

    def other(self, k):
        return lax.rem(self.member + k, self.group)

    def before(self, k):
        return lax.rem(self.member + self.group - k, self.group)

    def device(self, member):
        return (2 * member + self.parity, self.p.t)

    def pair_in(self, b):
        return remote(
            self.blocks.at[b, self.half(1 - self.parity), :],
            self.in_pair.at[b],
            self.pair_sems.at[0, 0, b],
            self.pair_sems.at[1, 0, b],
            (self.partner, self.p.t),
        )

    def spread(self, b, k):
        rows, cols = self.piece(self.other(k), 0)
        return remote(
            self.half_sum.at[b, rows, cols],
            self.in_group.at[b, k],
            self.group_sems.at[0, 0, b, k],
            self.group_sems.at[1, 0, b, k],
            self.device(self.other(k)),
        )

    def share(self, b, k):
        rows, cols = self.piece(self.member, self.parity * self.half_rows)
        ref = self.result.at[b, rows, cols]
        return remote(
            ref,
            ref,
            self.group_sems.at[0, 1, b, k],
            self.group_sems.at[1, 1, b, k],
            self.device(self.other(k)),
        )

    def pair_out(self, b):
        ref = self.result.at[b, self.half(self.parity), :]
        return remote(
            ref,
            ref,
            self.pair_sems.at[0, 1, b],
            self.pair_sems.at[1, 1, b],
            (self.partner, self.p.t),
        )

    def first(self, b):
        self.pair_in(b).start()

    def second(self, b):
        self.pair_in(b).wait_recv()
        mine = self.blocks[b, self.half(self.parity), :].astype(F32)
        self.half_sum[b] = (mine + self.in_pair[b].astype(F32)).astype(BF16)

        def send(k):
            @pl.when(self.other(k) < self.owners)
            def _():
                self.spread(b, k).start()

        loop(1, self.group, send)

    def third(self, b):
        @pl.when(self.member < self.owners)
        def _():
            rows, cols = self.piece(self.member, 0)
            total = self.half_sum[b, rows, cols].astype(F32)

            def add(k, total):
                self.spread(b, k).wait_recv()
                return total + self.in_group[b, k].astype(F32)

            total = lax.fori_loop(1, self.group, add, total)
            rows, cols = self.piece(self.member, self.parity * self.half_rows)
            self.result[b, rows, cols] = total.astype(BF16)
            loop(1, self.group, lambda k: self.share(b, k).start())

    def fourth(self, b):
        def wait(k):
            @pl.when(self.before(k) < self.owners)
            def _():
                self.share(b, k).wait_recv()

        loop(1, self.group, wait)
        self.pair_out(b).start()

    def last(self, b):
        self.pair_out(b).wait_recv()

    def finish(self, b):
        self.pair_in(b).wait_send()
        self.pair_out(b).wait_send()

        def wait(k):
            @pl.when(self.other(k) < self.owners)
            def _():
                self.spread(b, k).wait_send()

            @pl.when(self.member < self.owners)
            def _():
                self.share(b, k).wait_send()

        loop(1, self.group, wait)


def reduce_cut(z, rows):
    half_rows, group = rows // 2, z.experts // 2
    best = (1, 1)
    for row_parts in range(1, half_rows // 16 + 1):
        for col_parts in range(1, z.width // LANES + 1):
            if (half_rows // 16) % row_parts or (z.width // LANES) % col_parts:
                continue
            if best[0] * best[1] < row_parts * col_parts <= group:
                best = (row_parts, col_parts)
    return half_rows, group, best[0], best[1]


def reduce_scratch(z, blocks, rows):
    half_rows, group, row_parts, col_parts = reduce_cut(z, rows)
    piece = (half_rows // row_parts, z.width // col_parts)
    return [
        pltpu.VMEM((blocks, rows, z.width), BF16),
        pltpu.VMEM((blocks, half_rows, z.width), BF16),
        pltpu.VMEM((blocks, group) + piece, BF16),
        pltpu.VMEM((blocks, half_rows, z.width), BF16),
        pltpu.VMEM((blocks, rows, z.width), BF16),
        pltpu.SemaphoreType.DMA((2, 2, blocks)),
        pltpu.SemaphoreType.DMA((2, 2, blocks, group)),
    ]


def tail_sums(dbias):
    wide = dbias.shape[1]
    count = TILE
    while count > 8:
        half = count // 2
        dbias = dbias[0:half, :] + pltpu.roll(dbias[half:count, :], wide - half, 1)
        count = half
    total = dbias[0:1, :]
    for r in range(1, count):
        total = total + pltpu.roll(dbias[r : r + 1, :], wide - r, 1)
    return total


def split_dot(values, right):
    high = values.astype(BF16)
    rest = values - high.astype(F32)
    middle = rest.astype(BF16)
    low = (rest - middle.astype(F32)).astype(BF16)
    return dot_nn(high, right) + dot_nn(middle, right) + dot_nn(low, right)


def back_kernel(
    z, heads, mid_ref, nf_ref, gg_ref, gates_ref, nrm_ref, wr_ref, gain_ffn_ref, cot_ref, wao_ref,
    mixed_ref, qkv, probs, x_ref, gain_attn_ref, na_ref, wqkv_ref,
    grad_in_ref, blocks_out, early_out, late_out,
    wr_pad, dmix, dq, dk, dv, dbias, dqkv, wp, part, midg,
    blocks, in_pair, in_group, half_sum, result, pair_sems, group_sems,
    early, early_in, late, late_in, s_sems,
    n_core, n_sx, n_x, nag, n_sems,
):
    p = Place(z)
    experts = z.experts
    size = wao_ref.shape[0] // heads
    cols = wao_ref.shape[0]
    p.greet()
    red = Reduce(z, p, blocks, in_pair, in_group, half_sum, result, pair_sems, group_sems)
    wr_pad[...] = jnp.zeros_like(wr_pad)
    wr_pad[:, 0:experts] = wr_ref[...]
    router = jnp.zeros((LANES, z.width), F32)
    gain_sum = jnp.zeros((1, z.width), F32)
    for i in tiles_of(z.seq):
        rows = slice(i * TILE, (i + 1) * TILE)
        gate = gates_ref[rows, :]
        grads = gg_ref[rows, :]
        grads = grads + pltpu.roll(grads, LANES - experts, 1)
        dots = jnp.sum(gate * grads, axis=1, keepdims=True)
        logit = (gate * (grads - dots)).astype(BF16)
        router = router + dot_tn(logit, nrm_ref[rows, :])
        back = nf_ref[rows, :].astype(F32) + dot_nt(logit, wr_pad[...])
        mid = mid_ref[rows, :]
        root = lax.rsqrt(jnp.mean(mid * mid, axis=1, keepdims=True) + epsilon)
        unit = mid * root
        gain_sum = gain_sum + jnp.sum(back * unit, axis=0, keepdims=True)
        u = back * gain_ffn_ref[...]
        mean = jnp.mean(u * unit, axis=1, keepdims=True)
        grad = cot_ref[rows, :].astype(F32) + root * (u - unit * mean)
        midg[rows, :] = grad
        low = grad.astype(BF16)
        nag[rows, :] = low
        dmix[rows, :] = jnp.zeros((TILE, SLOT), BF16)
        dmix[rows, 0:cols] = dot_nt(low, wao_ref[...]).astype(BF16)
    for j in range(0, z.width, COL_TILE):
        cut = slice(j, j + COL_TILE)
        blocks[0, :, cut] = dot_tn(mixed_ref[...], nag[:, cut]).astype(BF16)
    red.first(0)
    tail_rows = early.shape[0] - experts
    first_row = lax.broadcasted_iota(jnp.int32, (tail_rows, z.width), 0) == 0
    early[...] = jnp.concatenate(
        [router[0:experts, :], jnp.where(first_row, gain_sum, 0.0)], axis=0
    ).astype(BF16)
    early_in[0] = early[...]

    def early_copy(k):
        return remote(
            early, early_in.at[k], s_sems.at[0, 0, k], s_sems.at[1, 0, k], (p.ahead(k), p.t)
        )

    loop(1, experts, lambda k: early_copy(k).start())
    dk[...] = jnp.zeros_like(dk)
    dv[...] = jnp.zeros_like(dv)
    dbias[...] = jnp.zeros_like(dbias)
    fill_weights(wqkv_ref, wp)

    def window(i):
        start, width = window_of(i)
        return slice(i * TILE, (i + 1) * TILE), slice(start, start + width), width

    for i in tiles_of(z.seq):
        rows, span, width = window(i)
        for h in range(heads):
            own = mask_head(dmix[rows, :], h, size)
            dv[span, :] += dot_tn(probs[h, rows, 0:width], own)
    red.second(0)
    dqkv[:, 2 * SLOT :] = dv[...].astype(BF16)

    def block(b, k):
        for j in range(0, z.width, COL_TILE):
            cut = slice(j, j + COL_TILE)
            full = dot_tn(dqkv[:, k * SLOT : (k + 1) * SLOT], na_ref[:, cut])
            blocks[b, :, cut] = full[0:cols, :].astype(BF16)

    block(1, 2)
    red.first(1)
    half = TILE // 2

    def tile_rows(i, c):
        return pl.ds(pl.multiple_of(i * TILE + c * half, 16), half)

    def nag_piece(i, x):
        return nag.at[
            tile_rows(i, p.c), pl.ds(pl.multiple_of(x * z.half_width, LANES), z.half_width)
        ]

    def n_to_core(i):
        return remote(
            part.at[tile_rows(i, 1 - p.c), :], n_core.at[i], n_sems.at[0, 0, i], n_sems.at[1, 0, i],
            (p.e, p.core_peer),
        )

    def n_to_x(i):
        return remote(
            n_sx.at[i], n_x.at[i], n_sems.at[0, 1, i], n_sems.at[1, 1, i], (p.e, p.x_peer)
        )

    def n_share(i, which):
        ref = nag_piece(i, p.x if which < 4 else 1 - p.x)
        peer = p.x_peer if which == 2 else p.core_peer
        return remote(ref, ref, n_sems.at[0, which, i], n_sems.at[1, which, i], (p.e, peer))

    def n_second(i):
        n_to_core(i).wait_recv()
        for x in (1 - p.x, p.x):
            cut = pl.ds(pl.multiple_of(x * z.half_width, LANES), z.half_width)
            both = part[tile_rows(i, p.c), cut].astype(F32) + n_core[i, :, cut].astype(F32)
            if x is p.x:
                nag_piece(i, p.x)[...] = both.astype(BF16)
            else:
                n_sx[i] = both.astype(BF16)
                n_to_x(i).start()

    def n_third(i):
        n_to_x(i).wait_recv()
        mine = nag_piece(i, p.x)
        mine[...] = (mine[...].astype(F32) + n_x[i].astype(F32)).astype(BF16)
        n_share(i, 2).start()
        n_share(i, 3).start()

    def n_fourth(i):
        n_share(i, 2).wait_recv()
        n_share(i, 4).start()

    count = len(tiles_of(z.seq))
    order = list(reversed(tiles_of(z.seq)))
    for step, i in enumerate(order):
        rows, span, width = window(i)
        total = jnp.zeros((TILE, SLOT), F32)
        for h in range(heads):
            own = mask_head(dmix[rows, :], h, size)
            weight = probs[h, rows, 0:width].astype(F32)
            back = dot_nt(own, qkv[span, 2 * SLOT :])
            dots = jnp.sum(weight * back, axis=1, keepdims=True)
            score = weight * (back - dots)
            low = score.astype(BF16)
            dbias[h, :, WINDOW - width : WINDOW] += low.astype(F32)
            total = total + dot_nn(low, mask_head(qkv[span, SLOT : 2 * SLOT], h, size))
            dk[span, :] += dot_tn(low, mask_head(qkv[rows, 0:SLOT], h, size))
        dqkv[rows, 0:SLOT] = (total * size ** (-0.5)).astype(BF16)
        dqkv[rows, SLOT : 2 * SLOT] = dk[rows, :].astype(BF16)
        for j in range(0, z.width, COL_TILE):
            part[rows, j : j + COL_TILE] = dot_nt(
                dqkv[rows, :], wp[j : j + COL_TILE, :]
            ).astype(BF16)
        n_to_core(i).start()
        if step == 0:
            red.third(0)
            red.second(1)
        if step >= 1:
            n_second(order[step - 1])
        if step == 1:
            red.fourth(0)
            red.third(1)
        if step >= 2:
            n_third(order[step - 2])
        if step == 2:
            red.fourth(1)
        if step >= 3:
            n_fourth(order[step - 3])
    block(2, 0)
    red.first(2)
    block(3, 1)
    red.first(3)
    n_second(order[count - 1])
    n_third(order[count - 2])
    n_fourth(order[count - 3])
    late[...] = jnp.zeros_like(late)
    lane = lax.broadcasted_iota(jnp.int32, (4 * TILE, LANES), 0)
    distance = distance_of(lane)
    which = lax.broadcasted_iota(jnp.int32, (4 * TILE, LANES), 1)
    hot = jnp.where((bucket_grid(distance) == which) & (distance >= 0), 1.0, 0.0).astype(BF16)
    red.second(2)
    red.second(3)
    sums = [tail_sums(dbias[h]) for h in range(heads)]
    sums = jnp.concatenate(sums + [jnp.zeros((8 - heads, 4 * TILE), F32)], axis=0)
    late[0:8, 0:LANES] = split_dot(sums, hot)
    n_third(order[count - 1])
    n_fourth(order[count - 2])
    red.third(2)
    red.third(3)
    n_fourth(order[count - 1])
    for i in order:
        n_share(i, 3).wait_recv()
        n_share(i, 4).wait_recv()
    gain_sum = jnp.zeros((1, z.width), F32)
    for i in tiles_of(z.seq):
        rows = slice(i * TILE, (i + 1) * TILE)
        stream = x_ref[rows, :].astype(F32)
        root = lax.rsqrt(jnp.mean(stream * stream, axis=1, keepdims=True) + epsilon)
        unit = stream * root
        back = nag[rows, :].astype(F32)
        gain_sum = gain_sum + jnp.sum(back * unit, axis=0, keepdims=True)
        w = back * gain_attn_ref[...]
        mean = jnp.mean(w * unit, axis=1, keepdims=True)
        grad_in_ref[rows, :] = midg[rows, :] + root * (w - unit * mean)
    for k in range(z.width // SLOT):
        late[8 + k : 9 + k, :] = gain_sum[:, k * SLOT : (k + 1) * SLOT]

    def late_copy(k):
        return remote(
            late, late_in.at[k], s_sems.at[0, 1, k], s_sems.at[1, 1, k], (p.ahead(k), p.t)
        )

    late_in[0] = late[...]
    loop(1, experts, lambda k: late_copy(k).start())
    red.fourth(2)
    red.fourth(3)

    def take_early(source, total):
        k = p.behind(source)

        @pl.when(k > 0)
        def _():
            early_copy(k).wait_recv()

        return total + early_in[k].astype(F32)

    early_out[...] = lax.fori_loop(0, experts, take_early, jnp.zeros(early_out.shape, F32))

    def take_late(source, total):
        k = p.behind(source)

        @pl.when(k > 0)
        def _():
            late_copy(k).wait_recv()

        return total + late_in[k]

    for b in range(4):
        red.last(b)
        blocks_out[b] = result[b]
    late_out[...] = lax.fori_loop(0, experts, take_late, jnp.zeros(late_out.shape, F32))
    for b in range(4):
        red.finish(b)

    def finish(k):
        early_copy(k).wait_send()
        late_copy(k).wait_send()

    loop(1, experts, finish)
    for i in order:
        n_to_core(i).wait_send()
        n_to_x(i).wait_send()
        for which in (2, 3, 4):
            n_share(i, which).wait_send()


def run_back(
    z, mid, nf, gg, gates, nrm, weight_router, gain_ffn, cot_full, wao, mixed, qkv, probs, inputs,
    gain_attn, na, weight_qkv,
):
    heads, cols = probs.shape[0], wao.shape[0]
    e, seq, width = z.experts, z.seq, z.width
    early_rows = round_up(e + 1, 16)
    tiles = seq // TILE
    half = TILE // 2
    return pl.pallas_call(
        functools.partial(back_kernel, z, heads),
        out_shape=(
            jax.ShapeDtypeStruct((seq, width), F32),
            jax.ShapeDtypeStruct((4, cols, width), BF16),
            jax.ShapeDtypeStruct((early_rows, width), F32),
            jax.ShapeDtypeStruct((16, SLOT), F32),
        ),
        in_specs=[VMEM_SPEC] * 16,
        out_specs=(VMEM_SPEC,) * 4,
        scratch_shapes=[
            pltpu.VMEM((width, LANES), BF16),
            pltpu.VMEM((seq, SLOT), BF16),
            pltpu.VMEM((8, LANES), F32),
            pltpu.VMEM((seq, SLOT), F32),
            pltpu.VMEM((seq, SLOT), F32),
            pltpu.VMEM((heads, TILE, 4 * TILE), F32),
            pltpu.VMEM((seq, 3 * SLOT), BF16),
            pltpu.VMEM((width, 3 * SLOT), BF16),
            pltpu.VMEM((seq, width), BF16),
            pltpu.VMEM((seq, width), F32),
        ]
        + reduce_scratch(z, 4, cols)
        + [
            pltpu.VMEM((early_rows, width), BF16),
            pltpu.VMEM((e, early_rows, width), BF16),
            pltpu.VMEM((16, SLOT), F32),
            pltpu.VMEM((e, 16, SLOT), F32),
            pltpu.SemaphoreType.DMA((2, 2, e)),
            pltpu.VMEM((tiles, half, width), BF16),
            pltpu.VMEM((tiles, half, z.half_width), BF16),
            pltpu.VMEM((tiles, half, z.half_width), BF16),
            pltpu.VMEM((seq, width), BF16),
            pltpu.SemaphoreType.DMA((2, 5, tiles)),
        ],
        compiler_params=pltpu.CompilerParams(
            collective_id=4, has_side_effects=True, vmem_limit_bytes=VMEM_LIMIT
        ),
        name="run_back",
    )(
        mid, nf, gg, gates, nrm, weight_router, gain_ffn.reshape(1, -1), cot_full, wao, mixed, qkv,
        probs, inputs, gain_attn.reshape(1, -1), na, weight_qkv,
    )


def per_device(
    inputs,
    gain_attn,
    gain_ffn,
    weight_qkv,
    weight_attn_out,
    rel_table,
    weight_router,
    weight_in,
    weight_out,
    routes,
    segments,
    cotangent,
):
    seq_len, width = inputs.shape
    heads = rel_table.shape[1]
    col_width = weight_qkv.shape[2]
    experts = weight_router.shape[1]
    z = Sizes(experts, seq_len, routes.shape[1], width)
    cot_full = lax.all_gather(cotangent, "tensor", axis=1, tiled=True)
    wao_full = lax.all_gather(weight_attn_out, "tensor", axis=0, tiled=True)
    rk_col, rk_row, na, qkv, mixed, mixed_all, og_rows, hg, probs = run_front(
        z, inputs, gain_attn, weight_qkv, rel_table, segments, routes, cotangent, weight_out[0]
    )
    mid, nrm, gates, nf, gg, gate_slots, slot_rows, hidden, pre_grads = run_experts(
        z, inputs, mixed_all, wao_full, gain_ffn, weight_router, rk_col, rk_row, weight_in[0], hg
    )
    activations = return_results(z, hidden, weight_out[0], rk_col, gates, mid)
    flat = (experts * z.slots, -1)
    grad_weight_in = jnp.einsum(
        "sd,sf->df",
        slot_rows.reshape(flat),
        pre_grads.reshape(flat),
        preferred_element_type=F32,
    )[None]
    slot_grads = (gate_slots[:, 0, : z.slots, None] * og_rows.astype(F32)).astype(BF16)
    grad_weight_out = jnp.einsum(
        "sf,sd->fd",
        hidden.reshape(flat),
        slot_grads.reshape(flat),
        preferred_element_type=F32,
    )[None]
    grad_input, blocks, early, late = run_back(
        z, mid, nf, gg, gates, nrm, weight_router, gain_ffn, cot_full, weight_attn_out, mixed, qkv,
        probs, inputs, gain_attn, na, weight_qkv,
    )
    blocks = blocks.astype(F32)
    grad_weight_qkv = jnp.stack([blocks[2].T, blocks[3].T, blocks[1].T], axis=0)
    return (
        activations,
        grad_input,
        late[8 : 8 + width // SLOT, :].reshape(width),
        early[experts],
        grad_weight_qkv,
        blocks[0],
        late[0:heads, 0:BUCKETS].T,
        early[0:experts].T,
        grad_weight_in,
        grad_weight_out,
    )


def solution(mesh):
    in_specs = (
        P("expert", None),
        P(),
        P(),
        P(None, None, "tensor"),
        P("tensor", None),
        P(None, "tensor"),
        P(),
        P("expert", None, "tensor"),
        P("expert", "tensor", None),
        P("expert", None),
        P("expert"),
        P("expert", "tensor"),
    )
    out_specs = (
        P("expert", "tensor"),
        P("expert", None),
        P(),
        P(),
        P(None, None, "tensor"),
        P("tensor", None),
        P(None, "tensor"),
        P(),
        P("expert", None, "tensor"),
        P("expert", "tensor", None),
    )
    return jax.shard_map(
        per_device, mesh=mesh, in_specs=in_specs, out_specs=out_specs, check_vma=False
    )
```

```python
import functools
import math

import jax
import jax.numpy as jnp
from jax import lax
from jax.experimental import pallas as pl
from jax.experimental.pallas import tpu as pltpu
from jax.sharding import PartitionSpec as P

BUCKETS = 32
epsilon = 1e-06
negative = -1e30
F32 = jnp.float32
BF16 = jnp.bfloat16
MESH = pl.DeviceIdType.MESH
VMEM_SPEC = pl.BlockSpec(memory_space=pltpu.VMEM)
ANY_SPEC = pl.BlockSpec(memory_space=pl.ANY)
LANES = 128
ROW_TILE = 256
COL_TILE = 256
VMEM_LIMIT = 60 * 2**20


def dot_nn(left, right):
    return lax.dot_general(left, right, (((1,), (0,)), ((), ())), preferred_element_type=F32)


def dot_nt(left, right):
    return lax.dot_general(left, right, (((1,), (1,)), ((), ())), preferred_element_type=F32)


def dot_tn(left, right):
    return lax.dot_general(left, right, (((0,), (0,)), ((), ())), preferred_element_type=F32)


def round_up(value, step):
    return (value + step - 1) // step * step


class Sizes:
    def __init__(self, experts, seq_len, top_count, width):
        self.experts = experts
        self.seq = seq_len
        self.width = width
        self.half_width = width // 2
        capacity = (4 * seq_len * top_count + 24 * experts - 1) // (24 * experts) * 8
        self.slots = round_up(capacity, 32)
        self.half = self.slots // 2
        self.slot_lanes = round_up(self.slots, LANES)


class Place:
    def __init__(self, sizes):
        self.count = sizes.experts
        self.e = lax.axis_index("expert")
        self.t = lax.axis_index("tensor")
        self.c = lax.rem(self.t, 2)
        self.x = lax.div(self.t, 2)
        self.core_peer = self.t + 1 - 2 * self.c
        self.x_peer = lax.rem(self.t + 2, 4)

    def shifted(self, k, sign):
        group = self.count // 2
        parity = lax.rem(self.e, 2)
        flip = lax.rem(k, 2)
        turn = lax.div(k, 2)
        member = lax.rem(lax.div(self.e, 2) + group + sign * turn, group)
        return 2 * member + parity + flip - 2 * parity * flip

    def ahead(self, k):
        return self.shifted(k, 1)

    def behind(self, k):
        return self.shifted(k, -1)

    def steps_from(self, other):
        group = self.count // 2
        turn = lax.rem(lax.div(self.e, 2) + group - lax.div(other, 2), group)
        return 2 * turn + lax.rem(self.e + other, 2)

    def greet(self, expert_peers=True, all_tensor=True):
        barrier = pltpu.get_barrier_semaphore()
        count = 0
        if expert_peers:

            def one(k, carry):
                pl.semaphore_signal(
                    barrier, inc=1, device_id=(self.ahead(k), self.t), device_id_type=MESH
                )
                return carry

            lax.fori_loop(1, self.count, one, 0)
            count += self.count - 1
        for d in range(1, 4):
            pl.semaphore_signal(
                barrier,
                inc=1,
                device_id=(self.e, lax.rem(self.t + d, 4)),
                device_id_type=MESH,
            )
        count += 3
        pl.semaphore_wait(barrier, count)


def remote(src, dst, send_sem, recv_sem, device):
    return pltpu.make_async_remote_copy(
        src_ref=src,
        dst_ref=dst,
        send_sem=send_sem,
        recv_sem=recv_sem,
        device_id=device,
        device_id_type=MESH,
    )


class Gather:
    sem_kinds = 4

    def __init__(self, sizes, place, stage, buf, send, recv):
        self.z, self.p = sizes, place
        self.stage, self.buf, self.send, self.recv = stage, buf, send, recv

    def quarter(self, k, c, x):
        h, w = self.z.half, self.z.half_width
        return self.buf.at[
            k, pl.ds(pl.multiple_of(c * h, 16), h), pl.ds(pl.multiple_of(x * w, LANES), w)
        ]

    def out(self, k):
        p = self.p
        return remote(
            self.stage.at[k],
            self.quarter(k, p.c, p.x),
            self.send.at[0, k],
            self.recv.at[0, k],
            (p.ahead(k), p.t),
        )

    def to_core(self, k):
        p = self.p
        ref = self.quarter(k, p.c, p.x)
        return remote(ref, ref, self.send.at[1, k], self.recv.at[1, k], (p.e, p.core_peer))

    def to_x(self, k):
        p = self.p
        ref = self.quarter(k, p.c, p.x)
        return remote(ref, ref, self.send.at[2, k], self.recv.at[2, k], (p.e, p.x_peer))

    def on_to_core(self, k):
        p = self.p
        ref = self.quarter(k, p.c, 1 - p.x)
        return remote(ref, ref, self.send.at[3, k], self.recv.at[3, k], (p.e, p.core_peer))

    def pack_own(self, rk_row, rows_ref):
        z, p = self.z, self.p
        pick = slot_onehot(rk_row[pl.ds(p.e, 1), :], z.slots, 0)
        for j in range(0, z.width, COL_TILE):
            self.buf[0, :, j : j + COL_TILE] = dot_nn(
                pick, rows_ref[:, j : j + COL_TILE]
            ).astype(BF16)

    def pack(self, k, pick, rows_ref):
        z, p = self.z, self.p
        cols = rows_ref[:, pl.ds(pl.multiple_of(p.x * z.half_width, LANES), z.half_width)]
        self.stage[k] = dot_nn(pick, cols).astype(BF16)

    def first(self, k):
        self.out(k).wait_recv()
        self.to_core(k).start()
        self.to_x(k).start()

    def second(self, k):
        self.to_x(k).wait_recv()
        self.on_to_core(k).start()

    def last(self, k):
        self.to_core(k).wait_recv()
        self.on_to_core(k).wait_recv()

    def finish(self, k):
        self.out(k).wait_send()
        self.to_core(k).wait_send()
        self.to_x(k).wait_send()
        self.on_to_core(k).wait_send()


class Return:
    sem_kinds = 3

    def __init__(self, sizes, place, part, from_core, stage_x, from_x, ret, send, recv):
        self.z, self.p = sizes, place
        self.part, self.from_core, self.stage_x = part, from_core, stage_x
        self.from_x, self.ret = from_x, ret
        self.send, self.recv = send, recv

    def part_rows(self, k, c):
        start = k * self.z.slots + c * self.z.half
        return pl.ds(pl.multiple_of(start, 16), self.z.half)

    def cols(self, x):
        return pl.ds(pl.multiple_of(x * self.z.half_width, LANES), self.z.half_width)

    def to_core(self, k):
        p = self.p
        return remote(
            self.part.at[self.part_rows(k, 1 - p.c), :],
            self.from_core.at[k],
            self.send.at[0, k],
            self.recv.at[0, k],
            (p.e, p.core_peer),
        )

    def to_x(self, k):
        p = self.p
        return remote(
            self.stage_x.at[k],
            self.from_x.at[k],
            self.send.at[1, k],
            self.recv.at[1, k],
            (p.e, p.x_peer),
        )

    def home(self, k):
        p = self.p
        return remote(
            self.from_core.at[k, :, self.cols(p.x)],
            self.ret.at[k],
            self.send.at[2, k],
            self.recv.at[2, k],
            (p.behind(k), p.t),
        )

    def first(self, k):
        self.to_core(k).start()

    def second(self, k):
        p = self.p
        self.to_core(k).wait_recv()
        rows = self.part_rows(k, p.c)
        for x in (1 - p.x, p.x):
            cols = self.cols(x)
            both = self.part[rows, cols].astype(F32) + self.from_core[k, :, cols].astype(F32)
            if x is p.x:
                self.from_core[k, :, cols] = both.astype(BF16)
            else:
                self.stage_x[k] = both.astype(BF16)
                self.to_x(k).start()

    def third(self, k):
        self.to_x(k).wait_recv()
        cols = self.cols(self.p.x)
        total = self.from_core[k, :, cols].astype(F32) + self.from_x[k].astype(F32)

        @pl.when(k == 0)
        def _():
            self.ret[0] = total.astype(BF16)

        @pl.when(k > 0)
        def _():
            self.from_core[k, :, cols] = total.astype(BF16)
            self.home(k).start()

    def arrive(self, k):
        @pl.when(k > 0)
        def _():
            self.home(k).wait_recv()

    def finish(self, k):
        self.to_core(k).wait_send()
        self.to_x(k).wait_send()

        @pl.when(k > 0)
        def _():
            self.home(k).wait_send()


def return_scratch(z):
    e, h, w = z.experts, z.half, z.half_width
    return [
        pltpu.VMEM((e * z.slots, z.width), BF16),
        pltpu.VMEM((e, h, z.width), BF16),
        pltpu.VMEM((e, h, w), BF16),
        pltpu.VMEM((e, h, w), BF16),
        pltpu.VMEM((e, h, w), BF16),
        pltpu.SemaphoreType.DMA((Return.sem_kinds, e)),
        pltpu.SemaphoreType.DMA((Return.sem_kinds, e)),
    ]


def gather_scratch(z):
    e, h, w = z.experts, z.half, z.half_width
    return [
        pltpu.VMEM((e, h, w), BF16),
        pltpu.VMEM((e, z.slots, z.width), BF16),
        pltpu.SemaphoreType.DMA((Gather.sem_kinds, e)),
        pltpu.SemaphoreType.DMA((Gather.sem_kinds, e)),
    ]


def slot_rows(z, k):
    return pl.ds(pl.multiple_of(k * z.slots, 16), z.slots)


def slot_onehot(rank_row, count, offset):
    slot = lax.broadcasted_iota(jnp.int32, (count, rank_row.shape[1]), 0).astype(F32)
    shift = lax.convert_element_type(offset, F32)
    return jnp.where(rank_row - shift == slot, 1.0, 0.0).astype(BF16)


def pick_lane(values, lane):
    lanes = lax.broadcasted_iota(jnp.int32, values.shape, 1)
    return jnp.sum(jnp.where(lanes == lane, values, 0.0), axis=1, keepdims=True)


def row_to_col(row, count, offset):
    rows = lax.broadcasted_iota(jnp.int32, (count, row.shape[1]), 0) + offset
    lanes = lax.broadcasted_iota(jnp.int32, (count, row.shape[1]), 1)
    return jnp.sum(jnp.where(rows == lanes, row, 0.0), axis=1, keepdims=True)


def col_to_row(col, lane_count):
    rows = lax.broadcasted_iota(jnp.int32, (col.shape[0], lane_count), 0)
    lanes = lax.broadcasted_iota(jnp.int32, (col.shape[0], lane_count), 1)
    return jnp.sum(jnp.where(rows == lanes, col, 0.0), axis=0, keepdims=True)


def loop(start, stop, body):
    def step(i, carry):
        body(i)
        return carry

    lax.fori_loop(start, stop, step, 0)


def fill_ranks(routes_ref, rk_col, rk_row):
    seq = routes_ref.shape[1]
    ids = lax.broadcasted_iota(jnp.int32, (LANES, seq), 0)
    hot = (routes_ref[0:1, :] == ids) | (routes_ref[1:2, :] == ids)
    hot_mark = jnp.where(hot, 1.0, 0.0)
    hot_low = hot_mark.astype(BF16)
    for s in range(0, seq, ROW_TILE):
        rows = lax.broadcasted_iota(jnp.int32, (seq, ROW_TILE), 0)
        cols = lax.broadcasted_iota(jnp.int32, (seq, ROW_TILE), 1) + s
        before = jnp.where(rows < cols, 1.0, 0.0).astype(BF16)
        rank = dot_nn(hot_low, before)
        rank = jnp.where(hot_mark[:, s : s + ROW_TILE] > 0.5, rank, -1.0)
        rk_row[:, s : s + ROW_TILE] = rank
        rk_col[s : s + ROW_TILE, :] = rank.T


def gelu_pair(h):
    scale = 0.7978845608028654
    square = h * h
    t = jnp.tanh(scale * h * (1.0 + 0.044715 * square))
    half = 0.5 + 0.5 * t
    slope = half + (0.5 * scale) * h * (1.0 - t * t) * (1.0 + 0.134145 * square)
    return h * half, slope


def results_kernel(
    z, hid_ref, w_out_ref, rk_row, gate_row, mid_ref, out_ref,
    part, from_core, stage_x, from_x, ret, r_send, r_recv,
    acc, d_send, d_recv, d_sems,
):
    p = Place(z)
    p.greet()
    b = Return(z, p, part, from_core, stage_x, from_x, ret, r_send, r_recv)

    def body(i):
        @pl.when(i < z.experts)
        def _():
            for j in range(0, z.width, COL_TILE):
                part[slot_rows(z, i), j : j + COL_TILE] = dot_nn(
                    hid_ref[i], w_out_ref[:, j : j + COL_TILE]
                ).astype(BF16)
            b.first(i)

        @pl.when((i >= 1) & (i <= z.experts))
        def _():
            b.second(i - 1)

        @pl.when(i >= 2)
        def _():
            b.third(i - 2)

    loop(0, z.experts + 2, body)
    acc[...] = jnp.zeros_like(acc)

    def combine(k):
        b.arrive(k)
        who = p.ahead(k)
        pick = slot_onehot(rk_row[pl.ds(who, 1), :], z.half, p.c * z.half)
        gate = gate_row[pl.ds(who, 1), :]
        for s in range(0, z.half_width, LANES):
            rows = slice(s, s + LANES)
            acc[rows, :] += gate * dot_tn(ret[k, :, rows], pick)

    loop(0, z.experts, combine)
    own = z.half_width // 2

    def part_of(c):
        return pl.ds(pl.multiple_of(c * own, 16), own)

    d_send[...] = acc[part_of(1 - p.c), :].astype(BF16)
    copy = remote(d_send, d_recv, d_sems.at[0], d_sems.at[1], (p.e, p.core_peer))
    copy.start()
    for s in range(0, z.seq, ROW_TILE):
        rows = slice(s, s + ROW_TILE)
        mid = mid_ref[rows, pl.ds(pl.multiple_of(p.x * z.half_width, LANES), z.half_width)].T
        acc[part_of(p.c), rows] += jnp.where(p.c == 0, mid[0:own, :], mid[own:, :])
    copy.wait_recv()
    out_ref[...] = (acc[part_of(p.c), :] + d_recv[...].astype(F32)).astype(BF16)
    copy.wait_send()
    loop(0, z.experts, b.finish)


def return_results(z, hid, w_out, rk_row, gate_row, mid):
    own = z.half_width // 2
    return pl.pallas_call(
        functools.partial(results_kernel, z),
        out_shape=jax.ShapeDtypeStruct((own, z.seq), BF16),
        in_specs=[VMEM_SPEC] * 5,
        out_specs=VMEM_SPEC,
        scratch_shapes=return_scratch(z)
        + [
            pltpu.VMEM((z.half_width, z.seq), F32),
            pltpu.VMEM((own, z.seq), BF16),
            pltpu.VMEM((own, z.seq), BF16),
            pltpu.SemaphoreType.DMA((2,)),
        ],
        compiler_params=pltpu.CompilerParams(
            collective_id=3, has_side_effects=True, vmem_limit_bytes=VMEM_LIMIT
        ),
        name="return_results",
    )(hid, w_out, rk_row, gate_row, mid)


def far_limits(buckets):
    half_size = buckets // 2
    base_ratio = 256.0 / buckets
    return [
        int(math.ceil(half_size * base_ratio ** (step / half_size))) for step in range(1, half_size)
    ]


TILE = 256
WINDOW = 3 * TILE
SLOT = 256


def distance_of(lane):
    return jnp.where(lane < WINDOW, 2 * TILE - lane, 2 * TILE + 4 * TILE - lane)


def bucket_grid(distance):
    half_size = BUCKETS // 2
    far = jnp.full(distance.shape, half_size, jnp.int32)
    for limit in far_limits(BUCKETS):
        far = far + jnp.where(distance >= limit, 1, 0)
    return jnp.where(distance < half_size, distance, far)


def fill_bias(table_ref, bias, heads):
    lane = lax.broadcasted_iota(jnp.int32, (1, 4 * TILE), 1)
    distance = distance_of(lane)
    bucket = bucket_grid(distance)
    for h in range(heads):
        values = jnp.full((1, 4 * TILE), negative, F32)
        for b in range(BUCKETS):
            values = jnp.where(bucket == b, table_ref[h, b], values)
        wide = jnp.broadcast_to(values, (TILE, 4 * TILE))
        rolled = pltpu.roll(wide, 0, 1, stride=1, stride_axis=0)
        bias[h] = rolled[:, 0:WINDOW]


def head_lanes(rows, h, size):
    lanes = lax.broadcasted_iota(jnp.int32, (rows, SLOT), 1)
    return (lanes >= h * size) & (lanes < (h + 1) * size)


def mask_head(values, h, size):
    keep = head_lanes(values.shape[0], h, size)
    return jnp.where(keep, values, jnp.zeros_like(values))


def tiles_of(seq):
    return range(seq // TILE)


def window_of(i):
    start = max(0, i - 2) * TILE
    return start, (i + 1) * TILE - start


def attention_tile(i, h, size, qkv, seg_col, seg_row, bias):
    start, width = window_of(i)
    query = mask_head(qkv[i * TILE : (i + 1) * TILE, 0:SLOT], h, size)
    keys = qkv[start : start + width, SLOT : 2 * SLOT]
    scores = dot_nt(query, keys) + bias[h, :, WINDOW - width :]
    same = seg_col[i * TILE : (i + 1) * TILE, 0:1] == seg_row[:, start : start + width].astype(F32)
    scores = jnp.where(same, scores, negative)
    power = jnp.exp(scores - jnp.max(scores, axis=1, keepdims=True))
    probs = power * (1.0 / jnp.sum(power, axis=1, keepdims=True))
    return probs.astype(BF16)


def layer_kernel(z, heads, names, *refs):
    r = Names(names, refs)
    p = Place(z)
    experts = z.experts
    cols = r.cot.shape[0]
    size = cols // heads
    tiles = list(tiles_of(z.seq))
    count = len(tiles)
    p.greet()
    saves = []
    save_ids = iter(range(16))

    def save(src, dst):
        copy = pltpu.make_async_copy(src, dst, r.save_sem.at[next(save_ids)])
        copy.start()
        saves.append(copy)

    cot_rows = lambda t: r.cot_all.at[pl.ds(pl.multiple_of(t * cols, 16), cols), :]
    wao_rows = lambda t: r.wao_all.at[pl.ds(pl.multiple_of(t * cols, 16), cols), :]

    def spread(rows, n):
        def copy(t, m, peer):
            return remote(
                rows(t), rows(t), r.c_sems.at[0, n, m], r.c_sems.at[1, n, m], (p.e, peer)
            )

        return (
            copy(p.t, 0, p.core_peer), copy(p.t, 1, p.x_peer), copy(p.x_peer, 2, p.core_peer)
        )

    cot_rows(p.t)[...] = r.cot[...]
    cot_copies = spread(cot_rows, 0)
    cot_copies[0].start()
    wao_rows(p.t)[...] = r.wao[...]
    wao_copies = spread(wao_rows, 1)
    wao_copies[1].start()
    wao_copies[0].start()
    cot_copies[1].start()
    fill_ranks(r.routes, r.rk_col, r.rk_row)
    save(r.rk_row, r.rk_out)
    og = Gather(z, p, r.stage, r.og_buf, r.og_send, r.og_recv)
    g = Gather(z, p, r.stage, r.buf, r.g_send, r.g_recv)
    b = Return(
        z, p, r.part, r.from_core, r.stage_x, r.from_x, r.ret, r.r_send, r.r_recv
    )

    def in_chip(own, peer):
        return jnp.where(
            p.c == 0,
            jnp.concatenate([own, peer], axis=1),
            jnp.concatenate([peer, own], axis=1),
        )

    cot_copies[0].wait_recv()

    def half_pick(k):
        return slot_onehot(r.rk_row[pl.ds(p.ahead(k), 1), :], z.half, p.c * z.half)

    def pack_og(k):
        own = r.cot_all[pl.ds(pl.multiple_of(p.x * z.half_width, 16), z.half_width), :]
        rows = dot_nt(half_pick(k), own).astype(BF16)

        @pl.when(k > 0)
        def _():
            r.stage[k] = rows
            og.out(k).start()

        @pl.when(k == 0)
        def _():
            og.quarter(0, p.c, p.x)[...] = rows
            og.to_core(0).start()
            og.to_x(0).start()

    loop(1, experts, pack_og)
    pack_og(0)
    wide_row = jnp.broadcast_to(r.seg_row[...].astype(F32), (LANES, z.seq))
    r.qkv[...] = jnp.zeros_like(r.qkv)
    for i in tiles:
        rows = slice(i * TILE, (i + 1) * TILE)
        r.seg_col[rows, :] = wide_row[:, rows].T
        stream = r.x[rows, :].astype(F32)
        root = lax.rsqrt(jnp.mean(stream * stream, axis=1, keepdims=True) + epsilon)
        normed = (stream * root * r.gains[0:1, :]).astype(BF16)
        r.na[rows, :] = normed
        for k in range(3):
            cut = slice(k * SLOT, k * SLOT + cols)
            out = dot_nt(normed, r.wqkv[k]).astype(BF16)
            if k == 0:
                out = (out.astype(F32) * size ** (-0.5)).astype(BF16)
            r.qkv[rows, cut] = out
    na_saved = len(saves)
    save(r.na, r.na_out)
    save(r.qkv, r.qkv_out)
    fill_bias(r.table, r.bias, heads)

    def probs_rows(i, h):
        return pl.ds((i % 2 * heads + h) * TILE, TILE)

    def save_probs(i, h):
        _, width = window_of(i)
        return pltpu.make_async_copy(
            r.part.at[probs_rows(i, h), pl.ds(0, width)],
            r.probs_out.at[h, pl.ds(i * TILE, TILE), pl.ds(0, width)],
            r.p_sem.at[i, h],
        )

    def mixed_core(i):
        rows = pl.ds(i * TILE, TILE)
        return remote(
            r.mixed.at[rows, :], r.mixed_in.at[rows, :], r.m_sems.at[0, 0, i],
            r.m_sems.at[1, 0, i], (p.e, p.core_peer),
        )

    def mixed_piece(i, x):
        half = TILE // 2
        return r.mc.at[
            pl.ds(pl.multiple_of(i * TILE + p.c * half, 16), half),
            pl.ds(pl.multiple_of(x * z.half_width, LANES), z.half_width),
        ]

    def mixed_x(i):
        ref = mixed_piece(i, p.x)
        return remote(ref, ref, r.m_sems.at[0, 1, i], r.m_sems.at[1, 1, i], (p.e, p.x_peer))

    def mixed_on(i):
        ref = mixed_piece(i, 1 - p.x)
        return remote(ref, ref, r.m_sems.at[0, 2, i], r.m_sems.at[1, 2, i], (p.e, p.core_peer))

    def attend(i):
        rows = slice(i * TILE, (i + 1) * TILE)
        start, width = window_of(i)
        total = jnp.zeros((TILE, SLOT), F32)
        for h in range(heads):
            if i >= 2:
                save_probs(i - 2, h).wait()
            low = attention_tile(i, h, size, r.qkv, r.seg_col, r.seg_row, r.bias)
            r.part[probs_rows(i, h), 0:width] = low
            save_probs(i, h).start()
            values = mask_head(r.qkv[start : start + width, 2 * SLOT :], h, size)
            total = total + dot_nn(low, values)
        r.mixed[rows, :] = total[:, 0:cols].astype(BF16)
        mixed_core(i).start()

    def share(i):
        mixed_core(i).wait_recv()
        rows = slice(i * TILE, (i + 1) * TILE)
        both = in_chip(r.mixed[rows, :], r.mixed_in[rows, :])
        r.mc[rows, pl.ds(pl.multiple_of(p.x * z.half_width, LANES), z.half_width)] = both
        mixed_x(i).start()

    for i in tiles:
        attend(i)
        if i >= 1:
            share(i - 1)
        if i >= 2:
            mixed_x(i - 2).wait_recv()
            mixed_on(i - 2).start()
        if i == 0:
            wao_copies[1].wait_recv()
            wao_copies[2].start()
        if i == 2:
            cot_copies[1].wait_recv()
            cot_copies[2].start()
    share(count - 1)
    save(r.mixed, r.mixed_out)
    saves.pop(na_saved).wait()
    r.wr_pad[...] = jnp.zeros_like(r.wr_pad)
    r.wr_pad[0:experts, :] = r.wr[...].astype(F32)
    router = r.wr_pad[...].astype(BF16)
    for copy in (wao_copies[0], wao_copies[2], cot_copies[2]):
        copy.wait_recv()

    def project(i):
        rows = slice(i * TILE, (i + 1) * TILE)
        mid = r.x[rows, :].astype(F32) + dot_nn(r.mc[rows, :], r.wao_all[...])
        r.mid[rows, :] = mid
        root = lax.rsqrt(jnp.mean(mid * mid, axis=1, keepdims=True) + epsilon)
        nrm = (mid * root * r.gains[1:2, :]).astype(BF16)
        r.na[rows, :] = nrm
        logits = dot_nt(nrm, router)
        hot = r.rk_col[rows, :] > -0.5
        logits = jnp.where(hot, logits, negative)
        peak = jnp.max(logits, axis=1, keepdims=True)
        power = jnp.where(hot, jnp.exp(logits - peak), 0.0)
        gates = power / jnp.sum(power, axis=1, keepdims=True)
        r.gates[rows, :] = gates
        r.gate_row[:, rows] = gates.T

    for i in tiles:
        if i + 2 >= count:
            mixed_x(i).wait_recv()
            mixed_on(i).start()
        if i == 2:
            og.second(0)
        mixed_on(i).wait_recv()
        project(i)
    for k in range(1, EARLY):
        og.first(k)
    mid_saved = len(saves)
    save(r.mid, r.mid_out)
    save(r.na, r.nrm_out)
    save(r.gates, r.gates_out)
    save(r.gate_row, r.gate_row_out)
    save(r.cot_all, r.cot_out)

    def gate_copy(k):
        return remote(
            r.gs_out.at[k], r.gs_in.at[k], r.gs_sems.at[0, k], r.gs_sems.at[1, k],
            (p.ahead(k), p.t),
        )

    def slot_gates(k):
        pick = slot_onehot(r.rk_row[pl.ds(p.ahead(k), 1), :], z.slot_lanes, 0)
        row = r.gate_row[pl.ds(p.ahead(k), 1), :]
        high = row.astype(BF16).astype(F32)
        low = row - high
        which = lax.broadcasted_iota(jnp.int32, (16, z.seq), 0)
        both = jnp.where(which == 0, high, jnp.where(which == 1, low, 0.0)).astype(BF16)
        sums = dot_nt(both, pick)
        return sums[0:1, :] + sums[1:2, :]

    for i in tiles[-2:]:
        for h in range(heads):
            save_probs(i, h).wait()

    def pack(k):
        og.out(k).wait_send()
        g.pack(k, half_pick(k), r.na)
        g.out(k).start()

    loop(1, experts, pack)

    def send_gates(k):
        r.gs_out[k] = slot_gates(k)
        gate_copy(k).start()

    loop(1, experts, send_gates)
    r.gs_in[0] = slot_gates(0)
    g.pack_own(r.rk_row, r.na)

    def gg_copy(k, d):
        return remote(
            r.gg_send.at[k],
            r.gg_recv.at[k, p.t],
            r.gg_sems.at[0, k, d],
            r.gg_sems.at[1, k, d],
            (p.behind(k), lax.rem(p.t + d, 4)),
        )

    def save_hid(k):
        return pltpu.make_async_copy(r.hid.at[lax.rem(k, 2)], r.hid_out.at[k], r.hid_sem.at[k])

    def expert(k):
        ring = lax.rem(k, 2)

        @pl.when(k > 0)
        def _():
            gate_copy(k).wait_recv()
            g.last(k)

        @pl.when(k > 1)
        def _():
            save_hid(k - 2).wait()

        og.last(k)
        gate = row_to_col(r.gs_in[k], z.slots, 0)
        sums = jnp.zeros((z.slots, 1), F32)
        for j in range(0, r.w_in.shape[1], COL_TILE):
            cut = slice(j, j + COL_TILE)
            up, slope = gelu_pair(dot_nn(r.buf[k], r.w_in[:, cut]))
            back = dot_nt(r.og_buf[k], r.w_out[cut, :])
            r.hid[ring, :, cut] = up.astype(BF16)
            r.pre[ring, :, cut] = (gate * back * slope).astype(BF16)
            sums = sums + jnp.sum(up * back, axis=1, keepdims=True)
        for j in range(0, z.width, COL_TILE):
            r.part[slot_rows(z, k), j : j + COL_TILE] = dot_nt(
                r.pre[ring], r.w_in[j : j + COL_TILE, :]
            ).astype(BF16)
        b.first(k)
        r.gg_send[k] = col_to_row(sums, z.slot_lanes)
        for d in range(1, 4):
            gg_copy(k, d).start()

        @pl.when(k > 0)
        def _():
            gg_copy(k, 0).start()

        @pl.when(k == 0)
        def _():
            r.gg_recv[0, p.t] = r.gg_send[0]

        save_hid(k).start()

    def weight_grads(k):
        ring = lax.rem(k, 2)
        gate = row_to_col(r.gs_in[k], z.slots, 0)
        r.gated[...] = (gate * r.og_buf[k].astype(F32)).astype(BF16)
        for j in range(0, z.width, COL_TILE):
            cut = slice(j, j + COL_TILE)
            r.gw_in[cut, :] += dot_tn(r.buf[k, :, cut], r.pre[ring])
            r.gw_out[cut, :] += dot_tn(r.hid[ring, :, cut], r.gated[...])

    r.gw_in[...] = jnp.zeros_like(r.gw_in)
    r.gw_out[...] = jnp.zeros_like(r.gw_out)

    def body(i):
        @pl.when(i + EARLY < experts)
        def _():
            og.first(i + EARLY)

        @pl.when(i + 1 < experts)
        def _():
            og.second(i + 1)

        @pl.when(i < experts)
        def _():
            expert(i)

        @pl.when(i == 0)
        def _():
            g.first(1)

        @pl.when(i + 2 < experts)
        def _():
            g.first(i + 2)

        @pl.when(i + 1 < experts)
        def _():
            g.second(i + 1)

        @pl.when((i >= 1) & (i <= experts))
        def _():
            b.second(i - 1)

        @pl.when(i >= 2)
        def _():
            b.third(i - 2)

        @pl.when((i >= 1) & (i <= experts))
        def _():
            weight_grads(i - 1)

    loop(0, experts + 2, body)
    save(r.gw_in, r.gw_in_out)
    save(r.gw_out, r.gw_out_out)
    saves.pop(mid_saved).wait()
    acc = r.mid.at[:, pl.ds(0, z.half_width + LANES)]
    acc[...] = jnp.zeros(acc.shape, F32)

    def combine(k):
        b.arrive(k)
        for d in range(1, 4):
            gg_copy(k, d).wait_recv()

        @pl.when(k > 0)
        def _():
            gg_copy(k, 0).wait_recv()

        row = r.gg_recv[k, 0] + r.gg_recv[k, 1] + r.gg_recv[k, 2] + r.gg_recv[k, 3]
        col = row_to_col(row, z.half, p.c * z.half)
        high = col.astype(BF16).astype(F32)
        lanes = lax.broadcasted_iota(jnp.int32, (z.half, LANES), 1)
        who = p.ahead(k)
        r.retx[:, 0 : z.half_width] = r.ret[k]
        r.retx[:, z.half_width :] = jnp.where(
            lanes == who, high, jnp.where(lanes == who + experts, col - high, 0.0)
        ).astype(BF16)
        for s in range(0, z.seq, ROW_TILE):
            rows = slice(s, s + ROW_TILE)
            rank = pick_lane(r.rk_col[rows, :], who) - lax.convert_element_type(p.c * z.half, F32)
            slot = lax.broadcasted_iota(jnp.int32, (ROW_TILE, z.half), 1).astype(F32)
            pick = jnp.where(rank == slot, 1.0, 0.0).astype(BF16)
            acc[rows, :] += dot_nn(pick, r.retx[...])

    loop(0, experts, combine)
    half_seq = z.seq // 2

    def tokens(c):
        return pl.ds(pl.multiple_of(c * half_seq, 16), half_seq)

    def d_copy(src, dst, n, peer):
        return remote(src, dst, r.d_sems.at[0, n], r.d_sems.at[1, n], (p.e, peer))

    r.d_send[...] = acc[tokens(1 - p.c), 0 : z.half_width].astype(BF16)
    r.gd_send[...] = acc[:, z.half_width :].astype(BF16)
    copy_d = d_copy(r.d_send, r.d_recv, 0, p.core_peer)
    copy_g = d_copy(r.gd_send, r.gd_recv, 1, p.core_peer)
    copy_d.start()
    copy_g.start()
    copy_d.wait_recv()

    def piece(x):
        return r.nf.at[tokens(p.c), pl.ds(pl.multiple_of(x * z.half_width, LANES), z.half_width)]

    piece(p.x)[...] = (
        acc[tokens(p.c), 0 : z.half_width] + r.d_recv[...].astype(F32)
    ).astype(BF16)
    to_x = d_copy(piece(p.x), piece(p.x), 2, p.x_peer)
    to_core = d_copy(piece(p.x), piece(p.x), 3, p.core_peer)
    on_to_core = d_copy(piece(1 - p.x), piece(1 - p.x), 4, p.core_peer)
    to_x.start()
    to_core.start()
    copy_g.wait_recv()
    r.gg[...] = acc[:, z.half_width :] + r.gd_recv[...].astype(F32)

    def finish(k):
        b.finish(k)
        for d in range(1, 4):
            gg_copy(k, d).wait_send()

        @pl.when(k > 0)
        def _():
            g.finish(k)
            gate_copy(k).wait_send()
            gg_copy(k, 0).wait_send()

        og.to_core(k).wait_send()
        og.to_x(k).wait_send()
        og.on_to_core(k).wait_send()

        @pl.when(k >= experts - 2)
        def _():
            save_hid(k).wait()

    loop(0, experts, finish)
    for copy in cot_copies + wao_copies:
        copy.wait_send()
    for i in tiles:
        mixed_core(i).wait_send()
        mixed_x(i).wait_send()
        mixed_on(i).wait_send()
    to_x.wait_recv()
    on_to_core.start()
    to_core.wait_recv()
    on_to_core.wait_recv()
    for copy in (copy_d, copy_g, to_x, to_core, on_to_core):
        copy.wait_send()
    for copy in saves:
        copy.wait()


class Names:
    def __init__(self, names, refs):
        for name, ref in zip(names, refs, strict=True):
            setattr(self, name, ref)


EARLY = 4


def run_layer(
    z, inputs, gains, weight_qkv, weight_attn_out, rel_table, weight_router, w_in, w_out,
    routes, segments, cotangent,
):
    e, seq, width = z.experts, z.seq, z.width
    heads, cols = rel_table.shape[0], weight_qkv.shape[1]
    hidden_count = w_in.shape[1]
    tiles = seq // TILE
    half_seq = seq // 2
    smem = pl.BlockSpec(memory_space=pltpu.SMEM)
    dma = pltpu.SemaphoreType.DMA
    args = {
        "table": rel_table,
        "x": inputs,
        "gains": gains,
        "wqkv": weight_qkv,
        "wao": weight_attn_out,
        "wr": weight_router,
        "w_in": w_in,
        "w_out": w_out,
        "routes": routes,
        "seg_row": segments.reshape(1, -1),
        "cot": cotangent,
    }
    outs = {
        "rk_out": ((LANES, seq), F32),
        "gate_row_out": ((LANES, seq), F32),
        "cot_out": ((width, seq), BF16),
        "na_out": ((seq, width), BF16),
        "qkv_out": ((seq, 3 * SLOT), BF16),
        "mixed_out": ((seq, cols), BF16),
        "probs_out": ((heads, seq, WINDOW), BF16),
        "mid_out": ((seq, width), F32),
        "nrm_out": ((seq, width), BF16),
        "gates_out": ((seq, LANES), F32),
        "hid_out": ((e, z.slots, hidden_count), BF16),
        "gw_in_out": ((width, hidden_count), F32),
        "gw_out_out": ((hidden_count, width), F32),
        "nf": ((seq, width), BF16),
        "gg": ((seq, LANES), F32),
    }
    in_vmem = ("nf", "gg")
    gather_names = (("stage", "og_buf", "og_send", "og_recv"), ("stage", "buf", "g_send", "g_recv"))
    scratch = {}
    for group in gather_names:
        scratch.update(zip(group, gather_scratch(z)))
    scratch.update(
        zip(
            ("part", "from_core", "stage_x", "from_x", "ret", "r_send", "r_recv"),
            return_scratch(z),
            strict=True,
        )
    )
    shapes = {
        "rk_col": ((seq, LANES), F32),
        "rk_row": ((LANES, seq), F32),
        "na": ((seq, width), BF16),
        "qkv": ((seq, 3 * SLOT), BF16),
        "mixed": ((seq, cols), BF16),
        "mid": ((seq, width), F32),
        "gates": ((seq, LANES), F32),
        "gw_in": ((width, hidden_count), F32),
        "gw_out": ((hidden_count, width), F32),
        "bias": ((heads, TILE, WINDOW), F32),
        "cot_all": ((width, seq), BF16),
        "wao_all": ((width, width), BF16),
        "wr_pad": ((LANES, width), F32),
        "seg_col": ((seq, LANES), F32),
        "mixed_in": ((seq, cols), BF16),
        "mc": ((seq, width), BF16),
        "hid": ((2, z.slots, hidden_count), BF16),
        "pre": ((2, z.slots, hidden_count), BF16),
        "gated": ((z.slots, width), BF16),
        "gate_row": ((LANES, seq), F32),
        "gs_out": ((e, 1, z.slot_lanes), F32),
        "gs_in": ((e, 1, z.slot_lanes), F32),
        "gg_send": ((e, 1, z.slot_lanes), F32),
        "gg_recv": ((e, 4, 1, z.slot_lanes), F32),
        "retx": ((z.half, z.half_width + LANES), BF16),
        "d_send": ((half_seq, z.half_width), BF16),
        "d_recv": ((half_seq, z.half_width), BF16),
        "gd_send": ((seq, LANES), BF16),
        "gd_recv": ((seq, LANES), BF16),
    }
    for name, (shape, dtype) in shapes.items():
        scratch[name] = pltpu.VMEM(shape, dtype)
    scratch.update(
        {
            "save_sem": dma((16,)),
            "hid_sem": dma((e,)),
            "p_sem": dma((tiles, heads)),
            "c_sems": dma((2, 2, 3)),
            "m_sems": dma((2, 3, tiles)),
            "gs_sems": dma((2, e)),
            "gg_sems": dma((2, e, 4)),
            "d_sems": dma((2, 5)),
        }
    )
    names = list(args) + list(outs) + list(scratch)
    results = pl.pallas_call(
        functools.partial(layer_kernel, z, heads, names),
        out_shape=tuple(jax.ShapeDtypeStruct(*outs[n]) for n in outs),
        in_specs=[smem] + [VMEM_SPEC] * (len(args) - 1),
        out_specs=tuple(VMEM_SPEC if n in in_vmem else ANY_SPEC for n in outs),
        scratch_shapes=list(scratch.values()),
        compiler_params=pltpu.CompilerParams(
            collective_id=1, has_side_effects=True, vmem_limit_bytes=VMEM_LIMIT
        ),
        name="run_layer",
    )(*args.values())
    return dict(zip(outs, results, strict=True))


class Reduce:
    def __init__(self, z, p, blocks, in_pair, in_group, half_sum, result, pair_sems, group_sems):
        self.z, self.p = z, p
        self.blocks, self.in_pair, self.in_group = blocks, in_pair, in_group
        self.half_sum, self.result = half_sum, result
        self.pair_sems, self.group_sems = pair_sems, group_sems
        self.half_rows, self.group, self.row_parts, self.col_parts = reduce_cut(z, blocks.shape[1])
        self.owners = self.row_parts * self.col_parts
        self.piece_rows = self.half_rows // self.row_parts
        self.piece_cols = z.width // self.col_parts
        self.parity = lax.rem(p.e, 2)
        self.member = lax.div(p.e, 2)
        self.partner = p.e + 1 - 2 * self.parity

    def half(self, which):
        return pl.ds(pl.multiple_of(which * self.half_rows, 16), self.half_rows)

    def piece(self, owner, base):
        row = base + lax.div(owner, self.col_parts) * self.piece_rows
        col = lax.rem(owner, self.col_parts) * self.piece_cols
        return (
            pl.ds(pl.multiple_of(row, 16), self.piece_rows),
            pl.ds(pl.multiple_of(col, LANES), self.piece_cols),
        )

    def other(self, k):
        return lax.rem(self.member + k, self.group)

    def before(self, k):
        return lax.rem(self.member + self.group - k, self.group)

    def device(self, member):
        return (2 * member + self.parity, self.p.t)

    def pair_in(self, b):
        return remote(
            self.blocks.at[b, self.half(1 - self.parity), :],
            self.in_pair.at[b],
            self.pair_sems.at[0, 0, b],
            self.pair_sems.at[1, 0, b],
            (self.partner, self.p.t),
        )

    def spread(self, b, k):
        rows, cols = self.piece(self.other(k), 0)
        return remote(
            self.half_sum.at[b, rows, cols],
            self.in_group.at[b, k],
            self.group_sems.at[0, 0, b, k],
            self.group_sems.at[1, 0, b, k],
            self.device(self.other(k)),
        )

    def share(self, b, k):
        rows, cols = self.piece(self.member, self.parity * self.half_rows)
        ref = self.result.at[b, rows, cols]
        return remote(
            ref,
            ref,
            self.group_sems.at[0, 1, b, k],
            self.group_sems.at[1, 1, b, k],
            self.device(self.other(k)),
        )

    def pair_out(self, b):
        ref = self.result.at[b, self.half(self.parity), :]
        return remote(
            ref,
            ref,
            self.pair_sems.at[0, 1, b],
            self.pair_sems.at[1, 1, b],
            (self.partner, self.p.t),
        )

    def first(self, b):
        self.pair_in(b).start()

    def second(self, b):
        self.pair_in(b).wait_recv()
        mine = self.blocks[b, self.half(self.parity), :].astype(F32)
        self.half_sum[b] = (mine + self.in_pair[b].astype(F32)).astype(BF16)

        def send(k):
            @pl.when(self.other(k) < self.owners)
            def _():
                self.spread(b, k).start()

        loop(1, self.group, send)

    def third(self, b):
        @pl.when(self.member < self.owners)
        def _():
            rows, cols = self.piece(self.member, 0)
            total = self.half_sum[b, rows, cols].astype(F32)

            def add(k, total):
                self.spread(b, k).wait_recv()
                return total + self.in_group[b, k].astype(F32)

            total = lax.fori_loop(1, self.group, add, total)
            rows, cols = self.piece(self.member, self.parity * self.half_rows)
            self.result[b, rows, cols] = total.astype(BF16)
            loop(1, self.group, lambda k: self.share(b, k).start())

    def fourth(self, b):
        def wait(k):
            @pl.when(self.before(k) < self.owners)
            def _():
                self.share(b, k).wait_recv()

        loop(1, self.group, wait)
        self.pair_out(b).start()

    def last(self, b):
        self.pair_out(b).wait_recv()

    def finish(self, b):
        self.pair_in(b).wait_send()
        self.pair_out(b).wait_send()

        def wait(k):
            @pl.when(self.other(k) < self.owners)
            def _():
                self.spread(b, k).wait_send()

            @pl.when(self.member < self.owners)
            def _():
                self.share(b, k).wait_send()

        loop(1, self.group, wait)


def reduce_cut(z, rows):
    half_rows, group = rows // 2, z.experts // 2
    best = (1, 1)
    for row_parts in range(1, half_rows // 16 + 1):
        for col_parts in range(1, z.width // LANES + 1):
            if (half_rows // 16) % row_parts or (z.width // LANES) % col_parts:
                continue
            if best[0] * best[1] < row_parts * col_parts <= group:
                best = (row_parts, col_parts)
    return half_rows, group, best[0], best[1]


def reduce_scratch(z, blocks, rows):
    half_rows, group, row_parts, col_parts = reduce_cut(z, rows)
    piece = (half_rows // row_parts, z.width // col_parts)
    return [
        pltpu.VMEM((blocks, rows, z.width), BF16),
        pltpu.VMEM((blocks, half_rows, z.width), BF16),
        pltpu.VMEM((blocks, group) + piece, BF16),
        pltpu.VMEM((blocks, half_rows, z.width), BF16),
        pltpu.VMEM((blocks, rows, z.width), BF16),
        pltpu.SemaphoreType.DMA((2, 2, blocks)),
        pltpu.SemaphoreType.DMA((2, 2, blocks, group)),
    ]


def tail_sums(dbias):
    wide = dbias.shape[1]
    count = TILE
    while count > 8:
        half = count // 2
        dbias = dbias[0:half, :] + pltpu.roll(dbias[half:count, :], wide - half, 1)
        count = half
    total = dbias[0:1, :]
    for r in range(1, count):
        total = total + pltpu.roll(dbias[r : r + 1, :], wide - r, 1)
    return total


def split_dot(values, right):
    high = values.astype(BF16)
    rest = values - high.astype(F32)
    middle = rest.astype(BF16)
    low = (rest - middle.astype(F32)).astype(BF16)
    return dot_nn(high, right) + dot_nn(middle, right) + dot_nn(low, right)


def back_kernel(
    z, heads, mid_ref, nf_ref, gg_ref, gates_ref, nrm_ref, wr_ref, gains_ref, cot_ref, wao_ref,
    mixed_ref, qkv, probs, x_ref, na_ref, wqkv_ref,
    grad_in_ref, blocks_out, early_out, late_out,
    wr_pad, dmix, dk, dv, dbias, dqkv, part, midg,
    blocks, in_pair, in_group, half_sum, result, pair_sems, group_sems,
    early, early_in, late, late_in, s_sems,
    n_core, n_sx, n_x, nag, n_sems,
):
    p = Place(z)
    experts = z.experts
    size = wao_ref.shape[0] // heads
    cols = wao_ref.shape[0]
    p.greet()
    red = Reduce(z, p, blocks, in_pair, in_group, half_sum, result, pair_sems, group_sems)
    wr_pad[...] = jnp.zeros_like(wr_pad)
    wr_pad[0:experts, :] = wr_ref[...].astype(F32)
    router_low = wr_pad[...].astype(BF16)
    router = jnp.zeros((LANES, z.width), F32)
    gain_sum = jnp.zeros((1, z.width), F32)
    for i in tiles_of(z.seq):
        rows = slice(i * TILE, (i + 1) * TILE)
        gate = gates_ref[rows, :]
        grads = gg_ref[rows, :]
        grads = grads + pltpu.roll(grads, LANES - experts, 1)
        dots = jnp.sum(gate * grads, axis=1, keepdims=True)
        logit = (gate * (grads - dots)).astype(BF16)
        router = router + dot_tn(logit, nrm_ref[rows, :])
        back = nf_ref[rows, :].astype(F32) + dot_nn(logit, router_low)
        mid = mid_ref[rows, :]
        root = lax.rsqrt(jnp.mean(mid * mid, axis=1, keepdims=True) + epsilon)
        unit = mid * root
        gain_sum = gain_sum + jnp.sum(back * unit, axis=0, keepdims=True)
        u = back * gains_ref[1:2, :]
        mean = jnp.mean(u * unit, axis=1, keepdims=True)
        grad = cot_ref[:, rows].astype(F32).T + root * (u - unit * mean)
        midg[rows, :] = grad
        low = grad.astype(BF16)
        nag[rows, :] = low
        dmix[rows, :] = jnp.zeros((TILE, SLOT), BF16)
        dmix[rows, 0:cols] = dot_nt(low, wao_ref[...]).astype(BF16)
    for j in range(0, z.width, COL_TILE):
        cut = slice(j, j + COL_TILE)
        blocks[3, :, cut] = dot_tn(mixed_ref[...], nag[:, cut]).astype(BF16)
    red.first(3)
    tail_rows = early.shape[0] - experts
    first_row = lax.broadcasted_iota(jnp.int32, (tail_rows, z.width), 0) == 0
    early[...] = jnp.concatenate(
        [router[0:experts, :], jnp.where(first_row, gain_sum, 0.0)], axis=0
    ).astype(BF16)
    early_in[0] = early[...]

    def early_copy(k):
        return remote(
            early, early_in.at[k], s_sems.at[0, 0, k], s_sems.at[1, 0, k], (p.ahead(k), p.t)
        )

    loop(1, experts, lambda k: early_copy(k).start())
    dk[...] = jnp.zeros_like(dk)
    dv[...] = jnp.zeros_like(dv)
    dbias[...] = jnp.zeros_like(dbias)

    def window(i):
        start, width = window_of(i)
        return slice(i * TILE, (i + 1) * TILE), slice(start, start + width), width

    for i in tiles_of(z.seq):
        rows, span, width = window(i)
        for h in range(heads):
            own = mask_head(dmix[rows, :], h, size)
            dv[span, :] += dot_tn(probs[h, rows, 0:width], own)
    red.second(3)
    dqkv[:, 2 * SLOT :] = dv[...].astype(BF16)

    def block(b, k):
        for j in range(0, z.width, COL_TILE):
            cut = slice(j, j + COL_TILE)
            full = dot_tn(dqkv[:, k * SLOT : (k + 1) * SLOT], na_ref[:, cut])
            blocks[b, :, cut] = full[0:cols, :].astype(BF16)

    block(2, 2)
    red.first(2)
    half = TILE // 2

    def tile_rows(i, c):
        return pl.ds(pl.multiple_of(i * TILE + c * half, 16), half)

    def nag_piece(i, x):
        return nag.at[
            tile_rows(i, p.c), pl.ds(pl.multiple_of(x * z.half_width, LANES), z.half_width)
        ]

    def n_to_core(i):
        return remote(
            part.at[tile_rows(i, 1 - p.c), :], n_core.at[i], n_sems.at[0, 0, i], n_sems.at[1, 0, i],
            (p.e, p.core_peer),
        )

    def n_to_x(i):
        return remote(
            n_sx.at[i], n_x.at[i], n_sems.at[0, 1, i], n_sems.at[1, 1, i], (p.e, p.x_peer)
        )

    def n_share(i, which):
        ref = nag_piece(i, p.x if which < 4 else 1 - p.x)
        peer = p.x_peer if which == 2 else p.core_peer
        return remote(ref, ref, n_sems.at[0, which, i], n_sems.at[1, which, i], (p.e, peer))

    def n_second(i):
        n_to_core(i).wait_recv()
        for x in (1 - p.x, p.x):
            cut = pl.ds(pl.multiple_of(x * z.half_width, LANES), z.half_width)
            both = part[tile_rows(i, p.c), cut].astype(F32) + n_core[i, :, cut].astype(F32)
            if x is p.x:
                nag_piece(i, p.x)[...] = both.astype(BF16)
            else:
                n_sx[i] = both.astype(BF16)
                n_to_x(i).start()

    def n_third(i):
        n_to_x(i).wait_recv()
        mine = nag_piece(i, p.x)
        mine[...] = (mine[...].astype(F32) + n_x[i].astype(F32)).astype(BF16)
        n_share(i, 2).start()
        n_share(i, 3).start()

    def n_fourth(i):
        n_share(i, 2).wait_recv()
        n_share(i, 4).start()

    count = len(tiles_of(z.seq))
    order = list(reversed(tiles_of(z.seq)))
    for step, i in enumerate(order):
        rows, span, width = window(i)
        total = jnp.zeros((TILE, SLOT), F32)
        for h in range(heads):
            own = mask_head(dmix[rows, :], h, size)
            weight = probs[h, rows, 0:width].astype(F32)
            back = dot_nt(own, qkv[span, 2 * SLOT :])
            dots = jnp.sum(weight * back, axis=1, keepdims=True)
            score = weight * (back - dots)
            low = score.astype(BF16)
            dbias[h, :, WINDOW - width : WINDOW] += low.astype(F32)
            total = total + dot_nn(low, mask_head(qkv[span, SLOT : 2 * SLOT], h, size))
            dk[span, :] += dot_tn(low, mask_head(qkv[rows, 0:SLOT], h, size))
        dqkv[rows, 0:SLOT] = (total * size ** (-0.5)).astype(BF16)
        dqkv[rows, SLOT : 2 * SLOT] = dk[rows, :].astype(BF16)
        for j in range(0, z.width, COL_TILE):
            part[rows, j : j + COL_TILE] = sum(
                dot_nn(
                    dqkv[rows, k * SLOT : k * SLOT + cols], wqkv_ref[k, :, j : j + COL_TILE]
                )
                for k in range(3)
            ).astype(BF16)
        n_to_core(i).start()
        if step == 0:
            red.third(3)
            red.second(2)
        if step >= 1:
            n_second(order[step - 1])
        if step == 1:
            red.fourth(3)
            red.third(2)
        if step >= 2:
            n_third(order[step - 2])
        if step == 2:
            red.fourth(2)
        if step >= 3:
            n_fourth(order[step - 3])
    block(0, 0)
    red.first(0)
    block(1, 1)
    red.first(1)
    n_second(order[count - 1])
    n_third(order[count - 2])
    n_fourth(order[count - 3])
    late[...] = jnp.zeros_like(late)
    lane = lax.broadcasted_iota(jnp.int32, (4 * TILE, LANES), 0)
    distance = distance_of(lane)
    which = lax.broadcasted_iota(jnp.int32, (4 * TILE, LANES), 1)
    hot = jnp.where((bucket_grid(distance) == which) & (distance >= 0), 1.0, 0.0).astype(BF16)
    red.second(0)
    red.second(1)
    sums = [tail_sums(dbias[h]) for h in range(heads)]
    sums = jnp.concatenate(sums + [jnp.zeros((8 - heads, 4 * TILE), F32)], axis=0)
    late[0:8, 0:LANES] = split_dot(sums, hot)
    n_third(order[count - 1])
    n_fourth(order[count - 2])
    red.third(0)
    red.third(1)
    n_fourth(order[count - 1])
    for i in order:
        n_share(i, 3).wait_recv()
        n_share(i, 4).wait_recv()
    gain_sum = jnp.zeros((1, z.width), F32)
    for i in tiles_of(z.seq):
        rows = slice(i * TILE, (i + 1) * TILE)
        stream = x_ref[rows, :].astype(F32)
        root = lax.rsqrt(jnp.mean(stream * stream, axis=1, keepdims=True) + epsilon)
        unit = stream * root
        back = nag[rows, :].astype(F32)
        gain_sum = gain_sum + jnp.sum(back * unit, axis=0, keepdims=True)
        w = back * gains_ref[0:1, :]
        mean = jnp.mean(w * unit, axis=1, keepdims=True)
        grad_in_ref[rows, :] = midg[rows, :] + root * (w - unit * mean)
    for k in range(z.width // SLOT):
        late[8 + k : 9 + k, :] = gain_sum[:, k * SLOT : (k + 1) * SLOT]

    def late_copy(k):
        return remote(
            late, late_in.at[k], s_sems.at[0, 1, k], s_sems.at[1, 1, k], (p.ahead(k), p.t)
        )

    late_in[0] = late[...]
    loop(1, experts, lambda k: late_copy(k).start())
    red.fourth(0)
    red.fourth(1)

    def take_early(source, total):
        k = p.steps_from(source)

        @pl.when(k > 0)
        def _():
            early_copy(k).wait_recv()

        return total + early_in[k].astype(F32)

    early_out[...] = lax.fori_loop(0, experts, take_early, jnp.zeros(early_out.shape, F32))

    def take_late(source, total):
        k = p.steps_from(source)

        @pl.when(k > 0)
        def _():
            late_copy(k).wait_recv()

        return total + late_in[k]

    for b in range(4):
        red.last(b)
        blocks_out[b] = result[b]
    late_out[...] = lax.fori_loop(0, experts, take_late, jnp.zeros(late_out.shape, F32))
    for b in range(4):
        red.finish(b)

    def finish(k):
        early_copy(k).wait_send()
        late_copy(k).wait_send()

    loop(1, experts, finish)
    for i in order:
        n_to_core(i).wait_send()
        n_to_x(i).wait_send()
        for which in (2, 3, 4):
            n_share(i, which).wait_send()


def run_back(
    z, mid, nf, gg, gates, nrm, weight_router, gains, cot_full, wao, mixed, qkv, probs, inputs,
    na, weight_qkv,
):
    heads, cols = probs.shape[0], wao.shape[0]
    e, seq, width = z.experts, z.seq, z.width
    early_rows = round_up(e + 1, 16)
    tiles = seq // TILE
    half = TILE // 2
    return pl.pallas_call(
        functools.partial(back_kernel, z, heads),
        out_shape=(
            jax.ShapeDtypeStruct((seq, width), F32),
            jax.ShapeDtypeStruct((4, cols, width), BF16),
            jax.ShapeDtypeStruct((early_rows, width), F32),
            jax.ShapeDtypeStruct((16, SLOT), F32),
        ),
        in_specs=[VMEM_SPEC] * 15,
        out_specs=(VMEM_SPEC,) * 4,
        scratch_shapes=[
            pltpu.VMEM((LANES, width), F32),
            pltpu.VMEM((seq, SLOT), BF16),
            pltpu.VMEM((seq, SLOT), F32),
            pltpu.VMEM((seq, SLOT), F32),
            pltpu.VMEM((heads, TILE, 4 * TILE), F32),
            pltpu.VMEM((seq, 3 * SLOT), BF16),
            pltpu.VMEM((seq, width), BF16),
            pltpu.VMEM((seq, width), F32),
        ]
        + reduce_scratch(z, 4, cols)
        + [
            pltpu.VMEM((early_rows, width), BF16),
            pltpu.VMEM((e, early_rows, width), BF16),
            pltpu.VMEM((16, SLOT), F32),
            pltpu.VMEM((e, 16, SLOT), F32),
            pltpu.SemaphoreType.DMA((2, 2, e)),
            pltpu.VMEM((tiles, half, width), BF16),
            pltpu.VMEM((tiles, half, z.half_width), BF16),
            pltpu.VMEM((tiles, half, z.half_width), BF16),
            pltpu.VMEM((seq, width), BF16),
            pltpu.SemaphoreType.DMA((2, 5, tiles)),
        ],
        compiler_params=pltpu.CompilerParams(
            collective_id=4, has_side_effects=True, vmem_limit_bytes=VMEM_LIMIT
        ),
        name="run_back",
    )(
        mid, nf, gg, gates, nrm, weight_router, gains, cot_full, wao, mixed, qkv,
        probs, inputs, na, weight_qkv,
    )


def per_device(
    inputs,
    gain_attn,
    gain_ffn,
    weight_qkv,
    weight_attn_out,
    rel_table,
    weight_router,
    weight_in,
    weight_out,
    routes,
    segments,
    cotangent,
):
    seq_len, width = inputs.shape
    heads = rel_table.shape[1]
    experts = weight_router.shape[1]
    z = Sizes(experts, seq_len, routes.shape[1], width)
    gains = jnp.stack([gain_attn, gain_ffn])
    wqkv = jnp.transpose(weight_qkv, (0, 2, 1))
    wr = weight_router.T
    kept = run_layer(
        z, inputs, gains, wqkv, weight_attn_out, rel_table.T, wr, weight_in[0], weight_out[0],
        routes.T, segments, cotangent.T,
    )
    activations = return_results(
        z, kept["hid_out"], weight_out[0], kept["rk_out"], kept["gate_row_out"], kept["mid_out"]
    )
    grad_input, blocks, early, late = run_back(
        z, kept["mid_out"], kept["nf"], kept["gg"], kept["gates_out"], kept["nrm_out"],
        wr, gains, kept["cot_out"], weight_attn_out, kept["mixed_out"], kept["qkv_out"],
        kept["probs_out"], inputs, kept["na_out"], wqkv,
    )
    return (
        activations.T,
        grad_input,
        late[8 : 8 + width // SLOT, :].reshape(width),
        early[experts],
        jnp.transpose(blocks[0:3].astype(F32), (0, 2, 1)),
        blocks[3].astype(F32),
        late[0:heads, 0:BUCKETS].T,
        early[0:experts].T,
        kept["gw_in_out"][None],
        kept["gw_out_out"][None],
    )


def solution(mesh):
    in_specs = (
        P("expert", None),
        P(),
        P(),
        P(None, None, "tensor"),
        P("tensor", None),
        P(None, "tensor"),
        P(),
        P("expert", None, "tensor"),
        P("expert", "tensor", None),
        P("expert", None),
        P("expert"),
        P("expert", "tensor"),
    )
    out_specs = (
        P("expert", "tensor"),
        P("expert", None),
        P(),
        P(),
        P(None, None, "tensor"),
        P("tensor", None),
        P(None, "tensor"),
        P(),
        P("expert", None, "tensor"),
        P("expert", "tensor", None),
    )
    return jax.shard_map(
        per_device, mesh=mesh, in_specs=in_specs, out_specs=out_specs, check_vma=False
    )
```

```python
import functools
import math

import jax
import jax.numpy as jnp
from jax import lax
from jax.experimental import pallas as pl
from jax.experimental.pallas import tpu as pltpu
from jax.sharding import PartitionSpec as P

BUCKETS = 32
epsilon = 1e-06
negative = -1e30
F32 = jnp.float32
BF16 = jnp.bfloat16
MESH = pl.DeviceIdType.MESH
VMEM_SPEC = pl.BlockSpec(memory_space=pltpu.VMEM)
ANY_SPEC = pl.BlockSpec(memory_space=pl.ANY)
LANES = 128
ROW_TILE = 256
COL_TILE = 256
VMEM_LIMIT = 60 * 2**20


def dot_nn(left, right):
    return lax.dot_general(left, right, (((1,), (0,)), ((), ())), preferred_element_type=F32)


def dot_nt(left, right):
    return lax.dot_general(left, right, (((1,), (1,)), ((), ())), preferred_element_type=F32)


def dot_tn(left, right):
    return lax.dot_general(left, right, (((0,), (0,)), ((), ())), preferred_element_type=F32)


def round_up(value, step):
    return (value + step - 1) // step * step


class Sizes:
    def __init__(self, experts, seq_len, top_count, width):
        self.experts = experts
        self.seq = seq_len
        self.width = width
        self.half_width = width // 2
        capacity = (4 * seq_len * top_count + 24 * experts - 1) // (24 * experts) * 8
        self.slots = round_up(capacity, 32)
        self.half = self.slots // 2
        self.slot_lanes = round_up(self.slots, LANES)


class Place:
    def __init__(self, sizes):
        self.count = sizes.experts
        self.e = lax.axis_index("expert")
        self.t = lax.axis_index("tensor")
        self.c = lax.rem(self.t, 2)
        self.x = lax.div(self.t, 2)
        self.core_peer = self.t + 1 - 2 * self.c
        self.x_peer = lax.rem(self.t + 2, 4)

    def shifted(self, k, sign):
        group = self.count // 2
        parity = lax.rem(self.e, 2)
        flip = lax.rem(k, 2)
        turn = lax.div(k, 2)
        member = lax.rem(lax.div(self.e, 2) + group + sign * turn, group)
        return 2 * member + parity + flip - 2 * parity * flip

    def ahead(self, k):
        return self.shifted(k, 1)

    def behind(self, k):
        return self.shifted(k, -1)

    def steps_from(self, other):
        group = self.count // 2
        turn = lax.rem(lax.div(self.e, 2) + group - lax.div(other, 2), group)
        return 2 * turn + lax.rem(self.e + other, 2)

    def greet(self, expert_peers=True, all_tensor=True):
        barrier = pltpu.get_barrier_semaphore()
        count = 0
        if expert_peers:

            def one(k, carry):
                pl.semaphore_signal(
                    barrier, inc=1, device_id=(self.ahead(k), self.t), device_id_type=MESH
                )
                return carry

            lax.fori_loop(1, self.count, one, 0)
            count += self.count - 1
        for d in range(1, 4):
            pl.semaphore_signal(
                barrier,
                inc=1,
                device_id=(self.e, lax.rem(self.t + d, 4)),
                device_id_type=MESH,
            )
        count += 3
        pl.semaphore_wait(barrier, count)


def remote(src, dst, send_sem, recv_sem, device):
    return pltpu.make_async_remote_copy(
        src_ref=src,
        dst_ref=dst,
        send_sem=send_sem,
        recv_sem=recv_sem,
        device_id=device,
        device_id_type=MESH,
    )


class Gather:
    sem_kinds = 4

    def __init__(self, sizes, place, stage, buf, send, recv):
        self.z, self.p = sizes, place
        self.stage, self.buf, self.send, self.recv = stage, buf, send, recv

    def quarter(self, k, c, x):
        h, w = self.z.half, self.z.half_width
        return self.buf.at[
            k, pl.ds(pl.multiple_of(c * h, 16), h), pl.ds(pl.multiple_of(x * w, LANES), w)
        ]

    def out(self, k):
        p = self.p
        return remote(
            self.stage.at[k],
            self.quarter(k, p.c, p.x),
            self.send.at[0, k],
            self.recv.at[0, k],
            (p.ahead(k), p.t),
        )

    def to_core(self, k):
        p = self.p
        ref = self.quarter(k, p.c, p.x)
        return remote(ref, ref, self.send.at[1, k], self.recv.at[1, k], (p.e, p.core_peer))

    def to_x(self, k):
        p = self.p
        ref = self.quarter(k, p.c, p.x)
        return remote(ref, ref, self.send.at[2, k], self.recv.at[2, k], (p.e, p.x_peer))

    def on_to_core(self, k):
        p = self.p
        ref = self.quarter(k, p.c, 1 - p.x)
        return remote(ref, ref, self.send.at[3, k], self.recv.at[3, k], (p.e, p.core_peer))

    def pack_own(self, rk_row, rows_ref):
        z, p = self.z, self.p
        pick = slot_onehot(rk_row[pl.ds(p.e, 1), :], z.slots, 0)
        for j in range(0, z.width, COL_TILE):
            self.buf[0, :, j : j + COL_TILE] = dot_nn(
                pick, rows_ref[:, j : j + COL_TILE]
            ).astype(BF16)

    def pack(self, k, pick, rows_ref):
        z, p = self.z, self.p
        cols = rows_ref[:, pl.ds(pl.multiple_of(p.x * z.half_width, LANES), z.half_width)]
        self.stage[k] = dot_nn(pick, cols).astype(BF16)

    def first(self, k):
        self.out(k).wait_recv()
        self.to_core(k).start()
        self.to_x(k).start()

    def second(self, k):
        self.to_x(k).wait_recv()
        self.on_to_core(k).start()

    def last(self, k):
        self.to_core(k).wait_recv()
        self.on_to_core(k).wait_recv()

    def finish(self, k):
        self.out(k).wait_send()
        self.to_core(k).wait_send()
        self.to_x(k).wait_send()
        self.on_to_core(k).wait_send()


class Return:
    sem_kinds = 3

    def __init__(self, sizes, place, part, from_core, stage_x, from_x, ret, send, recv):
        self.z, self.p = sizes, place
        self.part, self.from_core, self.stage_x = part, from_core, stage_x
        self.from_x, self.ret = from_x, ret
        self.send, self.recv = send, recv
        self.ring = part.shape[0] // sizes.slots

    def rows_of(self, k):
        return pl.ds(
            pl.multiple_of(lax.rem(k, self.ring) * self.z.slots, 16), self.z.slots
        )

    def make_room(self, k):
        @pl.when(k >= self.ring)
        def _():
            self.to_core(k - self.ring).wait_send()

    def part_rows(self, k, c):
        start = lax.rem(k, self.ring) * self.z.slots + c * self.z.half
        return pl.ds(pl.multiple_of(start, 16), self.z.half)

    def cols(self, x):
        return pl.ds(pl.multiple_of(x * self.z.half_width, LANES), self.z.half_width)

    def to_core(self, k):
        p = self.p
        return remote(
            self.part.at[self.part_rows(k, 1 - p.c), :],
            self.from_core.at[k],
            self.send.at[0, k],
            self.recv.at[0, k],
            (p.e, p.core_peer),
        )

    def to_x(self, k):
        p = self.p
        return remote(
            self.stage_x.at[k],
            self.from_x.at[k],
            self.send.at[1, k],
            self.recv.at[1, k],
            (p.e, p.x_peer),
        )

    def home(self, k):
        p = self.p
        return remote(
            self.from_core.at[k, :, self.cols(p.x)],
            self.ret.at[k],
            self.send.at[2, k],
            self.recv.at[2, k],
            (p.behind(k), p.t),
        )

    def first(self, k):
        self.to_core(k).start()

    def second(self, k):
        p = self.p
        self.to_core(k).wait_recv()
        rows = self.part_rows(k, p.c)
        for x in (1 - p.x, p.x):
            cols = self.cols(x)
            both = self.part[rows, cols].astype(F32) + self.from_core[k, :, cols].astype(F32)
            if x is p.x:
                self.from_core[k, :, cols] = both.astype(BF16)
            else:
                self.stage_x[k] = both.astype(BF16)
                self.to_x(k).start()

    def third(self, k):
        self.to_x(k).wait_recv()
        cols = self.cols(self.p.x)
        total = self.from_core[k, :, cols].astype(F32) + self.from_x[k].astype(F32)

        @pl.when(k == 0)
        def _():
            self.ret[0] = total.astype(BF16)

        @pl.when(k > 0)
        def _():
            self.from_core[k, :, cols] = total.astype(BF16)
            self.home(k).start()

    def arrive(self, k):
        @pl.when(k > 0)
        def _():
            self.home(k).wait_recv()

    def finish(self, k):
        @pl.when(k + self.ring >= self.z.experts)
        def _():
            self.to_core(k).wait_send()

        self.to_x(k).wait_send()

        @pl.when(k > 0)
        def _():
            self.home(k).wait_send()


def return_scratch(z, ring):
    e, h, w = z.experts, z.half, z.half_width
    return [
        pltpu.VMEM((ring * z.slots, z.width), BF16),
        pltpu.VMEM((e, h, z.width), BF16),
        pltpu.VMEM((e, h, w), BF16),
        pltpu.VMEM((e, h, w), BF16),
        pltpu.VMEM((e, h, w), BF16),
        pltpu.SemaphoreType.DMA((Return.sem_kinds, e)),
        pltpu.SemaphoreType.DMA((Return.sem_kinds, e)),
    ]


def gather_scratch(z):
    e, h, w = z.experts, z.half, z.half_width
    return [
        pltpu.VMEM((e, h, w), BF16),
        pltpu.VMEM((e, z.slots, z.width), BF16),
        pltpu.SemaphoreType.DMA((Gather.sem_kinds, e)),
        pltpu.SemaphoreType.DMA((Gather.sem_kinds, e)),
    ]


def slot_onehot(rank_row, count, offset):
    slot = lax.broadcasted_iota(jnp.int32, (count, rank_row.shape[1]), 0).astype(F32)
    shift = lax.convert_element_type(offset, F32)
    return jnp.where(rank_row - shift == slot, 1.0, 0.0).astype(BF16)


def pick_lane(values, lane):
    lanes = lax.broadcasted_iota(jnp.int32, values.shape, 1)
    return jnp.sum(jnp.where(lanes == lane, values, 0.0), axis=1, keepdims=True)


def row_to_col(row, count, offset):
    rows = lax.broadcasted_iota(jnp.int32, (count, row.shape[1]), 0) + offset
    lanes = lax.broadcasted_iota(jnp.int32, (count, row.shape[1]), 1)
    return jnp.sum(jnp.where(rows == lanes, row, 0.0), axis=1, keepdims=True)


def col_to_row(col, lane_count):
    rows = lax.broadcasted_iota(jnp.int32, (col.shape[0], lane_count), 0)
    lanes = lax.broadcasted_iota(jnp.int32, (col.shape[0], lane_count), 1)
    return jnp.sum(jnp.where(rows == lanes, col, 0.0), axis=0, keepdims=True)


def loop(start, stop, body):
    def step(i, carry):
        body(i)
        return carry

    lax.fori_loop(start, stop, step, 0)


def fill_ranks(routes_ref, rk_col, rk_row):
    seq = routes_ref.shape[1]
    ids = lax.broadcasted_iota(jnp.int32, (LANES, seq), 0)
    hot = (routes_ref[0:1, :] == ids) | (routes_ref[1:2, :] == ids)
    hot_mark = jnp.where(hot, 1.0, 0.0)
    hot_low = hot_mark.astype(BF16)
    for s in range(0, seq, ROW_TILE):
        rows = lax.broadcasted_iota(jnp.int32, (seq, ROW_TILE), 0)
        cols = lax.broadcasted_iota(jnp.int32, (seq, ROW_TILE), 1) + s
        before = jnp.where(rows < cols, 1.0, 0.0).astype(BF16)
        rank = dot_nn(hot_low, before)
        rank = jnp.where(hot_mark[:, s : s + ROW_TILE] > 0.5, rank, -1.0)
        rk_row[:, s : s + ROW_TILE] = rank
        rk_col[s : s + ROW_TILE, :] = rank.T


def gelu_pair(h):
    scale = 0.7978845608028654
    square = h * h
    t = jnp.tanh(scale * h * (1.0 + 0.044715 * square))
    half = 0.5 + 0.5 * t
    slope = half + (0.5 * scale) * h * (1.0 - t * t) * (1.0 + 0.134145 * square)
    return h * half, slope


def far_limits(buckets):
    half_size = buckets // 2
    base_ratio = 256.0 / buckets
    return [
        int(math.ceil(half_size * base_ratio ** (step / half_size))) for step in range(1, half_size)
    ]


TILE = 256
WINDOW = 3 * TILE
SLOT = 256


def distance_of(lane):
    return jnp.where(lane < WINDOW, 2 * TILE - lane, 2 * TILE + 4 * TILE - lane)


def bucket_grid(distance):
    half_size = BUCKETS // 2
    far = jnp.full(distance.shape, half_size, jnp.int32)
    for limit in far_limits(BUCKETS):
        far = far + jnp.where(distance >= limit, 1, 0)
    return jnp.where(distance < half_size, distance, far)


def fill_bias(table_ref, bias, heads):
    lane = lax.broadcasted_iota(jnp.int32, (1, 4 * TILE), 1)
    distance = distance_of(lane)
    bucket = bucket_grid(distance)
    for h in range(heads):
        values = jnp.full((1, 4 * TILE), negative, F32)
        for b in range(BUCKETS):
            values = jnp.where(bucket == b, table_ref[h, b], values)
        wide = jnp.broadcast_to(values, (TILE, 4 * TILE))
        rolled = pltpu.roll(wide, 0, 1, stride=1, stride_axis=0)
        bias[h] = rolled[:, 0:WINDOW]


def head_lanes(rows, h, size):
    lanes = lax.broadcasted_iota(jnp.int32, (rows, SLOT), 1)
    return (lanes >= h * size) & (lanes < (h + 1) * size)


def mask_head(values, h, size):
    keep = head_lanes(values.shape[0], h, size)
    return jnp.where(keep, values, jnp.zeros_like(values))


def tiles_of(seq):
    return range(seq // TILE)


def window_of(i):
    start = max(0, i - 2) * TILE
    return start, (i + 1) * TILE - start


def attention_tile(i, h, size, qkv, seg_col, seg_row, bias):
    start, width = window_of(i)
    query = mask_head(qkv[i * TILE : (i + 1) * TILE, 0:SLOT], h, size)
    keys = qkv[start : start + width, SLOT : 2 * SLOT]
    scores = dot_nt(query, keys) + bias[h, :, WINDOW - width :]
    same = seg_col[i * TILE : (i + 1) * TILE, 0:1] == seg_row[:, start : start + width].astype(F32)
    scores = jnp.where(same, scores, negative)
    power = jnp.exp(scores - jnp.max(scores, axis=1, keepdims=True))
    probs = power * (1.0 / jnp.sum(power, axis=1, keepdims=True))
    return probs.astype(BF16)


def layer_kernel(z, heads, names, *refs):
    r = Names(names, refs)
    p = Place(z)
    experts = z.experts
    cols = r.cot.shape[0]
    size = cols // heads
    tiles = list(tiles_of(z.seq))
    count = len(tiles)
    p.greet()
    saves = []
    save_ids = iter(range(16))

    def save(src, dst):
        copy = pltpu.make_async_copy(src, dst, r.save_sem.at[next(save_ids)])
        copy.start()
        saves.append(copy)

    cot_rows = lambda t: r.cot_all.at[pl.ds(pl.multiple_of(t * cols, 16), cols), :]
    wao_rows = lambda t: r.wao_all.at[pl.ds(pl.multiple_of(t * cols, 16), cols), :]

    def spread(rows, n):
        def copy(t, m, peer):
            return remote(
                rows(t), rows(t), r.c_sems.at[0, n, m], r.c_sems.at[1, n, m], (p.e, peer)
            )

        return (
            copy(p.t, 0, p.core_peer), copy(p.t, 1, p.x_peer), copy(p.x_peer, 2, p.core_peer)
        )

    cot_rows(p.t)[...] = r.cot[...]
    cot_copies = spread(cot_rows, 0)
    cot_copies[0].start()
    wao_rows(p.t)[...] = r.wao[...]
    wao_copies = spread(wao_rows, 1)
    wao_copies[1].start()
    wao_copies[0].start()
    cot_copies[1].start()
    fill_ranks(r.routes, r.rk_col, r.rk_row)
    save(r.rk_row, r.rk_out)
    og = Gather(z, p, r.stage, r.og_buf, r.og_send, r.og_recv)
    g = Gather(z, p, r.stage, r.buf, r.g_send, r.g_recv)
    b = Return(
        z, p, r.part, r.from_core, r.stage_x, r.from_x, r.ret, r.r_send, r.r_recv
    )

    def in_chip(own, peer):
        return jnp.where(
            p.c == 0,
            jnp.concatenate([own, peer], axis=1),
            jnp.concatenate([peer, own], axis=1),
        )

    cot_copies[0].wait_recv()

    def half_pick(k):
        return slot_onehot(r.rk_row[pl.ds(p.ahead(k), 1), :], z.half, p.c * z.half)

    def pack_og(k):
        own = r.cot_all[pl.ds(pl.multiple_of(p.x * z.half_width, 16), z.half_width), :]
        rows = dot_nt(half_pick(k), own).astype(BF16)

        @pl.when(k > 0)
        def _():
            r.stage[k] = rows
            og.out(k).start()

        @pl.when(k == 0)
        def _():
            og.quarter(0, p.c, p.x)[...] = rows
            og.to_core(0).start()
            og.to_x(0).start()

    loop(1, experts, pack_og)
    pack_og(0)
    wide_row = jnp.broadcast_to(r.seg_row[...].astype(F32), (LANES, z.seq))
    r.qkv[...] = jnp.zeros_like(r.qkv)
    for i in tiles:
        rows = slice(i * TILE, (i + 1) * TILE)
        r.seg_col[rows, :] = wide_row[:, rows].T
        stream = r.x[rows, :].astype(F32)
        root = lax.rsqrt(jnp.mean(stream * stream, axis=1, keepdims=True) + epsilon)
        normed = (stream * root * r.gains[0:1, :]).astype(BF16)
        r.na[rows, :] = normed
        for k in range(3):
            cut = slice(k * SLOT, k * SLOT + cols)
            out = dot_nt(normed, r.wqkv[k]).astype(BF16)
            if k == 0:
                out = (out.astype(F32) * size ** (-0.5)).astype(BF16)
            r.qkv[rows, cut] = out
    na_saved = len(saves)
    save(r.na, r.na_out)
    save(r.qkv, r.qkv_out)
    fill_bias(r.table, r.bias, heads)

    def probs_rows(i, h):
        return pl.ds((i % 2 * heads + h) * TILE, TILE)

    def save_probs(i, h):
        _, width = window_of(i)
        return pltpu.make_async_copy(
            r.part.at[probs_rows(i, h), pl.ds(0, width)],
            r.probs_out.at[h, pl.ds(i * TILE, TILE), pl.ds(0, width)],
            r.p_sem.at[i, h],
        )

    def mixed_core(i):
        rows = pl.ds(i * TILE, TILE)
        return remote(
            r.mixed.at[rows, :], r.mixed_in.at[rows, :], r.m_sems.at[0, 0, i],
            r.m_sems.at[1, 0, i], (p.e, p.core_peer),
        )

    def mixed_piece(i, x):
        half = TILE // 2
        return r.mc.at[
            pl.ds(pl.multiple_of(i * TILE + p.c * half, 16), half),
            pl.ds(pl.multiple_of(x * z.half_width, LANES), z.half_width),
        ]

    def mixed_x(i):
        ref = mixed_piece(i, p.x)
        return remote(ref, ref, r.m_sems.at[0, 1, i], r.m_sems.at[1, 1, i], (p.e, p.x_peer))

    def mixed_on(i):
        ref = mixed_piece(i, 1 - p.x)
        return remote(ref, ref, r.m_sems.at[0, 2, i], r.m_sems.at[1, 2, i], (p.e, p.core_peer))

    def attend(i):
        rows = slice(i * TILE, (i + 1) * TILE)
        start, width = window_of(i)
        total = jnp.zeros((TILE, SLOT), F32)
        for h in range(heads):
            if i >= 2:
                save_probs(i - 2, h).wait()
            low = attention_tile(i, h, size, r.qkv, r.seg_col, r.seg_row, r.bias)
            r.part[probs_rows(i, h), 0:width] = low
            save_probs(i, h).start()
            values = mask_head(r.qkv[start : start + width, 2 * SLOT :], h, size)
            total = total + dot_nn(low, values)
        r.mixed[rows, :] = total[:, 0:cols].astype(BF16)
        mixed_core(i).start()

    def share(i):
        mixed_core(i).wait_recv()
        rows = slice(i * TILE, (i + 1) * TILE)
        both = in_chip(r.mixed[rows, :], r.mixed_in[rows, :])
        r.mc[rows, pl.ds(pl.multiple_of(p.x * z.half_width, LANES), z.half_width)] = both
        mixed_x(i).start()

    for i in tiles:
        attend(i)
        if i >= 1:
            share(i - 1)
        if i >= 2:
            mixed_x(i - 2).wait_recv()
            mixed_on(i - 2).start()
        if i == 0:
            wao_copies[1].wait_recv()
            wao_copies[2].start()
        if i == 2:
            cot_copies[1].wait_recv()
            cot_copies[2].start()
    share(count - 1)
    save(r.mixed, r.mixed_out)
    saves.pop(na_saved).wait()
    r.wr_pad[...] = jnp.zeros_like(r.wr_pad)
    r.wr_pad[0:experts, :] = r.wr[...].astype(F32)
    router = r.wr_pad[...].astype(BF16)
    for copy in (wao_copies[0], wao_copies[2], cot_copies[2]):
        copy.wait_recv()

    def project(i):
        rows = slice(i * TILE, (i + 1) * TILE)
        mid = r.x[rows, :].astype(F32) + dot_nn(r.mc[rows, :], r.wao_all[...])
        r.mid[rows, :] = mid
        root = lax.rsqrt(jnp.mean(mid * mid, axis=1, keepdims=True) + epsilon)
        nrm = (mid * root * r.gains[1:2, :]).astype(BF16)
        r.na[rows, :] = nrm
        logits = dot_nt(nrm, router)
        hot = r.rk_col[rows, :] > -0.5
        logits = jnp.where(hot, logits, negative)
        peak = jnp.max(logits, axis=1, keepdims=True)
        power = jnp.where(hot, jnp.exp(logits - peak), 0.0)
        gates = power / jnp.sum(power, axis=1, keepdims=True)
        r.gates[rows, :] = gates
        r.gate_row[:, rows] = gates.T

    for i in tiles:
        if i + 2 >= count:
            mixed_x(i).wait_recv()
            mixed_on(i).start()
        if i == 2:
            og.second(0)
        mixed_on(i).wait_recv()
        project(i)
    for k in range(1, EARLY):
        og.first(k)
    mid_saved = len(saves)
    save(r.mid, r.mid_out)
    save(r.na, r.nrm_out)
    save(r.gates, r.gates_out)
    save(r.gate_row, r.gate_row_out)
    save(r.cot_all, r.cot_out)

    def gate_copy(k):
        return remote(
            r.gs_out.at[k], r.gs_in.at[k], r.gs_sems.at[0, k], r.gs_sems.at[1, k],
            (p.ahead(k), p.t),
        )

    def slot_gates(k):
        pick = slot_onehot(r.rk_row[pl.ds(p.ahead(k), 1), :], z.slot_lanes, 0)
        row = r.gate_row[pl.ds(p.ahead(k), 1), :]
        high = row.astype(BF16).astype(F32)
        low = row - high
        which = lax.broadcasted_iota(jnp.int32, (16, z.seq), 0)
        both = jnp.where(which == 0, high, jnp.where(which == 1, low, 0.0)).astype(BF16)
        sums = dot_nt(both, pick)
        return sums[0:1, :] + sums[1:2, :]

    for i in tiles[-2:]:
        for h in range(heads):
            save_probs(i, h).wait()

    def pack(k):
        og.out(k).wait_send()
        g.pack(k, half_pick(k), r.na)
        g.out(k).start()

    loop(1, experts, pack)

    def send_gates(k):
        r.gs_out[k] = slot_gates(k)
        gate_copy(k).start()

    loop(1, experts, send_gates)
    r.gs_in[0] = slot_gates(0)
    g.pack_own(r.rk_row, r.na)

    def gg_copy(k, d):
        return remote(
            r.gg_send.at[k],
            r.gg_recv.at[k, p.t],
            r.gg_sems.at[0, k, d],
            r.gg_sems.at[1, k, d],
            (p.behind(k), lax.rem(p.t + d, 4)),
        )

    def save_hid(k):
        return pltpu.make_async_copy(r.hid.at[lax.rem(k, 2)], r.hid_out.at[k], r.hid_sem.at[k])

    def expert(k):
        ring = lax.rem(k, 2)

        @pl.when(k > 0)
        def _():
            gate_copy(k).wait_recv()
            g.last(k)

        @pl.when(k > 1)
        def _():
            save_hid(k - 2).wait()

        og.last(k)
        gate = row_to_col(r.gs_in[k], z.slots, 0)
        sums = jnp.zeros((z.slots, 1), F32)
        for j in range(0, r.w_in.shape[1], COL_TILE):
            cut = slice(j, j + COL_TILE)
            up, slope = gelu_pair(dot_nn(r.buf[k], r.w_in[:, cut]))
            back = dot_nt(r.og_buf[k], r.w_out[cut, :])
            r.hid[ring, :, cut] = up.astype(BF16)
            r.pre[ring, :, cut] = (gate * back * slope).astype(BF16)
            sums = sums + jnp.sum(up * back, axis=1, keepdims=True)
        for j in range(0, z.width, COL_TILE):
            r.part[b.rows_of(k), j : j + COL_TILE] = dot_nt(
                r.pre[ring], r.w_in[j : j + COL_TILE, :]
            ).astype(BF16)
        b.first(k)
        r.gg_send[k] = col_to_row(sums, z.slot_lanes)
        for d in range(1, 4):
            gg_copy(k, d).start()

        @pl.when(k > 0)
        def _():
            gg_copy(k, 0).start()

        @pl.when(k == 0)
        def _():
            r.gg_recv[0, p.t] = r.gg_send[0]

        save_hid(k).start()

    def weight_grads(k):
        ring = lax.rem(k, 2)
        gate = row_to_col(r.gs_in[k], z.slots, 0)
        r.gated[...] = (gate * r.og_buf[k].astype(F32)).astype(BF16)
        for j in range(0, z.width, COL_TILE):
            cut = slice(j, j + COL_TILE)
            r.gw_in[cut, :] += dot_tn(r.buf[k, :, cut], r.pre[ring])
            r.gw_out[cut, :] += dot_tn(r.hid[ring, :, cut], r.gated[...])

    r.gw_in[...] = jnp.zeros_like(r.gw_in)
    r.gw_out[...] = jnp.zeros_like(r.gw_out)

    def body(i):
        @pl.when(i + EARLY < experts)
        def _():
            og.first(i + EARLY)

        @pl.when(i + 1 < experts)
        def _():
            og.second(i + 1)

        @pl.when(i < experts)
        def _():
            expert(i)

        @pl.when(i == 0)
        def _():
            g.first(1)

        @pl.when(i + 2 < experts)
        def _():
            g.first(i + 2)

        @pl.when(i + 1 < experts)
        def _():
            g.second(i + 1)

        @pl.when((i >= 1) & (i <= experts))
        def _():
            b.second(i - 1)

        @pl.when(i >= 2)
        def _():
            b.third(i - 2)

        @pl.when((i >= 1) & (i <= experts))
        def _():
            weight_grads(i - 1)

    loop(0, experts + 2, body)
    save(r.gw_in, r.gw_in_out)
    save(r.gw_out, r.gw_out_out)
    saves.pop(mid_saved).wait()
    acc = r.mid.at[:, pl.ds(0, z.half_width + LANES)]
    acc[...] = jnp.zeros(acc.shape, F32)

    def combine(k):
        b.arrive(k)
        for d in range(1, 4):
            gg_copy(k, d).wait_recv()

        @pl.when(k > 0)
        def _():
            gg_copy(k, 0).wait_recv()

        row = r.gg_recv[k, 0] + r.gg_recv[k, 1] + r.gg_recv[k, 2] + r.gg_recv[k, 3]
        col = row_to_col(row, z.half, p.c * z.half)
        high = col.astype(BF16).astype(F32)
        lanes = lax.broadcasted_iota(jnp.int32, (z.half, LANES), 1)
        who = p.ahead(k)
        r.retx[:, 0 : z.half_width] = r.ret[k]
        r.retx[:, z.half_width :] = jnp.where(
            lanes == who, high, jnp.where(lanes == who + experts, col - high, 0.0)
        ).astype(BF16)
        for s in range(0, z.seq, ROW_TILE):
            rows = slice(s, s + ROW_TILE)
            rank = pick_lane(r.rk_col[rows, :], who) - lax.convert_element_type(p.c * z.half, F32)
            slot = lax.broadcasted_iota(jnp.int32, (ROW_TILE, z.half), 1).astype(F32)
            pick = jnp.where(rank == slot, 1.0, 0.0).astype(BF16)
            acc[rows, :] += dot_nn(pick, r.retx[...])

    loop(0, experts, combine)
    half_seq = z.seq // 2

    def tokens(c):
        return pl.ds(pl.multiple_of(c * half_seq, 16), half_seq)

    def d_copy(src, dst, n, peer):
        return remote(src, dst, r.d_sems.at[0, n], r.d_sems.at[1, n], (p.e, peer))

    r.d_send[...] = acc[tokens(1 - p.c), 0 : z.half_width].astype(BF16)
    r.gd_send[...] = acc[:, z.half_width :].astype(BF16)
    copy_d = d_copy(r.d_send, r.d_recv, 0, p.core_peer)
    copy_g = d_copy(r.gd_send, r.gd_recv, 1, p.core_peer)
    copy_d.start()
    copy_g.start()
    copy_d.wait_recv()

    def piece(x):
        return r.nf.at[tokens(p.c), pl.ds(pl.multiple_of(x * z.half_width, LANES), z.half_width)]

    piece(p.x)[...] = (
        acc[tokens(p.c), 0 : z.half_width] + r.d_recv[...].astype(F32)
    ).astype(BF16)
    to_x = d_copy(piece(p.x), piece(p.x), 2, p.x_peer)
    to_core = d_copy(piece(p.x), piece(p.x), 3, p.core_peer)
    on_to_core = d_copy(piece(1 - p.x), piece(1 - p.x), 4, p.core_peer)
    to_x.start()
    to_core.start()
    copy_g.wait_recv()
    r.gg[...] = acc[:, z.half_width :] + r.gd_recv[...].astype(F32)

    def finish(k):
        b.finish(k)
        for d in range(1, 4):
            gg_copy(k, d).wait_send()

        @pl.when(k > 0)
        def _():
            g.finish(k)
            gate_copy(k).wait_send()
            gg_copy(k, 0).wait_send()

        og.to_core(k).wait_send()
        og.to_x(k).wait_send()
        og.on_to_core(k).wait_send()

        @pl.when(k >= experts - 2)
        def _():
            save_hid(k).wait()

    loop(0, experts, finish)
    for copy in cot_copies + wao_copies:
        copy.wait_send()
    for i in tiles:
        mixed_core(i).wait_send()
        mixed_x(i).wait_send()
        mixed_on(i).wait_send()
    to_x.wait_recv()
    on_to_core.start()
    to_core.wait_recv()
    on_to_core.wait_recv()
    for copy in (copy_d, copy_g, to_x, to_core, on_to_core):
        copy.wait_send()
    for copy in saves:
        copy.wait()


class Names:
    def __init__(self, names, refs):
        for name, ref in zip(names, refs, strict=True):
            setattr(self, name, ref)


EARLY = 4


def run_layer(
    z, inputs, gains, weight_qkv, weight_attn_out, rel_table, weight_router, w_in, w_out,
    routes, segments, cotangent,
):
    e, seq, width = z.experts, z.seq, z.width
    heads, cols = rel_table.shape[0], weight_qkv.shape[1]
    hidden_count = w_in.shape[1]
    tiles = seq // TILE
    half_seq = seq // 2
    smem = pl.BlockSpec(memory_space=pltpu.SMEM)
    dma = pltpu.SemaphoreType.DMA
    args = dict(
        table=rel_table,
        x=inputs,
        gains=gains,
        wqkv=weight_qkv,
        wao=weight_attn_out,
        wr=weight_router,
        w_in=w_in,
        w_out=w_out,
        routes=routes,
        seg_row=segments.reshape(1, -1),
        cot=cotangent,
    )
    outs = dict(
        rk_out=((LANES, seq), F32),
        gate_row_out=((LANES, seq), F32),
        cot_out=((width, seq), BF16),
        na_out=((seq, width), BF16),
        qkv_out=((seq, 3 * SLOT), BF16),
        mixed_out=((seq, cols), BF16),
        probs_out=((heads, seq, WINDOW), BF16),
        mid_out=((seq, width), F32),
        nrm_out=((seq, width), BF16),
        gates_out=((seq, LANES), F32),
        hid_out=((e, z.slots, hidden_count), BF16),
        gw_in_out=((width, hidden_count), F32),
        gw_out_out=((hidden_count, width), F32),
        nf=((seq, width), BF16),
        gg=((seq, LANES), F32),
    )
    in_vmem = ("nf", "gg")
    gather_names = (("stage", "og_buf", "og_send", "og_recv"), ("stage", "buf", "g_send", "g_recv"))
    scratch = {}
    for group in gather_names:
        scratch.update(zip(group, gather_scratch(z)))
    scratch.update(
        zip(
            ("part", "from_core", "stage_x", "from_x", "ret", "r_send", "r_recv"),
            return_scratch(z, e),
            strict=True,
        )
    )
    shapes = dict(
        rk_col=((seq, LANES), F32),
        rk_row=((LANES, seq), F32),
        na=((seq, width), BF16),
        qkv=((seq, 3 * SLOT), BF16),
        mixed=((seq, cols), BF16),
        mid=((seq, width), F32),
        gates=((seq, LANES), F32),
        gw_in=((width, hidden_count), F32),
        gw_out=((hidden_count, width), F32),
        bias=((heads, TILE, WINDOW), F32),
        cot_all=((width, seq), BF16),
        wao_all=((width, width), BF16),
        wr_pad=((LANES, width), F32),
        seg_col=((seq, LANES), F32),
        mixed_in=((seq, cols), BF16),
        mc=((seq, width), BF16),
        hid=((2, z.slots, hidden_count), BF16),
        pre=((2, z.slots, hidden_count), BF16),
        gated=((z.slots, width), BF16),
        gate_row=((LANES, seq), F32),
        gs_out=((e, 1, z.slot_lanes), F32),
        gs_in=((e, 1, z.slot_lanes), F32),
        gg_send=((e, 1, z.slot_lanes), F32),
        gg_recv=((e, 4, 1, z.slot_lanes), F32),
        retx=((z.half, z.half_width + LANES), BF16),
        d_send=((half_seq, z.half_width), BF16),
        d_recv=((half_seq, z.half_width), BF16),
        gd_send=((seq, LANES), BF16),
        gd_recv=((seq, LANES), BF16),
    )
    for name, (shape, dtype) in shapes.items():
        scratch[name] = pltpu.VMEM(shape, dtype)
    scratch.update(
        dict(
            save_sem=dma((16,)),
            hid_sem=dma((e,)),
            p_sem=dma((tiles, heads)),
            c_sems=dma((2, 2, 3)),
            m_sems=dma((2, 3, tiles)),
            gs_sems=dma((2, e)),
            gg_sems=dma((2, e, 4)),
            d_sems=dma((2, 5)),
        )
    )
    names = list(args) + list(outs) + list(scratch)
    results = pl.pallas_call(
        functools.partial(layer_kernel, z, heads, names),
        out_shape=tuple(jax.ShapeDtypeStruct(*outs[n]) for n in outs),
        in_specs=[smem] + [VMEM_SPEC] * (len(args) - 1),
        out_specs=tuple(VMEM_SPEC if n in in_vmem else ANY_SPEC for n in outs),
        scratch_shapes=list(scratch.values()),
        compiler_params=pltpu.CompilerParams(
            collective_id=1, has_side_effects=True, vmem_limit_bytes=VMEM_LIMIT
        ),
        name="run_layer",
    )(*args.values())
    return Names(list(outs), results)


class Reduce:
    def __init__(self, z, p, blocks, in_pair, in_group, half_sum, result, pair_sems, group_sems):
        self.z, self.p = z, p
        self.blocks, self.in_pair, self.in_group = blocks, in_pair, in_group
        self.half_sum, self.result = half_sum, result
        self.pair_sems, self.group_sems = pair_sems, group_sems
        self.half_rows, self.group, self.row_parts, self.col_parts = reduce_cut(z, blocks.shape[1])
        self.owners = self.row_parts * self.col_parts
        self.piece_rows = self.half_rows // self.row_parts
        self.piece_cols = z.width // self.col_parts
        self.parity = lax.rem(p.e, 2)
        self.member = lax.div(p.e, 2)
        self.partner = p.e + 1 - 2 * self.parity

    def half(self, which):
        return pl.ds(pl.multiple_of(which * self.half_rows, 16), self.half_rows)

    def piece(self, owner, base):
        row = base + lax.div(owner, self.col_parts) * self.piece_rows
        col = lax.rem(owner, self.col_parts) * self.piece_cols
        return (
            pl.ds(pl.multiple_of(row, 16), self.piece_rows),
            pl.ds(pl.multiple_of(col, LANES), self.piece_cols),
        )

    def other(self, k):
        return lax.rem(self.member + k, self.group)

    def before(self, k):
        return lax.rem(self.member + self.group - k, self.group)

    def device(self, member):
        return (2 * member + self.parity, self.p.t)

    def pair_in(self, b):
        return remote(
            self.blocks.at[b, self.half(1 - self.parity), :],
            self.in_pair.at[b],
            self.pair_sems.at[0, 0, b],
            self.pair_sems.at[1, 0, b],
            (self.partner, self.p.t),
        )

    def spread(self, b, k):
        rows, cols = self.piece(self.other(k), 0)
        return remote(
            self.half_sum.at[b, rows, cols],
            self.in_group.at[b, k],
            self.group_sems.at[0, 0, b, k],
            self.group_sems.at[1, 0, b, k],
            self.device(self.other(k)),
        )

    def share(self, b, k):
        rows, cols = self.piece(self.member, self.parity * self.half_rows)
        ref = self.result.at[b, rows, cols]
        return remote(
            ref,
            ref,
            self.group_sems.at[0, 1, b, k],
            self.group_sems.at[1, 1, b, k],
            self.device(self.other(k)),
        )

    def pair_out(self, b):
        ref = self.result.at[b, self.half(self.parity), :]
        return remote(
            ref,
            ref,
            self.pair_sems.at[0, 1, b],
            self.pair_sems.at[1, 1, b],
            (self.partner, self.p.t),
        )

    def first(self, b):
        self.pair_in(b).start()

    def second(self, b):
        self.pair_in(b).wait_recv()
        mine = self.blocks[b, self.half(self.parity), :].astype(F32)
        self.half_sum[b] = (mine + self.in_pair[b].astype(F32)).astype(BF16)

        def send(k):
            @pl.when(self.other(k) < self.owners)
            def _():
                self.spread(b, k).start()

        loop(1, self.group, send)

    def third(self, b):
        @pl.when(self.member < self.owners)
        def _():
            rows, cols = self.piece(self.member, 0)
            total = self.half_sum[b, rows, cols].astype(F32)

            def add(k, total):
                self.spread(b, k).wait_recv()
                return total + self.in_group[b, k].astype(F32)

            total = lax.fori_loop(1, self.group, add, total)
            rows, cols = self.piece(self.member, self.parity * self.half_rows)
            self.result[b, rows, cols] = total.astype(BF16)
            loop(1, self.group, lambda k: self.share(b, k).start())

    def fourth(self, b):
        def wait(k):
            @pl.when(self.before(k) < self.owners)
            def _():
                self.share(b, k).wait_recv()

        loop(1, self.group, wait)
        self.pair_out(b).start()

    def last(self, b):
        self.pair_out(b).wait_recv()

    def finish(self, b):
        self.pair_in(b).wait_send()
        self.pair_out(b).wait_send()

        def wait(k):
            @pl.when(self.other(k) < self.owners)
            def _():
                self.spread(b, k).wait_send()

            @pl.when(self.member < self.owners)
            def _():
                self.share(b, k).wait_send()

        loop(1, self.group, wait)


def reduce_cut(z, rows):
    half_rows, group = rows // 2, z.experts // 2
    best = (1, 1)
    for row_parts in range(1, half_rows // 16 + 1):
        for col_parts in range(1, z.width // LANES + 1):
            if (half_rows // 16) % row_parts or (z.width // LANES) % col_parts:
                continue
            if best[0] * best[1] < row_parts * col_parts <= group:
                best = (row_parts, col_parts)
    return half_rows, group, best[0], best[1]


def reduce_scratch(z, blocks, rows):
    half_rows, group, row_parts, col_parts = reduce_cut(z, rows)
    piece = (half_rows // row_parts, z.width // col_parts)
    return [
        pltpu.VMEM((blocks, rows, z.width), BF16),
        pltpu.VMEM((blocks, half_rows, z.width), BF16),
        pltpu.VMEM((blocks, group) + piece, BF16),
        pltpu.VMEM((blocks, half_rows, z.width), BF16),
        pltpu.VMEM((blocks, rows, z.width), BF16),
        pltpu.SemaphoreType.DMA((2, 2, blocks)),
        pltpu.SemaphoreType.DMA((2, 2, blocks, group)),
    ]


def tail_sums(dbias):
    wide = dbias.shape[1]
    count = TILE
    while count > 8:
        half = count // 2
        dbias = dbias[0:half, :] + pltpu.roll(dbias[half:count, :], wide - half, 1)
        count = half
    total = dbias[0:1, :]
    for r in range(1, count):
        total = total + pltpu.roll(dbias[r : r + 1, :], wide - r, 1)
    return total


def split_dot(values, right):
    high = values.astype(BF16)
    rest = values - high.astype(F32)
    middle = rest.astype(BF16)
    low = (rest - middle.astype(F32)).astype(BF16)
    return dot_nn(high, right) + dot_nn(middle, right) + dot_nn(low, right)


def back_kernel(z, heads, names, *refs):
    r = Names(names, refs)
    p = Place(z)
    experts = z.experts
    cols = r.wao.shape[0]
    size = cols // heads
    loads = {}
    for n, name in enumerate(BACK_LOADS):
        loads[name] = pltpu.make_async_copy(
            getattr(r, name), getattr(r, name + "_in"), r.load_sem.at[n]
        )
        loads[name].start()
    midg, probs, qkv, na_ref, x_ref = (getattr(r, name + "_in") for name in BACK_LOADS)
    blocks, nag, dmix, dqkv, part = r.blocks, r.nag, r.dmix, r.dqkv, r.part_sum
    dk, dv, dbias, late, late_in, s_sems = r.dk, r.dv, r.dbias, r.late, r.late_in, r.s_sems
    n_core, n_sx, n_x, n_sems = r.n_core, r.n_sx, r.n_x, r.n_sems
    wqkv_ref, gains_ref = r.wqkv, r.gains
    p.greet()
    red = Reduce(
        z, p, blocks, r.in_pair, r.in_group, r.half_sum, r.result, r.pair_sems, r.group_sems
    )
    b = Return(z, p, r.part, r.from_core, r.stage_x, r.from_x, r.ret, r.r_send, r.r_recv)

    def part_of(c):
        return pl.ds(pl.multiple_of(c * cols, 16), cols)

    def hid_copy(k):
        return pltpu.make_async_copy(r.hid.at[k], r.hid_in.at[lax.rem(k, 2)], r.hid_sem.at[k])

    def results_first(k):
        hid_copy(k).wait()

        @pl.when(k + 1 < experts)
        def _():
            hid_copy(k + 1).start()

        b.make_room(k)
        for j in range(0, z.width, COL_TILE):
            r.part[b.rows_of(k), j : j + COL_TILE] = dot_nn(
                r.hid_in[lax.rem(k, 2)], r.w_out[:, j : j + COL_TILE]
            ).astype(BF16)
        b.first(k)

        @pl.when(k >= 1)
        def _():
            b.second(k - 1)

    def results_combine(k):
        b.arrive(k)
        who = p.ahead(k)
        pick = slot_onehot(r.rk_row[pl.ds(who, 1), :], z.half, p.c * z.half)
        gate = r.gate_row[pl.ds(who, 1), :]
        for s in range(0, z.half_width, LANES):
            rows = slice(s, s + LANES)
            r.acc[rows, :] += gate * dot_tn(r.ret[k, :, rows], pick)

    def group(n):
        count = (experts + 3) // 4
        return min(n * count, experts), min((n + 1) * count, experts)

    hid_copy(0).start()
    r.wr_pad[...] = jnp.zeros_like(r.wr_pad)
    r.wr_pad[0:experts, :] = r.wr[...].astype(F32)
    router_low = r.wr_pad[...].astype(BF16)
    router = jnp.zeros((LANES, z.width), F32)
    gain_sum = jnp.zeros((1, z.width), F32)
    loads["mid"].wait()
    for i in tiles_of(z.seq):
        rows = slice(i * TILE, (i + 1) * TILE)
        gate = r.gates[rows, :]
        grads = r.gg[rows, :]
        grads = grads + pltpu.roll(grads, LANES - experts, 1)
        dots = jnp.sum(gate * grads, axis=1, keepdims=True)
        logit = (gate * (grads - dots)).astype(BF16)
        router = router + dot_tn(logit, r.nrm[rows, :])
        back = r.nf[rows, :].astype(F32) + dot_nn(logit, router_low)
        mid = midg[rows, :]
        flipped = midg[rows, pl.ds(pl.multiple_of(p.x * z.half_width, LANES), z.half_width)].T
        r.acc[part_of(p.c), rows] = jnp.where(p.c == 0, flipped[0:cols, :], flipped[cols:, :])
        r.acc[part_of(1 - p.c), rows] = jnp.zeros((cols, TILE), F32)
        root = lax.rsqrt(jnp.mean(mid * mid, axis=1, keepdims=True) + epsilon)
        unit = mid * root
        gain_sum = gain_sum + jnp.sum(back * unit, axis=0, keepdims=True)
        u = back * gains_ref[1:2, :]
        mean = jnp.mean(u * unit, axis=1, keepdims=True)
        grad = r.cot[:, rows].astype(F32).T + root * (u - unit * mean)
        midg[rows, :] = grad
        low = grad.astype(BF16)
        nag[rows, :] = low
        dmix[rows, :] = jnp.zeros((TILE, SLOT), BF16)
        dmix[rows, 0:cols] = dot_nt(low, r.wao[...]).astype(BF16)
        loop(*group(i), results_first)
    b.second(experts - 1)
    for j in range(0, z.width, COL_TILE):
        cut = slice(j, j + COL_TILE)
        blocks[3, :, cut] = dot_tn(r.mixed[...], nag[:, cut]).astype(BF16)
    red.first(3)
    rest = jnp.zeros((cols - experts, z.width), F32)
    first_row = lax.broadcasted_iota(jnp.int32, rest.shape, 0) == 0
    blocks[4] = jnp.concatenate(
        [router[0:experts, :], jnp.where(first_row, gain_sum, rest)], axis=0
    ).astype(BF16)
    red.first(4)
    loads["probs"].wait()
    loads["qkv"].wait()
    loads["na"].wait()
    dk[...] = jnp.zeros_like(dk)
    dv[...] = jnp.zeros_like(dv)
    dbias[...] = jnp.zeros_like(dbias)

    def window(i):
        start, width = window_of(i)
        return slice(i * TILE, (i + 1) * TILE), slice(start, start + width), width

    for i in tiles_of(z.seq):
        rows, span, width = window(i)
        for h in range(heads):
            own = mask_head(dmix[rows, :], h, size)
            dv[span, :] += dot_tn(probs[h, rows, 0:width], own)
    red.second(3)
    red.second(4)
    dqkv[:, 2 * SLOT :] = dv[...].astype(BF16)

    def block(b, k):
        for j in range(0, z.width, COL_TILE):
            cut = slice(j, j + COL_TILE)
            full = dot_tn(dqkv[:, k * SLOT : (k + 1) * SLOT], na_ref[:, cut])
            blocks[b, :, cut] = full[0:cols, :].astype(BF16)

    block(2, 2)
    red.first(2)
    loop(*group(0), b.third)
    half = TILE // 2

    def tile_rows(i, c):
        return pl.ds(pl.multiple_of(i * TILE + c * half, 16), half)

    def nag_piece(i, x):
        return nag.at[
            tile_rows(i, p.c), pl.ds(pl.multiple_of(x * z.half_width, LANES), z.half_width)
        ]

    def n_to_core(i):
        return remote(
            part.at[tile_rows(i, 1 - p.c), :], n_core.at[i], n_sems.at[0, 0, i], n_sems.at[1, 0, i],
            (p.e, p.core_peer),
        )

    def n_to_x(i):
        return remote(
            n_sx.at[i], n_x.at[i], n_sems.at[0, 1, i], n_sems.at[1, 1, i], (p.e, p.x_peer)
        )

    def n_share(i, which):
        ref = nag_piece(i, p.x if which < 4 else 1 - p.x)
        peer = p.x_peer if which == 2 else p.core_peer
        return remote(ref, ref, n_sems.at[0, which, i], n_sems.at[1, which, i], (p.e, peer))

    def n_second(i):
        n_to_core(i).wait_recv()
        for x in (1 - p.x, p.x):
            cut = pl.ds(pl.multiple_of(x * z.half_width, LANES), z.half_width)
            both = part[tile_rows(i, p.c), cut].astype(F32) + n_core[i, :, cut].astype(F32)
            if x is p.x:
                nag_piece(i, p.x)[...] = both.astype(BF16)
            else:
                n_sx[i] = both.astype(BF16)
                n_to_x(i).start()

    def n_third(i):
        n_to_x(i).wait_recv()
        mine = nag_piece(i, p.x)
        mine[...] = (mine[...].astype(F32) + n_x[i].astype(F32)).astype(BF16)
        n_share(i, 2).start()
        n_share(i, 3).start()

    def n_fourth(i):
        n_share(i, 2).wait_recv()
        n_share(i, 4).start()

    count = len(tiles_of(z.seq))
    order = list(reversed(tiles_of(z.seq)))
    for step, i in enumerate(order):
        rows, span, width = window(i)
        total = jnp.zeros((TILE, SLOT), F32)
        for h in range(heads):
            own = mask_head(dmix[rows, :], h, size)
            weight = probs[h, rows, 0:width].astype(F32)
            back = dot_nt(own, qkv[span, 2 * SLOT :])
            dots = jnp.sum(weight * back, axis=1, keepdims=True)
            score = weight * (back - dots)
            low = score.astype(BF16)
            dbias[h, :, WINDOW - width : WINDOW] += low.astype(F32)
            total = total + dot_nn(low, mask_head(qkv[span, SLOT : 2 * SLOT], h, size))
            dk[span, :] += dot_tn(low, mask_head(qkv[rows, 0:SLOT], h, size))
        dqkv[rows, 0:SLOT] = (total * size ** (-0.5)).astype(BF16)
        dqkv[rows, SLOT : 2 * SLOT] = dk[rows, :].astype(BF16)
        for j in range(0, z.width, COL_TILE):
            part[rows, j : j + COL_TILE] = sum(
                dot_nn(
                    dqkv[rows, k * SLOT : k * SLOT + cols], wqkv_ref[k, :, j : j + COL_TILE]
                )
                for k in range(3)
            ).astype(BF16)
        n_to_core(i).start()
        if step == 0:
            red.third(3)
            red.third(4)
            red.second(2)
        if step >= 1:
            n_second(order[step - 1])
        if step == 1:
            red.fourth(3)
            red.fourth(4)
            red.third(2)
        if step >= 2:
            n_third(order[step - 2])
        if step == 2:
            red.fourth(2)
        if step >= 3:
            n_fourth(order[step - 3])
        if step < 3:
            loop(*group(step + 1), b.third)
    block(0, 0)
    red.first(0)
    block(1, 1)
    red.first(1)
    n_second(order[count - 1])
    n_third(order[count - 2])
    n_fourth(order[count - 3])
    late[...] = jnp.zeros_like(late)
    lane = lax.broadcasted_iota(jnp.int32, (4 * TILE, LANES), 0)
    distance = distance_of(lane)
    which = lax.broadcasted_iota(jnp.int32, (4 * TILE, LANES), 1)
    hot = jnp.where((bucket_grid(distance) == which) & (distance >= 0), 1.0, 0.0).astype(BF16)
    red.second(0)
    red.second(1)
    sums = [tail_sums(dbias[h]) for h in range(heads)]
    sums = jnp.concatenate(sums + [jnp.zeros((8 - heads, 4 * TILE), F32)], axis=0)
    late[0:8, 0:LANES] = split_dot(sums, hot)
    n_third(order[count - 1])
    n_fourth(order[count - 2])
    red.third(0)
    red.third(1)
    n_fourth(order[count - 1])
    for i in order:
        n_share(i, 3).wait_recv()
        n_share(i, 4).wait_recv()
    loads["x"].wait()

    def grad_copy(i):
        rows = pl.ds(i * TILE, TILE)
        return pltpu.make_async_copy(midg.at[rows, :], r.grad_in.at[rows, :], r.out_sem.at[i])

    def result_copy(n):
        return pltpu.make_async_copy(r.result.at[n], r.blocks_out.at[n], r.res_sem.at[n])

    gain_sum = jnp.zeros((1, z.width), F32)
    for i in tiles_of(z.seq):
        rows = slice(i * TILE, (i + 1) * TILE)
        stream = x_ref[rows, :].astype(F32)
        root = lax.rsqrt(jnp.mean(stream * stream, axis=1, keepdims=True) + epsilon)
        unit = stream * root
        back = nag[rows, :].astype(F32)
        gain_sum = gain_sum + jnp.sum(back * unit, axis=0, keepdims=True)
        w = back * gains_ref[0:1, :]
        mean = jnp.mean(w * unit, axis=1, keepdims=True)
        midg[rows, :] += root * (w - unit * mean)
        grad_copy(i).start()
    for k in range(z.width // SLOT):
        late[8 + k : 9 + k, :] = gain_sum[:, k * SLOT : (k + 1) * SLOT]

    def late_copy(k):
        return remote(
            late, late_in.at[k], s_sems.at[0, 1, k], s_sems.at[1, 1, k], (p.ahead(k), p.t)
        )

    late_in[0] = late[...]
    loop(1, experts, lambda k: late_copy(k).start())
    red.fourth(0)
    red.fourth(1)

    def take_late(source, total):
        k = p.steps_from(source)

        @pl.when(k > 0)
        def _():
            late_copy(k).wait_recv()

        return total + late_in[k]

    loop(0, experts, results_combine)
    r.d_send[...] = r.acc[part_of(1 - p.c), :].astype(BF16)
    d_copy = remote(
        r.d_send, r.d_recv, r.d_sems.at[0], r.d_sems.at[1], (p.e, p.core_peer)
    )
    d_copy.start()
    for n in range(5):
        red.last(n)
        result_copy(n).start()
    r.late_out[...] = lax.fori_loop(0, experts, take_late, jnp.zeros(late.shape, F32))
    d_copy.wait_recv()
    r.act[...] = (r.acc[part_of(p.c), :] + r.d_recv[...].astype(F32)).astype(BF16)
    d_copy.wait_send()
    for n in range(5):
        red.finish(n)
        result_copy(n).wait()
    for i in tiles_of(z.seq):
        grad_copy(i).wait()

    def finish(k):
        b.finish(k)

        @pl.when(k > 0)
        def _():
            late_copy(k).wait_send()

    loop(0, experts, finish)
    for i in order:
        n_to_core(i).wait_send()
        n_to_x(i).wait_send()
        for which in (2, 3, 4):
            n_share(i, which).wait_send()


BACK_LOADS = ("mid", "probs", "qkv", "na", "x")


def run_back(z, kept, inputs, weight_router, gains, wao, wqkv, w_out):
    heads, cols = kept.probs_out.shape[0], wao.shape[0]
    e, seq, width = z.experts, z.seq, z.width
    tiles = seq // TILE
    half = TILE // 2
    dma = pltpu.SemaphoreType.DMA
    args = dict(
        mid=kept.mid_out,
        probs=kept.probs_out,
        qkv=kept.qkv_out,
        na=kept.na_out,
        x=inputs,
        hid=kept.hid_out,
        nf=kept.nf,
        gg=kept.gg,
        gates=kept.gates_out,
        nrm=kept.nrm_out,
        wr=weight_router,
        gains=gains,
        cot=kept.cot_out,
        wao=wao,
        mixed=kept.mixed_out,
        wqkv=wqkv,
        w_out=w_out,
        rk_row=kept.rk_out,
        gate_row=kept.gate_row_out,
    )
    in_hbm = BACK_LOADS + ("hid",)
    outs = dict(
        grad_in=((seq, width), F32),
        blocks_out=((5, cols, width), BF16),
        late_out=((16, SLOT), F32),
        act=((cols, seq), BF16),
    )
    scratch = {name + "_in": pltpu.VMEM(args[name].shape, args[name].dtype) for name in BACK_LOADS}
    scratch.update(
        zip(
            ("part", "from_core", "stage_x", "from_x", "ret", "r_send", "r_recv"),
            return_scratch(z, min(e, 8)),
            strict=True,
        )
    )
    scratch.update(
        zip(
            ("blocks", "in_pair", "in_group", "half_sum", "result", "pair_sems", "group_sems"),
            reduce_scratch(z, 5, cols),
            strict=True,
        )
    )
    shapes = dict(
        hid_in=((2,) + kept.hid_out.shape[1:], BF16),
        acc=((z.half_width, seq), F32),
        d_send=((cols, seq), BF16),
        d_recv=((cols, seq), BF16),
        wr_pad=((LANES, width), F32),
        dmix=((seq, SLOT), BF16),
        dk=((seq, SLOT), F32),
        dv=((seq, SLOT), F32),
        dbias=((heads, TILE, 4 * TILE), F32),
        dqkv=((seq, 3 * SLOT), BF16),
        part_sum=((seq, width), BF16),
        late=((16, SLOT), F32),
        late_in=((e, 16, SLOT), F32),
        n_core=((tiles, half, width), BF16),
        n_sx=((tiles, half, z.half_width), BF16),
        n_x=((tiles, half, z.half_width), BF16),
        nag=((seq, width), BF16),
    )
    for name, (shape, dtype) in shapes.items():
        scratch[name] = pltpu.VMEM(shape, dtype)
    scratch.update(
        dict(
            load_sem=dma((len(BACK_LOADS),)),
            hid_sem=dma((e,)),
            d_sems=dma((2,)),
            s_sems=dma((2, 2, e)),
            n_sems=dma((2, 5, tiles)),
            out_sem=dma((tiles,)),
            res_sem=dma((5,)),
        )
    )
    names = list(args) + list(outs) + list(scratch)
    results = pl.pallas_call(
        functools.partial(back_kernel, z, heads, names),
        out_shape=tuple(jax.ShapeDtypeStruct(*outs[n]) for n in outs),
        in_specs=[ANY_SPEC if n in in_hbm else VMEM_SPEC for n in args],
        out_specs=(ANY_SPEC, ANY_SPEC, VMEM_SPEC, VMEM_SPEC),
        scratch_shapes=list(scratch.values()),
        compiler_params=pltpu.CompilerParams(
            collective_id=4, has_side_effects=True, vmem_limit_bytes=VMEM_LIMIT
        ),
        name="run_back",
    )(*args.values())
    return Names(list(outs), results)


PIECES = 4


def finish_kernel(
    experts, heads, blocks, late, grad_in, gw_in, gw_out,
    grad_out, gw_in_out, gw_out_out, qkv, wao, router, gain_attn, gain_ffn, table,
    grad_held, gw_in_held, gw_out_held, sems,
):
    pieces = []
    for n, (src, dst, held) in enumerate(
        (
            (grad_in, grad_out, grad_held),
            (gw_in, gw_in_out, gw_in_held),
            (gw_out, gw_out_out, gw_out_held),
        )
    ):
        count = src.shape[0] // PIECES
        for m in range(PIECES):
            rows = pl.ds(m * count, count)
            load = pltpu.make_async_copy(src.at[rows, :], held.at[rows, :], sems.at[0, n, m])
            store = pltpu.make_async_copy(held.at[rows, :], dst.at[rows, :], sems.at[1, n, m])
            pieces.append((load, store))
    for load, _ in pieces:
        load.start()
    for load, store in pieces:
        load.wait()
        store.start()
    qkv[...] = blocks[0:3].astype(F32)
    wao[...] = blocks[3].astype(F32)
    small = blocks[4].astype(F32)
    router[...] = small[0:experts, :]
    gain_ffn[...] = small[experts : experts + 1, :]
    table[...] = late[0:heads, 0:BUCKETS]
    for k in range(gain_attn.shape[1] // SLOT):
        gain_attn[:, k * SLOT : (k + 1) * SLOT] = late[8 + k : 9 + k, :]
    for _, store in pieces:
        store.wait()


def run_finish(z, heads, blocks, late, grad_in, gw_in, gw_out):
    cols, width = blocks.shape[1:]
    shapes = (
        grad_in.shape, gw_in.shape, gw_out.shape, (3, cols, width), (cols, width),
        (z.experts, width), (1, width), (1, width), (heads, BUCKETS),
    )
    return pl.pallas_call(
        functools.partial(finish_kernel, z.experts, heads),
        out_shape=tuple(jax.ShapeDtypeStruct(shape, F32) for shape in shapes),
        in_specs=[VMEM_SPEC] * 2 + [ANY_SPEC] * 3,
        out_specs=(ANY_SPEC,) * 3 + (VMEM_SPEC,) * 6,
        scratch_shapes=[pltpu.VMEM(shape, F32) for shape in shapes[:3]]
        + [pltpu.SemaphoreType.DMA((2, 3, PIECES))],
        compiler_params=pltpu.CompilerParams(vmem_limit_bytes=VMEM_LIMIT),
        name="run_finish",
    )(blocks, late, grad_in, gw_in, gw_out)


def per_device(
    inputs,
    gain_attn,
    gain_ffn,
    weight_qkv,
    weight_attn_out,
    rel_table,
    weight_router,
    weight_in,
    weight_out,
    routes,
    segments,
    cotangent,
):
    seq_len, width = inputs.shape
    heads = rel_table.shape[1]
    experts = weight_router.shape[1]
    z = Sizes(experts, seq_len, routes.shape[1], width)
    gains = jnp.stack([gain_attn, gain_ffn])
    wqkv = jnp.transpose(weight_qkv, (0, 2, 1))
    wr = weight_router.T
    kept = run_layer(
        z, inputs, gains, wqkv, weight_attn_out, rel_table.T, wr, weight_in[0], weight_out[0],
        routes.T, segments, cotangent.T,
    )
    grads = run_back(
        z, kept, inputs, wr, gains, weight_attn_out, wqkv, weight_out[0]
    )
    grad_input, gw_in, gw_out, gw_qkv, gw_attn_out, router, gain_a, gain_f, table = run_finish(
        z, heads, grads.blocks_out, grads.late_out, grads.grad_in, kept.gw_in_out,
        kept.gw_out_out,
    )
    return (
        grads.act.T,
        grad_input,
        gain_a.reshape(width),
        gain_f.reshape(width),
        jnp.transpose(gw_qkv, (0, 2, 1)),
        gw_attn_out,
        table.T,
        router.T,
        gw_in[None],
        gw_out[None],
    )


def solution(mesh):
    in_specs = (
        P("expert", None),
        P(),
        P(),
        P(None, None, "tensor"),
        P("tensor", None),
        P(None, "tensor"),
        P(),
        P("expert", None, "tensor"),
        P("expert", "tensor", None),
        P("expert", None),
        P("expert"),
        P("expert", "tensor"),
    )
    out_specs = (
        P("expert", "tensor"),
        P("expert", None),
        P(),
        P(),
        P(None, None, "tensor"),
        P("tensor", None),
        P(None, "tensor"),
        P(),
        P("expert", None, "tensor"),
        P("expert", "tensor", None),
    )
    return jax.shard_map(
        per_device, mesh=mesh, in_specs=in_specs, out_specs=out_specs, check_vma=False
    )
```

```python
import functools
import math

import jax
import jax.numpy as jnp
from jax import lax
from jax.experimental import pallas as pl
from jax.experimental.pallas import tpu as pltpu
from jax.sharding import PartitionSpec as P

BUCKETS = 32
epsilon = 1e-06
negative = -1e30
F32 = jnp.float32
BF16 = jnp.bfloat16
MESH = pl.DeviceIdType.MESH
VMEM_SPEC = pl.BlockSpec(memory_space=pltpu.VMEM)
ANY_SPEC = pl.BlockSpec(memory_space=pl.ANY)
LANES = 128
ROW_TILE = 256
COL_TILE = 256
VMEM_LIMIT = 60 * 2**20


def dot_nn(left, right):
    return lax.dot_general(left, right, (((1,), (0,)), ((), ())), preferred_element_type=F32)


def dot_nt(left, right):
    return lax.dot_general(left, right, (((1,), (1,)), ((), ())), preferred_element_type=F32)


def dot_tn(left, right):
    return lax.dot_general(left, right, (((0,), (0,)), ((), ())), preferred_element_type=F32)


def round_up(value, step):
    return (value + step - 1) // step * step


class Sizes:
    def __init__(self, experts, seq_len, top_count, width):
        self.experts = experts
        self.seq = seq_len
        self.width = width
        self.half_width = width // 2
        capacity = (4 * seq_len * top_count + 24 * experts - 1) // (24 * experts) * 8
        self.slots = round_up(capacity, 32)
        self.half = self.slots // 2
        self.slot_lanes = round_up(self.slots, LANES)


class Place:
    def __init__(self, sizes):
        self.count = sizes.experts
        self.e = lax.axis_index("expert")
        self.t = lax.axis_index("tensor")
        self.c = lax.rem(self.t, 2)
        self.x = lax.div(self.t, 2)
        self.core_peer = self.t + 1 - 2 * self.c
        self.x_peer = lax.rem(self.t + 2, 4)

    def shifted(self, k, sign):
        group = self.count // 2
        parity = lax.rem(self.e, 2)
        flip = lax.rem(k, 2)
        turn = lax.div(k, 2)
        member = lax.rem(lax.div(self.e, 2) + group + sign * turn, group)
        return 2 * member + parity + flip - 2 * parity * flip

    def ahead(self, k):
        return self.shifted(k, 1)

    def behind(self, k):
        return self.shifted(k, -1)

    def steps_from(self, other):
        group = self.count // 2
        turn = lax.rem(lax.div(self.e, 2) + group - lax.div(other, 2), group)
        return 2 * turn + lax.rem(self.e + other, 2)

    def greet(self, expert_peers=True, all_tensor=True):
        barrier = pltpu.get_barrier_semaphore()
        count = 0
        if expert_peers:

            def one(k, carry):
                pl.semaphore_signal(
                    barrier, inc=1, device_id=(self.ahead(k), self.t), device_id_type=MESH
                )
                return carry

            lax.fori_loop(1, self.count, one, 0)
            count += self.count - 1
        for d in range(1, 4):
            pl.semaphore_signal(
                barrier,
                inc=1,
                device_id=(self.e, lax.rem(self.t + d, 4)),
                device_id_type=MESH,
            )
        count += 3
        pl.semaphore_wait(barrier, count)


def remote(src, dst, send_sem, recv_sem, device):
    return pltpu.make_async_remote_copy(
        src_ref=src,
        dst_ref=dst,
        send_sem=send_sem,
        recv_sem=recv_sem,
        device_id=device,
        device_id_type=MESH,
    )


class Gather:
    sem_kinds = 4

    def __init__(self, sizes, place, stage, buf, send, recv):
        self.z, self.p = sizes, place
        self.stage, self.buf, self.send, self.recv = stage, buf, send, recv

    def quarter(self, k, c, x):
        h, w = self.z.half, self.z.half_width
        return self.buf.at[
            k, pl.ds(pl.multiple_of(c * h, 16), h), pl.ds(pl.multiple_of(x * w, LANES), w)
        ]

    def out(self, k):
        p = self.p
        return remote(
            self.stage.at[k],
            self.quarter(k, p.c, p.x),
            self.send.at[0, k],
            self.recv.at[0, k],
            (p.ahead(k), p.t),
        )

    def to_core(self, k):
        p = self.p
        ref = self.quarter(k, p.c, p.x)
        return remote(ref, ref, self.send.at[1, k], self.recv.at[1, k], (p.e, p.core_peer))

    def to_x(self, k):
        p = self.p
        ref = self.quarter(k, p.c, p.x)
        return remote(ref, ref, self.send.at[2, k], self.recv.at[2, k], (p.e, p.x_peer))

    def on_to_core(self, k):
        p = self.p
        ref = self.quarter(k, p.c, 1 - p.x)
        return remote(ref, ref, self.send.at[3, k], self.recv.at[3, k], (p.e, p.core_peer))

    def pack_own(self, rk_row, rows_ref):
        z, p = self.z, self.p
        pick = slot_onehot(rk_row[pl.ds(p.e, 1), :], z.slots, 0)
        for j in range(0, z.width, COL_TILE):
            self.buf[0, :, j : j + COL_TILE] = dot_nn(
                pick, rows_ref[:, j : j + COL_TILE]
            ).astype(BF16)

    def pack(self, k, pick, rows_ref):
        z, p = self.z, self.p
        cols = rows_ref[:, pl.ds(pl.multiple_of(p.x * z.half_width, LANES), z.half_width)]
        self.stage[k] = dot_nn(pick, cols).astype(BF16)

    def first(self, k):
        self.out(k).wait_recv()
        self.to_core(k).start()
        self.to_x(k).start()

    def out_wide(self, stage):
        z, p = self.z, self.p
        return remote(
            stage,
            self.buf.at[1, pl.ds(pl.multiple_of(p.c * z.half, 16), z.half), :],
            self.send.at[0, 1],
            self.recv.at[0, 1],
            (p.ahead(1), p.t),
        )

    def first_wide(self, stage):
        self.out_wide(stage).wait_recv()
        self.to_core(1).start()
        self.on_to_core(1).start()

    def second(self, k):
        self.to_x(k).wait_recv()
        self.on_to_core(k).start()

    def last(self, k):
        self.to_core(k).wait_recv()
        self.on_to_core(k).wait_recv()

    def finish(self, k):
        self.out(k).wait_send()
        self.to_core(k).wait_send()
        self.to_x(k).wait_send()
        self.on_to_core(k).wait_send()


class Return:
    sem_kinds = 3

    def __init__(self, sizes, place, part, from_core, stage_x, from_x, ret, send, recv):
        self.z, self.p = sizes, place
        self.part, self.from_core, self.stage_x = part, from_core, stage_x
        self.from_x, self.ret = from_x, ret
        self.send, self.recv = send, recv
        self.ring = part.shape[0] // sizes.slots

    def rows_of(self, k):
        return pl.ds(
            pl.multiple_of(lax.rem(k, self.ring) * self.z.slots, 16), self.z.slots
        )

    def make_room(self, k):
        @pl.when(k >= self.ring)
        def _():
            self.to_core(k - self.ring).wait_send()

    def part_rows(self, k, c):
        start = lax.rem(k, self.ring) * self.z.slots + c * self.z.half
        return pl.ds(pl.multiple_of(start, 16), self.z.half)

    def cols(self, x):
        return pl.ds(pl.multiple_of(x * self.z.half_width, LANES), self.z.half_width)

    def to_core(self, k):
        p = self.p
        return remote(
            self.part.at[self.part_rows(k, 1 - p.c), :],
            self.from_core.at[k],
            self.send.at[0, k],
            self.recv.at[0, k],
            (p.e, p.core_peer),
        )

    def to_x(self, k):
        p = self.p
        return remote(
            self.stage_x.at[k],
            self.from_x.at[k],
            self.send.at[1, k],
            self.recv.at[1, k],
            (p.e, p.x_peer),
        )

    def home(self, k):
        p = self.p
        return remote(
            self.from_core.at[k, :, self.cols(p.x)],
            self.ret.at[k],
            self.send.at[2, k],
            self.recv.at[2, k],
            (p.behind(k), p.t),
        )

    def first(self, k):
        self.to_core(k).start()

    def second(self, k):
        p = self.p
        self.to_core(k).wait_recv()
        rows = self.part_rows(k, p.c)
        for x in (1 - p.x, p.x):
            cols = self.cols(x)
            both = self.part[rows, cols].astype(F32) + self.from_core[k, :, cols].astype(F32)
            if x is p.x:
                self.from_core[k, :, cols] = both.astype(BF16)
            else:
                self.stage_x[k] = both.astype(BF16)
                self.to_x(k).start()

    def third(self, k):
        self.to_x(k).wait_recv()
        cols = self.cols(self.p.x)
        total = self.from_core[k, :, cols].astype(F32) + self.from_x[k].astype(F32)

        @pl.when(k == 0)
        def _():
            self.ret[0] = total.astype(BF16)

        @pl.when(k > 0)
        def _():
            self.from_core[k, :, cols] = total.astype(BF16)
            self.home(k).start()

    def arrive(self, k):
        @pl.when(k > 0)
        def _():
            self.home(k).wait_recv()

    def finish(self, k):
        @pl.when(k + self.ring >= self.z.experts)
        def _():
            self.to_core(k).wait_send()

        self.to_x(k).wait_send()

        @pl.when(k > 0)
        def _():
            self.home(k).wait_send()


def return_scratch(z, ring):
    e, h, w = z.experts, z.half, z.half_width
    return [
        pltpu.VMEM((ring * z.slots, z.width), BF16),
        pltpu.VMEM((e, h, z.width), BF16),
        pltpu.VMEM((e, h, w), BF16),
        pltpu.VMEM((e, h, w), BF16),
        pltpu.VMEM((e, h, w), BF16),
        pltpu.SemaphoreType.DMA((Return.sem_kinds, e)),
        pltpu.SemaphoreType.DMA((Return.sem_kinds, e)),
    ]


def gather_scratch(z):
    e, h, w = z.experts, z.half, z.half_width
    return [
        pltpu.VMEM((e, h, w), BF16),
        pltpu.VMEM((e, z.slots, z.width), BF16),
        pltpu.SemaphoreType.DMA((Gather.sem_kinds, e)),
        pltpu.SemaphoreType.DMA((Gather.sem_kinds, e)),
    ]


def slot_onehot(rank_row, count, offset):
    slot = lax.broadcasted_iota(jnp.int32, (count, rank_row.shape[1]), 0).astype(F32)
    shift = lax.convert_element_type(offset, F32)
    return jnp.where(rank_row - shift == slot, 1.0, 0.0).astype(BF16)


def pick_lane(values, lane):
    lanes = lax.broadcasted_iota(jnp.int32, values.shape, 1)
    return jnp.sum(jnp.where(lanes == lane, values, 0.0), axis=1, keepdims=True)


def row_to_col(row, count, offset):
    rows = lax.broadcasted_iota(jnp.int32, (count, row.shape[1]), 0) + offset
    lanes = lax.broadcasted_iota(jnp.int32, (count, row.shape[1]), 1)
    return jnp.sum(jnp.where(rows == lanes, row, 0.0), axis=1, keepdims=True)


def col_to_row(col, lane_count):
    rows = lax.broadcasted_iota(jnp.int32, (col.shape[0], lane_count), 0)
    lanes = lax.broadcasted_iota(jnp.int32, (col.shape[0], lane_count), 1)
    return jnp.sum(jnp.where(rows == lanes, col, 0.0), axis=0, keepdims=True)


def loop(start, stop, body):
    def step(i, carry):
        body(i)
        return carry

    lax.fori_loop(start, stop, step, 0)


def fill_ranks(routes_ref, rk_col, rk_row):
    seq = routes_ref.shape[1]
    ids = lax.broadcasted_iota(jnp.int32, (LANES, seq), 0)
    hot = (routes_ref[0:1, :] == ids) | (routes_ref[1:2, :] == ids)
    hot_mark = jnp.where(hot, 1.0, 0.0)
    hot_low = hot_mark.astype(BF16)
    for s in range(0, seq, ROW_TILE):
        rows = lax.broadcasted_iota(jnp.int32, (seq, ROW_TILE), 0)
        cols = lax.broadcasted_iota(jnp.int32, (seq, ROW_TILE), 1) + s
        before = jnp.where(rows < cols, 1.0, 0.0).astype(BF16)
        rank = dot_nn(hot_low, before)
        rank = jnp.where(hot_mark[:, s : s + ROW_TILE] > 0.5, rank, -1.0)
        rk_row[:, s : s + ROW_TILE] = rank
        rk_col[s : s + ROW_TILE, :] = rank.T


def gelu_pair(h):
    scale = 0.7978845608028654
    square = h * h
    t = jnp.tanh(scale * h * (1.0 + 0.044715 * square))
    half = 0.5 + 0.5 * t
    slope = half + (0.5 * scale) * h * (1.0 - t * t) * (1.0 + 0.134145 * square)
    return h * half, slope


def far_limits(buckets):
    half_size = buckets // 2
    base_ratio = 256.0 / buckets
    return [
        int(math.ceil(half_size * base_ratio ** (step / half_size))) for step in range(1, half_size)
    ]


TILE = 256
WINDOW = 3 * TILE
SLOT = 256


def distance_of(lane):
    return jnp.where(lane < WINDOW, 2 * TILE - lane, 2 * TILE + 4 * TILE - lane)


def bucket_grid(distance):
    half_size = BUCKETS // 2
    far = jnp.full(distance.shape, half_size, jnp.int32)
    for limit in far_limits(BUCKETS):
        far = far + jnp.where(distance >= limit, 1, 0)
    return jnp.where(distance < half_size, distance, far)


def fill_bias(table_ref, bias, heads):
    lane = lax.broadcasted_iota(jnp.int32, (1, 4 * TILE), 1)
    distance = distance_of(lane)
    bucket = bucket_grid(distance)
    for h in range(heads):
        values = jnp.full((1, 4 * TILE), negative, F32)
        for b in range(BUCKETS):
            values = jnp.where(bucket == b, table_ref[h, b], values)
        wide = jnp.broadcast_to(values, (TILE, 4 * TILE))
        rolled = pltpu.roll(wide, 0, 1, stride=1, stride_axis=0)
        bias[h] = rolled[:, 0:WINDOW]


def head_lanes(rows, h, size):
    lanes = lax.broadcasted_iota(jnp.int32, (rows, SLOT), 1)
    return (lanes >= h * size) & (lanes < (h + 1) * size)


def mask_head(values, h, size):
    keep = head_lanes(values.shape[0], h, size)
    return jnp.where(keep, values, jnp.zeros_like(values))


def tiles_of(seq):
    return range(seq // TILE)


def window_of(i):
    start = max(0, i - 2) * TILE
    return start, (i + 1) * TILE - start


def attention_tile(i, h, size, qkv, seg_col, seg_row, bias):
    start, width = window_of(i)
    query = mask_head(qkv[i * TILE : (i + 1) * TILE, 0:SLOT], h, size)
    keys = qkv[start : start + width, SLOT : 2 * SLOT]
    scores = dot_nt(query, keys) + bias[h, :, WINDOW - width :]
    same = seg_col[i * TILE : (i + 1) * TILE, 0:1] == seg_row[:, start : start + width].astype(F32)
    scores = jnp.where(same, scores, negative)
    power = jnp.exp(scores - jnp.max(scores, axis=1, keepdims=True))
    probs = power * (1.0 / jnp.sum(power, axis=1, keepdims=True))
    return probs.astype(BF16)


def layer_kernel(z, heads, names, *refs):
    r = Names(names, refs)
    p = Place(z)
    experts = z.experts
    cols = r.cot.shape[0]
    size = cols // heads
    tiles = list(tiles_of(z.seq))
    count = len(tiles)
    p.greet()
    saves = []
    save_ids = iter(range(16))

    def save(src, dst):
        copy = pltpu.make_async_copy(src, dst, r.save_sem.at[next(save_ids)])
        copy.start()
        saves.append(copy)

    cot_rows = lambda t: r.cot_all.at[pl.ds(pl.multiple_of(t * cols, 16), cols), :]
    wao_rows = lambda t: r.wao_all.at[pl.ds(pl.multiple_of(t * cols, 16), cols), :]

    def spread(rows, n):
        def copy(t, m, peer):
            return remote(
                rows(t), rows(t), r.c_sems.at[0, n, m], r.c_sems.at[1, n, m], (p.e, peer)
            )

        return (
            copy(p.t, 0, p.core_peer), copy(p.t, 1, p.x_peer), copy(p.x_peer, 2, p.core_peer)
        )

    cot_rows(p.t)[...] = r.cot[...]
    cot_copies = spread(cot_rows, 0)
    cot_copies[0].start()
    wao_rows(p.t)[...] = r.wao[...]
    wao_copies = spread(wao_rows, 1)
    wao_copies[1].start()
    wao_copies[0].start()
    cot_copies[1].start()
    fill_ranks(r.routes, r.rk_col, r.rk_row)
    save(r.rk_row, r.rk_out)
    og = Gather(z, p, r.stage, r.og_buf, r.og_send, r.og_recv)
    g = Gather(z, p, r.stage, r.buf, r.g_send, r.g_recv)
    b = Return(
        z, p, r.part, r.from_core, r.stage_x, r.from_x, r.ret, r.r_send, r.r_recv
    )

    def in_chip(own, peer):
        return jnp.where(
            p.c == 0,
            jnp.concatenate([own, peer], axis=1),
            jnp.concatenate([peer, own], axis=1),
        )

    cot_copies[0].wait_recv()

    def half_pick(k):
        return slot_onehot(r.rk_row[pl.ds(p.ahead(k), 1), :], z.half, p.c * z.half)

    def pack_og(k):
        own = r.cot_all[pl.ds(pl.multiple_of(p.x * z.half_width, 16), z.half_width), :]
        rows = dot_nt(half_pick(k), own).astype(BF16)

        @pl.when(k > 0)
        def _():
            r.stage[k] = rows
            og.out(k).start()

        @pl.when(k == 0)
        def _():
            og.quarter(0, p.c, p.x)[...] = rows
            og.to_core(0).start()
            og.to_x(0).start()

    loop(1, experts, pack_og)
    pack_og(0)
    wide_row = jnp.broadcast_to(r.seg_row[...].astype(F32), (LANES, z.seq))
    r.qkv[...] = jnp.zeros_like(r.qkv)
    for i in tiles:
        rows = slice(i * TILE, (i + 1) * TILE)
        r.seg_col[rows, :] = wide_row[:, rows].T
        stream = r.x[rows, :].astype(F32)
        root = lax.rsqrt(jnp.mean(stream * stream, axis=1, keepdims=True) + epsilon)
        normed = (stream * root * r.gains[0:1, :]).astype(BF16)
        r.na[rows, :] = normed
        for k in range(3):
            cut = slice(k * SLOT, k * SLOT + cols)
            out = dot_nt(normed, r.wqkv[k]).astype(BF16)
            if k == 0:
                out = (out.astype(F32) * size ** (-0.5)).astype(BF16)
            r.qkv[rows, cut] = out
    na_saved = len(saves)
    save(r.na, r.na_out)
    save(r.qkv, r.qkv_out)
    fill_bias(r.table, r.bias, heads)

    def probs_rows(i, h):
        return pl.ds((i % 2 * heads + h) * TILE, TILE)

    def save_probs(i, h):
        _, width = window_of(i)
        return pltpu.make_async_copy(
            r.part.at[probs_rows(i, h), pl.ds(0, width)],
            r.probs_out.at[h, pl.ds(i * TILE, TILE), pl.ds(0, width)],
            r.p_sem.at[i, h],
        )

    def mixed_core(i):
        rows = pl.ds(i * TILE, TILE)
        return remote(
            r.mixed.at[rows, :], r.mixed_in.at[rows, :], r.m_sems.at[0, 0, i],
            r.m_sems.at[1, 0, i], (p.e, p.core_peer),
        )

    def mixed_piece(i, x):
        half = TILE // 2
        return r.mc.at[
            pl.ds(pl.multiple_of(i * TILE + p.c * half, 16), half),
            pl.ds(pl.multiple_of(x * z.half_width, LANES), z.half_width),
        ]

    def mixed_x(i):
        ref = mixed_piece(i, p.x)
        return remote(ref, ref, r.m_sems.at[0, 1, i], r.m_sems.at[1, 1, i], (p.e, p.x_peer))

    def mixed_on(i):
        ref = mixed_piece(i, 1 - p.x)
        return remote(ref, ref, r.m_sems.at[0, 2, i], r.m_sems.at[1, 2, i], (p.e, p.core_peer))

    def attend(i):
        rows = slice(i * TILE, (i + 1) * TILE)
        start, width = window_of(i)
        total = jnp.zeros((TILE, SLOT), F32)
        for h in range(heads):
            if i >= 2:
                save_probs(i - 2, h).wait()
            low = attention_tile(i, h, size, r.qkv, r.seg_col, r.seg_row, r.bias)
            r.part[probs_rows(i, h), 0:width] = low
            save_probs(i, h).start()
            values = mask_head(r.qkv[start : start + width, 2 * SLOT :], h, size)
            total = total + dot_nn(low, values)
        r.mixed[rows, :] = total[:, 0:cols].astype(BF16)
        mixed_core(i).start()

    def share(i):
        mixed_core(i).wait_recv()
        rows = slice(i * TILE, (i + 1) * TILE)
        both = in_chip(r.mixed[rows, :], r.mixed_in[rows, :])
        r.mc[rows, pl.ds(pl.multiple_of(p.x * z.half_width, LANES), z.half_width)] = both
        mixed_x(i).start()

    for i in tiles:
        attend(i)
        if i >= 1:
            share(i - 1)
        if i >= 2:
            mixed_x(i - 2).wait_recv()
            mixed_on(i - 2).start()
        if i == 0:
            wao_copies[1].wait_recv()
            wao_copies[2].start()
        if i == 2:
            cot_copies[1].wait_recv()
            cot_copies[2].start()
    share(count - 1)
    save(r.mixed, r.mixed_out)
    saves.pop(na_saved).wait()
    r.wr_pad[...] = jnp.zeros_like(r.wr_pad)
    r.wr_pad[0:experts, :] = r.wr[...].astype(F32)
    router = r.wr_pad[...].astype(BF16)
    for copy in (wao_copies[0], wao_copies[2], cot_copies[2]):
        copy.wait_recv()

    def project(i):
        rows = slice(i * TILE, (i + 1) * TILE)
        mid = r.x[rows, :].astype(F32) + dot_nn(r.mc[rows, :], r.wao_all[...])
        r.mid[rows, :] = mid
        root = lax.rsqrt(jnp.mean(mid * mid, axis=1, keepdims=True) + epsilon)
        nrm = (mid * root * r.gains[1:2, :]).astype(BF16)
        r.na[rows, :] = nrm
        logits = dot_nt(nrm, router)
        hot = r.rk_col[rows, :] > -0.5
        logits = jnp.where(hot, logits, negative)
        peak = jnp.max(logits, axis=1, keepdims=True)
        power = jnp.where(hot, jnp.exp(logits - peak), 0.0)
        gates = power / jnp.sum(power, axis=1, keepdims=True)
        r.gates[rows, :] = gates
        r.gate_row[:, rows] = gates.T

    for i in tiles:
        if i + 2 >= count:
            mixed_x(i).wait_recv()
            mixed_on(i).start()
        if i == 2:
            og.second(0)
        mixed_on(i).wait_recv()
        project(i)
    for k in range(1, EARLY):
        og.first(k)
    mid_saved = len(saves)
    save(r.mid, r.mid_out)
    save(r.na, r.nrm_out)
    save(r.gates, r.gates_out)
    save(r.gate_row, r.gate_row_out)
    save(r.cot_all, r.cot_out)

    def gate_copy(k):
        return remote(
            r.gs_out.at[k], r.gs_in.at[k], r.gs_sems.at[0, k], r.gs_sems.at[1, k],
            (p.ahead(k), p.t),
        )

    def slot_gates(k):
        pick = slot_onehot(r.rk_row[pl.ds(p.ahead(k), 1), :], z.slot_lanes, 0)
        row = r.gate_row[pl.ds(p.ahead(k), 1), :]
        high = row.astype(BF16).astype(F32)
        low = row - high
        which = lax.broadcasted_iota(jnp.int32, (16, z.seq), 0)
        both = jnp.where(which == 0, high, jnp.where(which == 1, low, 0.0)).astype(BF16)
        sums = dot_nt(both, pick)
        return sums[0:1, :] + sums[1:2, :]

    for i in tiles[-2:]:
        for h in range(heads):
            save_probs(i, h).wait()

    def pack(k):
        og.out(k).wait_send()
        g.pack(k, half_pick(k), r.na)
        g.out(k).start()

    og.out(1).wait_send()
    wide = half_pick(1)
    for j in range(0, z.width, COL_TILE):
        r.stage_wide[:, j : j + COL_TILE] = dot_nn(wide, r.na[:, j : j + COL_TILE]).astype(BF16)
    g.out_wide(r.stage_wide).start()
    loop(2, experts, pack)

    def send_gates(k):
        r.gs_out[k] = slot_gates(k)
        gate_copy(k).start()

    loop(1, experts, send_gates)
    r.gs_in[0] = slot_gates(0)
    g.pack_own(r.rk_row, r.na)

    def gg_copy(k, d):
        return remote(
            r.gg_send.at[k],
            r.gg_recv.at[k, p.t],
            r.gg_sems.at[0, k, d],
            r.gg_sems.at[1, k, d],
            (p.behind(k), lax.rem(p.t + d, 4)),
        )

    def save_hid(k):
        return pltpu.make_async_copy(r.hid.at[lax.rem(k, 2)], r.hid_out.at[k], r.hid_sem.at[k])

    def expert(k):
        ring = lax.rem(k, 2)

        @pl.when(k > 0)
        def _():
            gate_copy(k).wait_recv()
            g.last(k)

        @pl.when(k > 1)
        def _():
            save_hid(k - 2).wait()

        og.last(k)
        gate = row_to_col(r.gs_in[k], z.slots, 0)
        sums = jnp.zeros((z.slots, 1), F32)
        for j in range(0, r.w_in.shape[1], COL_TILE):
            cut = slice(j, j + COL_TILE)
            up, slope = gelu_pair(dot_nn(r.buf[k], r.w_in[:, cut]))
            back = dot_nt(r.og_buf[k], r.w_out[cut, :])
            r.hid[ring, :, cut] = up.astype(BF16)
            r.pre[ring, :, cut] = (gate * back * slope).astype(BF16)
            sums = sums + jnp.sum(up * back, axis=1, keepdims=True)
        for j in range(0, z.width, COL_TILE):
            r.part[b.rows_of(k), j : j + COL_TILE] = dot_nt(
                r.pre[ring], r.w_in[j : j + COL_TILE, :]
            ).astype(BF16)
        b.first(k)
        r.gg_send[k] = col_to_row(sums, z.slot_lanes)
        for d in range(1, 4):
            gg_copy(k, d).start()

        @pl.when(k > 0)
        def _():
            gg_copy(k, 0).start()

        @pl.when(k == 0)
        def _():
            r.gg_recv[0, p.t] = r.gg_send[0]

        save_hid(k).start()

    def weight_grads(k):
        ring = lax.rem(k, 2)
        gate = row_to_col(r.gs_in[k], z.slots, 0)
        r.gated[...] = (gate * r.og_buf[k].astype(F32)).astype(BF16)
        for j in range(0, z.width, COL_TILE):
            cut = slice(j, j + COL_TILE)
            r.gw_in[cut, :] += dot_tn(r.buf[k, :, cut], r.pre[ring])
            r.gw_out[cut, :] += dot_tn(r.hid[ring, :, cut], r.gated[...])

    r.gw_in[...] = jnp.zeros_like(r.gw_in)
    r.gw_out[...] = jnp.zeros_like(r.gw_out)

    def body(i):
        @pl.when(i + EARLY < experts)
        def _():
            og.first(i + EARLY)

        @pl.when(i + 1 < experts)
        def _():
            og.second(i + 1)

        @pl.when(i < experts)
        def _():
            expert(i)

        @pl.when(i == 0)
        def _():
            g.first_wide(r.stage_wide)

        @pl.when(i + 2 < experts)
        def _():
            g.first(i + 2)

        @pl.when((i >= 1) & (i + 1 < experts))
        def _():
            g.second(i + 1)

        @pl.when((i >= 1) & (i <= experts))
        def _():
            b.second(i - 1)

        @pl.when(i >= 2)
        def _():
            b.third(i - 2)

        @pl.when((i >= 1) & (i <= experts))
        def _():
            weight_grads(i - 1)

    loop(0, experts + 2, body)
    save(r.gw_in, r.gw_in_out)
    save(r.gw_out, r.gw_out_out)
    saves.pop(mid_saved).wait()
    acc = r.mid.at[:, pl.ds(0, z.half_width + LANES)]
    acc[...] = jnp.zeros(acc.shape, F32)

    def combine(k):
        b.arrive(k)
        for d in range(1, 4):
            gg_copy(k, d).wait_recv()

        @pl.when(k > 0)
        def _():
            gg_copy(k, 0).wait_recv()

        row = r.gg_recv[k, 0] + r.gg_recv[k, 1] + r.gg_recv[k, 2] + r.gg_recv[k, 3]
        col = row_to_col(row, z.half, p.c * z.half)
        high = col.astype(BF16).astype(F32)
        lanes = lax.broadcasted_iota(jnp.int32, (z.half, LANES), 1)
        who = p.ahead(k)
        r.retx[:, 0 : z.half_width] = r.ret[k]
        r.retx[:, z.half_width :] = jnp.where(
            lanes == who, high, jnp.where(lanes == who + experts, col - high, 0.0)
        ).astype(BF16)
        for s in range(0, z.seq, ROW_TILE):
            rows = slice(s, s + ROW_TILE)
            rank = pick_lane(r.rk_col[rows, :], who) - lax.convert_element_type(p.c * z.half, F32)
            slot = lax.broadcasted_iota(jnp.int32, (ROW_TILE, z.half), 1).astype(F32)
            pick = jnp.where(rank == slot, 1.0, 0.0).astype(BF16)
            acc[rows, :] += dot_nn(pick, r.retx[...])

    loop(0, experts, combine)
    half_seq = z.seq // 2

    def tokens(c):
        return pl.ds(pl.multiple_of(c * half_seq, 16), half_seq)

    def d_copy(src, dst, n, peer):
        return remote(src, dst, r.d_sems.at[0, n], r.d_sems.at[1, n], (p.e, peer))

    r.d_send[...] = acc[tokens(1 - p.c), 0 : z.half_width].astype(BF16)
    r.gd_send[...] = acc[:, z.half_width :].astype(BF16)
    copy_d = d_copy(r.d_send, r.d_recv, 0, p.core_peer)
    copy_g = d_copy(r.gd_send, r.gd_recv, 1, p.core_peer)
    copy_d.start()
    copy_g.start()
    copy_d.wait_recv()

    def piece(x):
        return r.nf.at[tokens(p.c), pl.ds(pl.multiple_of(x * z.half_width, LANES), z.half_width)]

    piece(p.x)[...] = (
        acc[tokens(p.c), 0 : z.half_width] + r.d_recv[...].astype(F32)
    ).astype(BF16)
    to_x = d_copy(piece(p.x), piece(p.x), 2, p.x_peer)
    to_core = d_copy(piece(p.x), piece(p.x), 3, p.core_peer)
    on_to_core = d_copy(piece(1 - p.x), piece(1 - p.x), 4, p.core_peer)
    to_x.start()
    to_core.start()
    copy_g.wait_recv()
    r.gg[...] = acc[:, z.half_width :] + r.gd_recv[...].astype(F32)

    def finish(k):
        b.finish(k)
        for d in range(1, 4):
            gg_copy(k, d).wait_send()

        @pl.when(k > 0)
        def _():
            g.to_core(k).wait_send()
            g.on_to_core(k).wait_send()
            gate_copy(k).wait_send()
            gg_copy(k, 0).wait_send()

        @pl.when(k > 1)
        def _():
            g.out(k).wait_send()
            g.to_x(k).wait_send()

        og.to_core(k).wait_send()
        og.to_x(k).wait_send()
        og.on_to_core(k).wait_send()

        @pl.when(k >= experts - 2)
        def _():
            save_hid(k).wait()

    loop(0, experts, finish)
    g.out_wide(r.stage_wide).wait_send()
    for copy in cot_copies + wao_copies:
        copy.wait_send()
    for i in tiles:
        mixed_core(i).wait_send()
        mixed_x(i).wait_send()
        mixed_on(i).wait_send()
    to_x.wait_recv()
    on_to_core.start()
    to_core.wait_recv()
    on_to_core.wait_recv()
    for copy in (copy_d, copy_g, to_x, to_core, on_to_core):
        copy.wait_send()
    for copy in saves:
        copy.wait()


class Names:
    def __init__(self, names, refs):
        for name, ref in zip(names, refs, strict=True):
            setattr(self, name, ref)


EARLY = 4


def run_layer(
    z, inputs, gains, weight_qkv, weight_attn_out, rel_table, weight_router, w_in, w_out,
    routes, segments, cotangent,
):
    e, seq, width = z.experts, z.seq, z.width
    heads, cols = rel_table.shape[0], weight_qkv.shape[1]
    hidden_count = w_in.shape[1]
    tiles = seq // TILE
    half_seq = seq // 2
    smem = pl.BlockSpec(memory_space=pltpu.SMEM)
    dma = pltpu.SemaphoreType.DMA
    args = dict(
        table=rel_table,
        x=inputs,
        gains=gains,
        wqkv=weight_qkv,
        wao=weight_attn_out,
        wr=weight_router,
        w_in=w_in,
        w_out=w_out,
        routes=routes,
        seg_row=segments.reshape(1, -1),
        cot=cotangent,
    )
    outs = dict(
        rk_out=((LANES, seq), F32),
        gate_row_out=((LANES, seq), F32),
        cot_out=((width, seq), BF16),
        na_out=((seq, width), BF16),
        qkv_out=((seq, 3 * SLOT), BF16),
        mixed_out=((seq, cols), BF16),
        probs_out=((heads, seq, WINDOW), BF16),
        mid_out=((seq, width), F32),
        nrm_out=((seq, width), BF16),
        gates_out=((seq, LANES), F32),
        hid_out=((e, z.slots, hidden_count), BF16),
        gw_in_out=((width, hidden_count), F32),
        gw_out_out=((hidden_count, width), F32),
        nf=((seq, width), BF16),
        gg=((seq, LANES), F32),
    )
    in_vmem = ("nf", "gg")
    gather_names = (("stage", "og_buf", "og_send", "og_recv"), ("stage", "buf", "g_send", "g_recv"))
    scratch = {}
    for group in gather_names:
        scratch.update(zip(group, gather_scratch(z)))
    scratch.update(
        zip(
            ("part", "from_core", "stage_x", "from_x", "ret", "r_send", "r_recv"),
            return_scratch(z, e),
            strict=True,
        )
    )
    shapes = dict(
        rk_col=((seq, LANES), F32),
        rk_row=((LANES, seq), F32),
        na=((seq, width), BF16),
        qkv=((seq, 3 * SLOT), BF16),
        mixed=((seq, cols), BF16),
        mid=((seq, width), F32),
        gates=((seq, LANES), F32),
        gw_in=((width, hidden_count), F32),
        gw_out=((hidden_count, width), F32),
        bias=((heads, TILE, WINDOW), F32),
        cot_all=((width, seq), BF16),
        wao_all=((width, width), BF16),
        wr_pad=((LANES, width), F32),
        seg_col=((seq, LANES), F32),
        mixed_in=((seq, cols), BF16),
        mc=((seq, width), BF16),
        hid=((2, z.slots, hidden_count), BF16),
        pre=((2, z.slots, hidden_count), BF16),
        gated=((z.slots, width), BF16),
        gate_row=((LANES, seq), F32),
        gs_out=((e, 1, z.slot_lanes), F32),
        gs_in=((e, 1, z.slot_lanes), F32),
        gg_send=((e, 1, z.slot_lanes), F32),
        gg_recv=((e, 4, 1, z.slot_lanes), F32),
        stage_wide=((z.half, width), BF16),
        retx=((z.half, z.half_width + LANES), BF16),
        d_send=((half_seq, z.half_width), BF16),
        d_recv=((half_seq, z.half_width), BF16),
        gd_send=((seq, LANES), BF16),
        gd_recv=((seq, LANES), BF16),
    )
    for name, (shape, dtype) in shapes.items():
        scratch[name] = pltpu.VMEM(shape, dtype)
    scratch.update(
        dict(
            save_sem=dma((16,)),
            hid_sem=dma((e,)),
            p_sem=dma((tiles, heads)),
            c_sems=dma((2, 2, 3)),
            m_sems=dma((2, 3, tiles)),
            gs_sems=dma((2, e)),
            gg_sems=dma((2, e, 4)),
            d_sems=dma((2, 5)),
        )
    )
    names = list(args) + list(outs) + list(scratch)
    results = pl.pallas_call(
        functools.partial(layer_kernel, z, heads, names),
        out_shape=tuple(jax.ShapeDtypeStruct(*outs[n]) for n in outs),
        in_specs=[smem] + [VMEM_SPEC] * (len(args) - 1),
        out_specs=tuple(VMEM_SPEC if n in in_vmem else ANY_SPEC for n in outs),
        scratch_shapes=list(scratch.values()),
        compiler_params=pltpu.CompilerParams(
            collective_id=1, has_side_effects=True, vmem_limit_bytes=VMEM_LIMIT
        ),
        name="run_layer",
    )(*args.values())
    return Names(list(outs), results)


class Reduce:
    def __init__(self, z, p, blocks, in_pair, in_group, half_sum, result, pair_sems, group_sems):
        self.z, self.p = z, p
        self.blocks, self.in_pair, self.in_group = blocks, in_pair, in_group
        self.half_sum, self.result = half_sum, result
        self.pair_sems, self.group_sems = pair_sems, group_sems
        self.half_rows, self.group, self.row_parts, self.col_parts = reduce_cut(z, blocks.shape[1])
        self.owners = self.row_parts * self.col_parts
        self.piece_rows = self.half_rows // self.row_parts
        self.piece_cols = z.width // self.col_parts
        self.parity = lax.rem(p.e, 2)
        self.member = lax.div(p.e, 2)
        self.partner = p.e + 1 - 2 * self.parity

    def half(self, which):
        return pl.ds(pl.multiple_of(which * self.half_rows, 16), self.half_rows)

    def piece(self, owner, base):
        row = base + lax.div(owner, self.col_parts) * self.piece_rows
        col = lax.rem(owner, self.col_parts) * self.piece_cols
        return (
            pl.ds(pl.multiple_of(row, 16), self.piece_rows),
            pl.ds(pl.multiple_of(col, LANES), self.piece_cols),
        )

    def other(self, k):
        return lax.rem(self.member + k, self.group)

    def before(self, k):
        return lax.rem(self.member + self.group - k, self.group)

    def device(self, member):
        return (2 * member + self.parity, self.p.t)

    def pair_in(self, b):
        return remote(
            self.blocks.at[b, self.half(1 - self.parity), :],
            self.in_pair.at[b],
            self.pair_sems.at[0, 0, b],
            self.pair_sems.at[1, 0, b],
            (self.partner, self.p.t),
        )

    def spread(self, b, k):
        rows, cols = self.piece(self.other(k), 0)
        return remote(
            self.half_sum.at[b, rows, cols],
            self.in_group.at[b, k],
            self.group_sems.at[0, 0, b, k],
            self.group_sems.at[1, 0, b, k],
            self.device(self.other(k)),
        )

    def share(self, b, k):
        rows, cols = self.piece(self.member, self.parity * self.half_rows)
        ref = self.result.at[b, rows, cols]
        return remote(
            ref,
            ref,
            self.group_sems.at[0, 1, b, k],
            self.group_sems.at[1, 1, b, k],
            self.device(self.other(k)),
        )

    def pair_out(self, b):
        ref = self.result.at[b, self.half(self.parity), :]
        return remote(
            ref,
            ref,
            self.pair_sems.at[0, 1, b],
            self.pair_sems.at[1, 1, b],
            (self.partner, self.p.t),
        )

    def first(self, b):
        self.pair_in(b).start()

    def second(self, b):
        self.pair_in(b).wait_recv()
        mine = self.blocks[b, self.half(self.parity), :].astype(F32)
        self.half_sum[b] = (mine + self.in_pair[b].astype(F32)).astype(BF16)

        def send(k):
            @pl.when(self.other(k) < self.owners)
            def _():
                self.spread(b, k).start()

        loop(1, self.group, send)

    def third(self, b):
        @pl.when(self.member < self.owners)
        def _():
            rows, cols = self.piece(self.member, 0)
            total = self.half_sum[b, rows, cols].astype(F32)

            def add(k, total):
                self.spread(b, k).wait_recv()
                return total + self.in_group[b, k].astype(F32)

            total = lax.fori_loop(1, self.group, add, total)
            rows, cols = self.piece(self.member, self.parity * self.half_rows)
            self.result[b, rows, cols] = total.astype(BF16)
            loop(1, self.group, lambda k: self.share(b, k).start())

    def fourth(self, b):
        def wait(k):
            @pl.when(self.before(k) < self.owners)
            def _():
                self.share(b, k).wait_recv()

        loop(1, self.group, wait)
        self.pair_out(b).start()

    def last(self, b):
        self.pair_out(b).wait_recv()

    def finish(self, b):
        self.pair_in(b).wait_send()
        self.pair_out(b).wait_send()

        def wait(k):
            @pl.when(self.other(k) < self.owners)
            def _():
                self.spread(b, k).wait_send()

            @pl.when(self.member < self.owners)
            def _():
                self.share(b, k).wait_send()

        loop(1, self.group, wait)


def reduce_cut(z, rows):
    half_rows, group = rows // 2, z.experts // 2
    best = (1, 1)
    for row_parts in range(1, half_rows // 16 + 1):
        for col_parts in range(1, z.width // LANES + 1):
            if (half_rows // 16) % row_parts or (z.width // LANES) % col_parts:
                continue
            if best[0] * best[1] < row_parts * col_parts <= group:
                best = (row_parts, col_parts)
    return half_rows, group, best[0], best[1]


def reduce_scratch(z, blocks, rows):
    half_rows, group, row_parts, col_parts = reduce_cut(z, rows)
    piece = (half_rows // row_parts, z.width // col_parts)
    return [
        pltpu.VMEM((blocks, rows, z.width), BF16),
        pltpu.VMEM((blocks, half_rows, z.width), BF16),
        pltpu.VMEM((blocks, group) + piece, BF16),
        pltpu.VMEM((blocks, half_rows, z.width), BF16),
        pltpu.VMEM((blocks, rows, z.width), BF16),
        pltpu.SemaphoreType.DMA((2, 2, blocks)),
        pltpu.SemaphoreType.DMA((2, 2, blocks, group)),
    ]


def tail_sums(dbias):
    wide = dbias.shape[1]
    count = TILE
    while count > 8:
        half = count // 2
        dbias = dbias[0:half, :] + pltpu.roll(dbias[half:count, :], wide - half, 1)
        count = half
    total = dbias[0:1, :]
    for r in range(1, count):
        total = total + pltpu.roll(dbias[r : r + 1, :], wide - r, 1)
    return total


def split_dot(values, right):
    high = values.astype(BF16)
    rest = values - high.astype(F32)
    middle = rest.astype(BF16)
    low = (rest - middle.astype(F32)).astype(BF16)
    return dot_nn(high, right) + dot_nn(middle, right) + dot_nn(low, right)


def back_kernel(z, heads, names, *refs):
    r = Names(names, refs)
    p = Place(z)
    experts = z.experts
    cols = r.wao.shape[0]
    size = cols // heads
    loads = {}
    for n, name in enumerate(BACK_LOADS):
        loads[name] = pltpu.make_async_copy(
            getattr(r, name), getattr(r, name + "_in"), r.load_sem.at[n]
        )
        loads[name].start()
    midg, probs, qkv, na_ref, x_ref = (getattr(r, name + "_in") for name in BACK_LOADS)
    blocks, nag, dmix, dqkv, part = r.blocks, r.nag, r.dmix, r.dqkv, r.part_sum
    dk, dv, dbias, late, late_in, s_sems = r.dk, r.dv, r.dbias, r.late, r.late_in, r.s_sems
    n_core, n_sx, n_x, n_sems = r.n_core, r.n_sx, r.n_x, r.n_sems
    wqkv_ref, gains_ref = r.wqkv, r.gains
    p.greet()
    red = Reduce(
        z, p, blocks, r.in_pair, r.in_group, r.half_sum, r.result, r.pair_sems, r.group_sems
    )
    b = Return(z, p, r.part, r.from_core, r.stage_x, r.from_x, r.ret, r.r_send, r.r_recv)

    def part_of(c):
        return pl.ds(pl.multiple_of(c * cols, 16), cols)

    def hid_copy(k):
        return pltpu.make_async_copy(r.hid.at[k], r.hid_in.at[lax.rem(k, 2)], r.hid_sem.at[k])

    def results_first(k):
        hid_copy(k).wait()

        @pl.when(k + 1 < experts)
        def _():
            hid_copy(k + 1).start()

        b.make_room(k)
        for j in range(0, z.width, COL_TILE):
            r.part[b.rows_of(k), j : j + COL_TILE] = dot_nn(
                r.hid_in[lax.rem(k, 2)], r.w_out[:, j : j + COL_TILE]
            ).astype(BF16)
        b.first(k)

        @pl.when(k >= 1)
        def _():
            b.second(k - 1)

    def results_combine(k):
        b.arrive(k)
        who = p.ahead(k)
        pick = slot_onehot(r.rk_row[pl.ds(who, 1), :], z.half, p.c * z.half)
        gate = r.gate_row[pl.ds(who, 1), :]
        for s in range(0, z.half_width, LANES):
            rows = slice(s, s + LANES)
            r.acc[rows, :] += gate * dot_tn(r.ret[k, :, rows], pick)

    def group(n):
        count = (experts + 3) // 4
        return min(n * count, experts), min((n + 1) * count, experts)

    hid_copy(0).start()
    r.wr_pad[...] = jnp.zeros_like(r.wr_pad)
    r.wr_pad[0:experts, :] = r.wr[...].astype(F32)
    router_low = r.wr_pad[...].astype(BF16)
    router = jnp.zeros((LANES, z.width), F32)
    gain_sum = jnp.zeros((1, z.width), F32)
    loads["mid"].wait()
    for i in tiles_of(z.seq):
        rows = slice(i * TILE, (i + 1) * TILE)
        gate = r.gates[rows, :]
        grads = r.gg[rows, :]
        grads = grads + pltpu.roll(grads, LANES - experts, 1)
        dots = jnp.sum(gate * grads, axis=1, keepdims=True)
        logit = (gate * (grads - dots)).astype(BF16)
        router = router + dot_tn(logit, r.nrm[rows, :])
        back = r.nf[rows, :].astype(F32) + dot_nn(logit, router_low)
        mid = midg[rows, :]
        flipped = midg[rows, pl.ds(pl.multiple_of(p.x * z.half_width, LANES), z.half_width)].T
        r.acc[part_of(p.c), rows] = jnp.where(p.c == 0, flipped[0:cols, :], flipped[cols:, :])
        r.acc[part_of(1 - p.c), rows] = jnp.zeros((cols, TILE), F32)
        root = lax.rsqrt(jnp.mean(mid * mid, axis=1, keepdims=True) + epsilon)
        unit = mid * root
        gain_sum = gain_sum + jnp.sum(back * unit, axis=0, keepdims=True)
        u = back * gains_ref[1:2, :]
        mean = jnp.mean(u * unit, axis=1, keepdims=True)
        grad = r.cot[:, rows].astype(F32).T + root * (u - unit * mean)
        midg[rows, :] = grad
        low = grad.astype(BF16)
        nag[rows, :] = low
        dmix[rows, :] = jnp.zeros((TILE, SLOT), BF16)
        dmix[rows, 0:cols] = dot_nt(low, r.wao[...]).astype(BF16)
        loop(*group(i), results_first)
    b.second(experts - 1)
    for j in range(0, z.width, COL_TILE):
        cut = slice(j, j + COL_TILE)
        blocks[3, :, cut] = dot_tn(r.mixed[...], nag[:, cut]).astype(BF16)
    red.first(3)
    rest = jnp.zeros((cols - experts, z.width), F32)
    first_row = lax.broadcasted_iota(jnp.int32, rest.shape, 0) == 0
    blocks[4] = jnp.concatenate(
        [router[0:experts, :], jnp.where(first_row, gain_sum, rest)], axis=0
    ).astype(BF16)
    red.first(4)
    loads["probs"].wait()
    loads["qkv"].wait()
    loads["na"].wait()
    dk[...] = jnp.zeros_like(dk)
    dv[...] = jnp.zeros_like(dv)
    dbias[...] = jnp.zeros_like(dbias)

    def window(i):
        start, width = window_of(i)
        return slice(i * TILE, (i + 1) * TILE), slice(start, start + width), width

    for i in tiles_of(z.seq):
        rows, span, width = window(i)
        for h in range(heads):
            own = mask_head(dmix[rows, :], h, size)
            dv[span, :] += dot_tn(probs[h, rows, 0:width], own)
    red.second(3)
    red.second(4)
    dqkv[:, 2 * SLOT :] = dv[...].astype(BF16)

    def block(b, k):
        for j in range(0, z.width, COL_TILE):
            cut = slice(j, j + COL_TILE)
            full = dot_tn(dqkv[:, k * SLOT : (k + 1) * SLOT], na_ref[:, cut])
            blocks[b, :, cut] = full[0:cols, :].astype(BF16)

    block(2, 2)
    red.first(2)
    loop(*group(0), b.third)
    half = TILE // 2

    def tile_rows(i, c):
        return pl.ds(pl.multiple_of(i * TILE + c * half, 16), half)

    def nag_piece(i, x):
        return nag.at[
            tile_rows(i, p.c), pl.ds(pl.multiple_of(x * z.half_width, LANES), z.half_width)
        ]

    def n_to_core(i):
        return remote(
            part.at[tile_rows(i, 1 - p.c), :], n_core.at[i], n_sems.at[0, 0, i], n_sems.at[1, 0, i],
            (p.e, p.core_peer),
        )

    def n_to_x(i):
        return remote(
            n_sx.at[i], n_x.at[i], n_sems.at[0, 1, i], n_sems.at[1, 1, i], (p.e, p.x_peer)
        )

    def n_share(i, which):
        ref = nag_piece(i, p.x if which < 4 else 1 - p.x)
        peer = p.x_peer if which == 2 else p.core_peer
        return remote(ref, ref, n_sems.at[0, which, i], n_sems.at[1, which, i], (p.e, peer))

    def n_second(i):
        n_to_core(i).wait_recv()
        for x in (1 - p.x, p.x):
            cut = pl.ds(pl.multiple_of(x * z.half_width, LANES), z.half_width)
            both = part[tile_rows(i, p.c), cut].astype(F32) + n_core[i, :, cut].astype(F32)
            if x is p.x:
                nag_piece(i, p.x)[...] = both.astype(BF16)
            else:
                n_sx[i] = both.astype(BF16)
                n_to_x(i).start()

    def n_third(i):
        n_to_x(i).wait_recv()
        mine = nag_piece(i, p.x)
        mine[...] = (mine[...].astype(F32) + n_x[i].astype(F32)).astype(BF16)
        n_share(i, 2).start()
        n_share(i, 3).start()

    def n_fourth(i):
        n_share(i, 2).wait_recv()
        n_share(i, 4).start()

    count = len(tiles_of(z.seq))
    order = list(reversed(tiles_of(z.seq)))
    for step, i in enumerate(order):
        rows, span, width = window(i)
        total = jnp.zeros((TILE, SLOT), F32)
        for h in range(heads):
            own = mask_head(dmix[rows, :], h, size)
            weight = probs[h, rows, 0:width].astype(F32)
            back = dot_nt(own, qkv[span, 2 * SLOT :])
            dots = jnp.sum(weight * back, axis=1, keepdims=True)
            score = weight * (back - dots)
            low = score.astype(BF16)
            dbias[h, :, WINDOW - width : WINDOW] += low.astype(F32)
            total = total + dot_nn(low, mask_head(qkv[span, SLOT : 2 * SLOT], h, size))
            dk[span, :] += dot_tn(low, mask_head(qkv[rows, 0:SLOT], h, size))
        dqkv[rows, 0:SLOT] = (total * size ** (-0.5)).astype(BF16)
        dqkv[rows, SLOT : 2 * SLOT] = dk[rows, :].astype(BF16)
        for j in range(0, z.width, COL_TILE):
            part[rows, j : j + COL_TILE] = sum(
                dot_nn(
                    dqkv[rows, k * SLOT : k * SLOT + cols], wqkv_ref[k, :, j : j + COL_TILE]
                )
                for k in range(3)
            ).astype(BF16)
        n_to_core(i).start()
        if step == 0:
            red.third(3)
            red.third(4)
            red.second(2)
        if step >= 1:
            n_second(order[step - 1])
        if step == 1:
            red.fourth(3)
            red.fourth(4)
            red.third(2)
        if step >= 2:
            n_third(order[step - 2])
        if step == 2:
            red.fourth(2)
        if step >= 3:
            n_fourth(order[step - 3])
        if step < 3:
            loop(*group(step + 1), b.third)
    block(0, 0)
    red.first(0)
    block(1, 1)
    red.first(1)
    n_second(order[count - 1])
    n_third(order[count - 2])
    n_fourth(order[count - 3])
    late[...] = jnp.zeros_like(late)
    lane = lax.broadcasted_iota(jnp.int32, (4 * TILE, LANES), 0)
    distance = distance_of(lane)
    which = lax.broadcasted_iota(jnp.int32, (4 * TILE, LANES), 1)
    hot = jnp.where((bucket_grid(distance) == which) & (distance >= 0), 1.0, 0.0).astype(BF16)
    red.second(0)
    red.second(1)
    sums = [tail_sums(dbias[h]) for h in range(heads)]
    sums = jnp.concatenate(sums + [jnp.zeros((8 - heads, 4 * TILE), F32)], axis=0)
    late[0:8, 0:LANES] = split_dot(sums, hot)
    n_third(order[count - 1])
    n_fourth(order[count - 2])
    red.third(0)
    red.third(1)
    n_fourth(order[count - 1])
    for i in order:
        n_share(i, 3).wait_recv()
        n_share(i, 4).wait_recv()
    loads["x"].wait()

    def grad_copy(i):
        rows = pl.ds(i * TILE, TILE)
        return pltpu.make_async_copy(midg.at[rows, :], r.grad_in.at[rows, :], r.out_sem.at[i])

    def result_copy(n):
        return pltpu.make_async_copy(r.result.at[n], r.blocks_out.at[n], r.res_sem.at[n])

    gain_sum = jnp.zeros((1, z.width), F32)
    for i in tiles_of(z.seq):
        rows = slice(i * TILE, (i + 1) * TILE)
        stream = x_ref[rows, :].astype(F32)
        root = lax.rsqrt(jnp.mean(stream * stream, axis=1, keepdims=True) + epsilon)
        unit = stream * root
        back = nag[rows, :].astype(F32)
        gain_sum = gain_sum + jnp.sum(back * unit, axis=0, keepdims=True)
        w = back * gains_ref[0:1, :]
        mean = jnp.mean(w * unit, axis=1, keepdims=True)
        midg[rows, :] += root * (w - unit * mean)
        grad_copy(i).start()
    for k in range(z.width // SLOT):
        late[8 + k : 9 + k, :] = gain_sum[:, k * SLOT : (k + 1) * SLOT]

    def late_copy(k):
        return remote(
            late, late_in.at[k], s_sems.at[0, 1, k], s_sems.at[1, 1, k], (p.ahead(k), p.t)
        )

    late_in[0] = late[...]
    loop(1, experts, lambda k: late_copy(k).start())
    red.fourth(0)
    red.fourth(1)

    def take_late(source, total):
        k = p.steps_from(source)

        @pl.when(k > 0)
        def _():
            late_copy(k).wait_recv()

        return total + late_in[k]

    loop(0, experts, results_combine)
    r.d_send[...] = r.acc[part_of(1 - p.c), :].astype(BF16)
    d_copy = remote(
        r.d_send, r.d_recv, r.d_sems.at[0], r.d_sems.at[1], (p.e, p.core_peer)
    )
    d_copy.start()
    for n in range(5):
        red.last(n)
        result_copy(n).start()
    r.late_out[...] = lax.fori_loop(0, experts, take_late, jnp.zeros(late.shape, F32))
    d_copy.wait_recv()
    r.act[...] = (r.acc[part_of(p.c), :] + r.d_recv[...].astype(F32)).astype(BF16)
    d_copy.wait_send()
    for n in range(5):
        red.finish(n)
        result_copy(n).wait()
    for i in tiles_of(z.seq):
        grad_copy(i).wait()

    def finish(k):
        b.finish(k)

        @pl.when(k > 0)
        def _():
            late_copy(k).wait_send()

    loop(0, experts, finish)
    for i in order:
        n_to_core(i).wait_send()
        n_to_x(i).wait_send()
        for which in (2, 3, 4):
            n_share(i, which).wait_send()


BACK_LOADS = ("mid", "probs", "qkv", "na", "x")


def run_back(z, kept, inputs, weight_router, gains, wao, wqkv, w_out):
    heads, cols = kept.probs_out.shape[0], wao.shape[0]
    e, seq, width = z.experts, z.seq, z.width
    tiles = seq // TILE
    half = TILE // 2
    dma = pltpu.SemaphoreType.DMA
    args = dict(
        mid=kept.mid_out,
        probs=kept.probs_out,
        qkv=kept.qkv_out,
        na=kept.na_out,
        x=inputs,
        hid=kept.hid_out,
        nf=kept.nf,
        gg=kept.gg,
        gates=kept.gates_out,
        nrm=kept.nrm_out,
        wr=weight_router,
        gains=gains,
        cot=kept.cot_out,
        wao=wao,
        mixed=kept.mixed_out,
        wqkv=wqkv,
        w_out=w_out,
        rk_row=kept.rk_out,
        gate_row=kept.gate_row_out,
    )
    in_hbm = BACK_LOADS + ("hid",)
    outs = dict(
        grad_in=((seq, width), F32),
        blocks_out=((5, cols, width), BF16),
        late_out=((16, SLOT), F32),
        act=((cols, seq), BF16),
    )
    scratch = {name + "_in": pltpu.VMEM(args[name].shape, args[name].dtype) for name in BACK_LOADS}
    scratch.update(
        zip(
            ("part", "from_core", "stage_x", "from_x", "ret", "r_send", "r_recv"),
            return_scratch(z, min(e, 8)),
            strict=True,
        )
    )
    scratch.update(
        zip(
            ("blocks", "in_pair", "in_group", "half_sum", "result", "pair_sems", "group_sems"),
            reduce_scratch(z, 5, cols),
            strict=True,
        )
    )
    shapes = dict(
        hid_in=((2,) + kept.hid_out.shape[1:], BF16),
        acc=((z.half_width, seq), F32),
        d_send=((cols, seq), BF16),
        d_recv=((cols, seq), BF16),
        wr_pad=((LANES, width), F32),
        dmix=((seq, SLOT), BF16),
        dk=((seq, SLOT), F32),
        dv=((seq, SLOT), F32),
        dbias=((heads, TILE, 4 * TILE), F32),
        dqkv=((seq, 3 * SLOT), BF16),
        part_sum=((seq, width), BF16),
        late=((16, SLOT), F32),
        late_in=((e, 16, SLOT), F32),
        n_core=((tiles, half, width), BF16),
        n_sx=((tiles, half, z.half_width), BF16),
        n_x=((tiles, half, z.half_width), BF16),
        nag=((seq, width), BF16),
    )
    for name, (shape, dtype) in shapes.items():
        scratch[name] = pltpu.VMEM(shape, dtype)
    scratch.update(
        dict(
            load_sem=dma((len(BACK_LOADS),)),
            hid_sem=dma((e,)),
            d_sems=dma((2,)),
            s_sems=dma((2, 2, e)),
            n_sems=dma((2, 5, tiles)),
            out_sem=dma((tiles,)),
            res_sem=dma((5,)),
        )
    )
    names = list(args) + list(outs) + list(scratch)
    results = pl.pallas_call(
        functools.partial(back_kernel, z, heads, names),
        out_shape=tuple(jax.ShapeDtypeStruct(*outs[n]) for n in outs),
        in_specs=[ANY_SPEC if n in in_hbm else VMEM_SPEC for n in args],
        out_specs=(ANY_SPEC, ANY_SPEC, VMEM_SPEC, VMEM_SPEC),
        scratch_shapes=list(scratch.values()),
        compiler_params=pltpu.CompilerParams(
            collective_id=4, has_side_effects=True, vmem_limit_bytes=VMEM_LIMIT
        ),
        name="run_back",
    )(*args.values())
    return Names(list(outs), results)


PIECES = 4


def finish_kernel(
    experts, heads, blocks, late, grad_in, gw_in, gw_out,
    grad_out, gw_in_out, gw_out_out, qkv, wao, router, gain_attn, gain_ffn, table,
    grad_held, gw_in_held, gw_out_held, sems,
):
    pieces = []
    for n, (src, dst, held) in enumerate(
        (
            (grad_in, grad_out, grad_held),
            (gw_in, gw_in_out, gw_in_held),
            (gw_out, gw_out_out, gw_out_held),
        )
    ):
        count = src.shape[0] // PIECES
        for m in range(PIECES):
            rows = pl.ds(m * count, count)
            load = pltpu.make_async_copy(src.at[rows, :], held.at[rows, :], sems.at[0, n, m])
            store = pltpu.make_async_copy(held.at[rows, :], dst.at[rows, :], sems.at[1, n, m])
            pieces.append((load, store))
    for load, _ in pieces:
        load.start()
    for load, store in pieces:
        load.wait()
        store.start()
    qkv[...] = blocks[0:3].astype(F32)
    wao[...] = blocks[3].astype(F32)
    small = blocks[4].astype(F32)
    router[...] = small[0:experts, :]
    gain_ffn[...] = small[experts : experts + 1, :]
    table[...] = late[0:heads, 0:BUCKETS]
    for k in range(gain_attn.shape[1] // SLOT):
        gain_attn[:, k * SLOT : (k + 1) * SLOT] = late[8 + k : 9 + k, :]
    for _, store in pieces:
        store.wait()


def run_finish(z, heads, blocks, late, grad_in, gw_in, gw_out):
    cols, width = blocks.shape[1:]
    shapes = (
        grad_in.shape, gw_in.shape, gw_out.shape, (3, cols, width), (cols, width),
        (z.experts, width), (1, width), (1, width), (heads, BUCKETS),
    )
    return pl.pallas_call(
        functools.partial(finish_kernel, z.experts, heads),
        out_shape=tuple(jax.ShapeDtypeStruct(shape, F32) for shape in shapes),
        in_specs=[VMEM_SPEC] * 2 + [ANY_SPEC] * 3,
        out_specs=(ANY_SPEC,) * 3 + (VMEM_SPEC,) * 6,
        scratch_shapes=[pltpu.VMEM(shape, F32) for shape in shapes[:3]]
        + [pltpu.SemaphoreType.DMA((2, 3, PIECES))],
        compiler_params=pltpu.CompilerParams(vmem_limit_bytes=VMEM_LIMIT),
        name="run_finish",
    )(blocks, late, grad_in, gw_in, gw_out)


def per_device(
    inputs,
    gain_attn,
    gain_ffn,
    weight_qkv,
    weight_attn_out,
    rel_table,
    weight_router,
    weight_in,
    weight_out,
    routes,
    segments,
    cotangent,
):
    seq_len, width = inputs.shape
    heads = rel_table.shape[1]
    experts = weight_router.shape[1]
    z = Sizes(experts, seq_len, routes.shape[1], width)
    gains = jnp.stack([gain_attn, gain_ffn])
    wqkv = jnp.transpose(weight_qkv, (0, 2, 1))
    wr = weight_router.T
    kept = run_layer(
        z, inputs, gains, wqkv, weight_attn_out, rel_table.T, wr, weight_in[0], weight_out[0],
        routes.T, segments, cotangent.T,
    )
    grads = run_back(
        z, kept, inputs, wr, gains, weight_attn_out, wqkv, weight_out[0]
    )
    grad_input, gw_in, gw_out, gw_qkv, gw_attn_out, router, gain_a, gain_f, table = run_finish(
        z, heads, grads.blocks_out, grads.late_out, grads.grad_in, kept.gw_in_out,
        kept.gw_out_out,
    )
    return (
        grads.act.T,
        grad_input,
        gain_a.reshape(width),
        gain_f.reshape(width),
        jnp.transpose(gw_qkv, (0, 2, 1)),
        gw_attn_out,
        table.T,
        router.T,
        gw_in[None],
        gw_out[None],
    )


def solution(mesh):
    in_specs = (
        P("expert", None),
        P(),
        P(),
        P(None, None, "tensor"),
        P("tensor", None),
        P(None, "tensor"),
        P(),
        P("expert", None, "tensor"),
        P("expert", "tensor", None),
        P("expert", None),
        P("expert"),
        P("expert", "tensor"),
    )
    out_specs = (
        P("expert", "tensor"),
        P("expert", None),
        P(),
        P(),
        P(None, None, "tensor"),
        P("tensor", None),
        P(None, "tensor"),
        P(),
        P("expert", None, "tensor"),
        P("expert", "tensor", None),
    )
    return jax.shard_map(
        per_device, mesh=mesh, in_specs=in_specs, out_specs=out_specs, check_vma=False
    )
```
